32 devices in a mesh: fsdp: 4 (over x, core), seq: 8 (over z, y).
Axes of the slice: x: 2, y: 2, z: 4, core: 2. Of those that a mesh axis runs over, the one named last changes fastest.
Arguments:
- hidden: bfloat16 [4, 1024, 2880], P('fsdp', 'seq'), may hold values from -6 to 6
- out_grad: bfloat16 [4, 1024, 2880], P('fsdp', 'seq'), may hold values from -6 to 6
- routes: int32 [4, 1024, 4], P('fsdp', 'seq'), may hold values from 0 to 7, all different within a row; in each aligned block of 128 rows (0 to 127, 128 to 255, ..., all dimensions but the last counted through in order) at most 72 rows name the same one
- norm1_gain: float32 [2880], replicated, may hold values from 0.5 to 1.5
- qkv_weight: bfloat16 [2880, 5120], P(None, ('fsdp', 'seq')), may hold values from -0.109375 to 0.109375
- qkv_bias: float32 [5120], replicated, may hold values from -0.625 to 0.625
- sink_logits: float32 [64], replicated, may hold values from -6 to 6
- out_weight: bfloat16 [4096, 2880], P(('fsdp', 'seq')), may hold values from -0.1875 to 0.1875
- out_bias: float32 [2880], replicated, may hold values from -0.625 to 0.625
- norm2_gain: float32 [2880], replicated, may hold values from 0.5 to 1.5
- router_weight: bfloat16 [2880, 8], replicated, may hold values from -0.0546875 to 0.0546875
- router_bias: float32 [8], replicated, may hold values from -0.625 to 0.625
- gate_up_weight: bfloat16 [8, 2880, 5760], P('seq', 'fsdp'), may hold values from -0.109375 to 0.109375
- gate_up_bias: bfloat16 [8, 5760], P('seq', 'fsdp'), may hold values from -0.625 to 0.625
- down_weight: bfloat16 [8, 2880, 2880], P('seq', 'fsdp'), may hold values from -0.109375 to 0.109375
- down_bias: bfloat16 [8, 2880], P('seq', 'fsdp'), may hold values from -0.625 to 0.625
Outputs:
- out_hidden: bfloat16 [4, 1024, 2880], P('fsdp', 'seq')
- grad_hidden: bfloat16 [4, 1024, 2880], P('fsdp', 'seq')
- grad_norm1_gain: float32 [2880], replicated
- grad_qkv_weight: float32 [2880, 5120], P(None, ('fsdp', 'seq'))
- grad_qkv_bias: float32 [5120], replicated
- grad_sink_logits: float32 [64], replicated
- grad_out_weight: float32 [4096, 2880], P(('fsdp', 'seq'))
- grad_out_bias: float32 [2880], replicated
- grad_norm2_gain: float32 [2880], replicated
- grad_router_weight: float32 [2880, 8], replicated
- grad_router_bias: float32 [8], replicated
- grad_gate_up_weight: float32 [8, 2880, 5760], P('seq', 'fsdp')
- grad_gate_up_bias: float32 [8, 5760], P('seq', 'fsdp')
- grad_down_weight: float32 [8, 2880, 2880], P('seq', 'fsdp')
- grad_down_bias: float32 [8, 2880], P('seq', 'fsdp')
The draws below stay inside these ranges and needn't reach their ends.
Inputs may be any that keep to these rules, and one draw needn't show every extreme that they name: `routes`: the 4 experts of a token differ. Within the 128 positions of one device, no expert is named more than 72 times, a bound that some block reaches.
All inputs are finite; a program needn't handle non-finite values.
Results may differ from the reference program's by a relative error of at most 0.018.
Values may be sent and summed in bfloat16 or wider, within the bound.
No kernel may reach another device: no remote copies, remote signals or barrier semaphores. Data moves between devices by JAX's collectives and lax.ppermute only.
A program may use at most 576 MiB of HBM per device.

```python
import math
import jax
import jax.numpy as jnp
import numpy as np
from jax import lax

D = 2880
FF = 2880
HEADS = 64
KV_HEADS = 8
HD = 64
TOPK = 4
TOK_DEV = 128
SEQS = 4
LENGTH = 1024
EXPERTS = 8
CAP = 72
QKV = 5120
QBLOCK = 512
N_SEQ = 8


def shard_levels(stream_key, dims, pieces, low, top_value):
    def one(position, shards_of):
        steps = jax.random.uniform(jax.random.fold_in(jax.random.fold_in(stream_key, 6), position), (shards_of,), jnp.float32, low / len(pieces), top_value / len(pieces))
        return jnp.repeat(jnp.exp(steps), dims[position] // shards_of).reshape((-1,) + (1,) * (len(dims) - position - 1))

    gain = one(*pieces[0])
    for cut in pieces[1:]:
        gain = gain * one(*cut)
    return gain


def shared_out(key, own, number, rows, number_of, top, limit, slope):
    sequence = jax.random.permutation(key, number_of)
    heavy_load, usual = portions_of(number_of, rows * top, limit, slope, True), portions_of(number_of, rows * top, limit, slope, False)
    places = jnp.arange(number_of)

    def named(tallies, rotation):
        used = int((tallies > 0).sum())
        fixed = max(1, used // 4)
        shifted = fixed + (places - fixed + rotation * (used - fixed)) % max(1, number_of - fixed)
        return jnp.zeros((number_of,), jnp.int32).at[sequence[jnp.where(places < fixed, places, shifted)]].set(jnp.asarray(tallies, jnp.int32))

    tallies = jnp.where(number % 4 == 0, named(heavy_load, number // 4), named(usual, number - number // 4 - 1))
    mixed = jax.random.permutation(jax.random.fold_in(own, 3), number_of)
    source_of, taker = mixed[0:number_of // 2 * 2:2], mixed[1:number_of // 2 * 2:2]
    margin = jnp.minimum(tallies[source_of] - 1, limit - tallies[taker]) // 2
    margin = jnp.where((source_of == sequence[0]) | (taker == sequence[0]) | (tallies[taker] == 0), 0, jnp.maximum(margin, 0))
    shifted = jax.random.randint(jax.random.fold_in(own, 4), (number_of // 2,), 0, 1 << 20) % (margin + 1)
    tallies = tallies.at[source_of].add(-shifted).at[taker].add(shifted)
    members = jnp.searchsorted(jnp.cumsum(tallies), jnp.arange(rows * top), side="right").astype(jnp.int32)
    table = members.reshape(top, rows).T
    table = table[jax.random.permutation(jax.random.fold_in(own, 1), rows)]
    rotation = jax.random.randint(jax.random.fold_in(own, 2), (rows, 1), 0, top)
    return jnp.take_along_axis(table, (jnp.arange(top)[None, :] + rotation) % top, axis=1)


def portions_of(amount, total, bound, lean, full):
    weights = [(1 << 20) // math.isqrt(grade ** lean) + 1 for grade in range(1, amount + 1)]
    largest = bound if full else min(bound, max(-(-total // amount), total * weights[0] // sum(weights)))
    least = 1 if total - largest >= amount - 1 else 0
    given, rest = [largest] + [least] * (amount - 1), total - largest - least * (amount - 1)
    while rest > 0:
        candidates = [i for i in range(1, amount) if given[i] < largest] or [i for i in range(1, amount) if given[i] < bound]
        whole, budget = sum([weights[i] for i in candidates]), rest
        for i in candidates:
            extra = min(bound - given[i], max(1, budget * weights[i] // whole), rest)
            given[i] = given[i] + extra
            rest = rest - extra
    return np.array(given)


def noise(rng, dims, width, limit, split=(), held_as=jnp.bfloat16):
    values = width * jax.random.normal(rng, dims, jnp.float32)
    if split:
        values = values * shard_levels(rng, dims, split, -0.22, 0.18)
    return jnp.clip(values, -limit, limit).astype(held_as)


def setup_inputs(seed: int = 0) -> dict:
    seeds = jax.random.split(jax.random.key(seed), 17)
    hidden = noise(seeds[0], (SEQS, LENGTH, D), 1.0, 6.0, ((0, 4), (1, 8)))
    out_grad = noise(seeds[1], (SEQS, LENGTH, D), 1.0, 6.0, ((0, 4), (1, 8)))
    routes_keys = jax.random.split(jax.random.fold_in(seeds[2], 1), SEQS * LENGTH // TOK_DEV)
    routes_turns = jax.random.permutation(jax.random.fold_in(seeds[2], 3), SEQS * LENGTH // TOK_DEV)
    routes = jax.vmap(lambda own, number: shared_out(jax.random.fold_in(seeds[2], 2), own, number, TOK_DEV, EXPERTS, TOPK, CAP, 0))(routes_keys, routes_turns).reshape((SEQS, LENGTH, TOPK))
    norm1_gain = jnp.clip(1.0 + 0.1 * jax.random.normal(seeds[3], (D,), jnp.float32), 0.5, 1.5)
    qkv_weight = noise(seeds[4], (D, QKV), D ** -0.5, 0.109375, ((1, 32),))
    qkv_bias = noise(seeds[5], (QKV,), 0.1, 0.625, (), jnp.float32)
    sink_logits = noise(seeds[6], (HEADS,), 1.0, 6.0, (), jnp.float32)
    out_weight = noise(seeds[7], (HEADS * HD, D), (HEADS * HD // 4) ** -0.5, 0.1875, ((0, 32),))
    out_bias = noise(seeds[8], (D,), 0.1, 0.625, (), jnp.float32)
    norm2_gain = jnp.clip(1.0 + 0.1 * jax.random.normal(seeds[9], (D,), jnp.float32), 0.5, 1.5)
    router_weight = noise(seeds[10], (D, EXPERTS), (4 * D) ** -0.5, 0.0546875)
    router_bias = noise(seeds[11], (EXPERTS,), 0.1, 0.625, (), jnp.float32)
    gate_up_weight = noise(seeds[12], (EXPERTS, D, 2 * FF), D ** -0.5, 0.109375, ((0, 8), (1, 4)))
    gate_up_bias = noise(seeds[13], (EXPERTS, 2 * FF), 0.1, 0.625, ((0, 8), (1, 4)))
    down_weight = noise(seeds[14], (EXPERTS, FF, D), FF ** -0.5, 0.109375, ((0, 8), (1, 4)))
    down_bias = noise(seeds[15], (EXPERTS, D), 0.1, 0.625, ((0, 8), (1, 4)))
    return {"hidden": hidden, "out_grad": out_grad, "routes": routes, "norm1_gain": norm1_gain, "qkv_weight": qkv_weight, "qkv_bias": qkv_bias, "sink_logits": sink_logits, "out_weight": out_weight, "out_bias": out_bias, "norm2_gain": norm2_gain, "router_weight": router_weight, "router_bias": router_bias, "gate_up_weight": gate_up_weight, "gate_up_bias": gate_up_bias, "down_weight": down_weight, "down_bias": down_bias}


ROPE_BASE = 150000.0
SWIGLU_SLOPE = 1.702
CLAMP_LIMIT = 7.0
NORM_EPSILON = 1e-05
PRECISE = lax.Precision.HIGHEST

@jax.custom_vjp
def low(v):
    return lax.optimization_barrier(v.astype(jnp.bfloat16)).astype(jnp.float32)

@jax.custom_vjp
def low_back(v):
    return v

def low_keep(v):
    return (low(v), None)

def low_pass(kept, grad):
    return (grad,)

def back_keep(v):
    return (v, None)

def back_low(kept, grad):
    return (low(grad),)
low.defvjp(low_keep, low_pass)
low_back.defvjp(back_keep, back_low)

def rms_scale(values, norm_gain):
    factor = lax.rsqrt(lax.optimization_barrier(jnp.mean(values * values, axis=-1, keepdims=True)) + NORM_EPSILON)
    return values * factor * norm_gain

def rope_tables(positions, head_width):
    half_width = head_width // 2
    frequency = ROPE_BASE ** (-(jnp.arange(half_width, dtype=jnp.float32) * 2.0) / head_width)
    angles = positions.astype(jnp.float32)[:, None] * frequency[None, :]
    return (jnp.cos(angles), jnp.sin(angles))

def rotate(values, cosine_table, sine_table):
    half_width = values.shape[-1] // 2
    front_part = values[..., :half_width]
    back_part = values[..., half_width:]
    cosine_rows = cosine_table[:, None, :]
    sine_rows = sine_table[:, None, :]
    return jnp.concatenate([front_part * cosine_rows - back_part * sine_rows, back_part * cosine_rows + front_part * sine_rows], axis=-1)

def clamped_glu(joined, expert_width):
    gate_part = jnp.minimum(joined[:, :expert_width], CLAMP_LIMIT)
    linear_part = jnp.clip(joined[:, expert_width:], -CLAMP_LIMIT, CLAMP_LIMIT)
    return (linear_part + 1.0) * gate_part * jax.nn.sigmoid(SWIGLU_SLOPE * gate_part)

def attend_sequence(queries, key_rows, value_rows, sink_logits):
    group_size = HEADS // KV_HEADS
    score_scale = HD ** (-0.5)
    grouped = queries.reshape(LENGTH, KV_HEADS, group_size, HD)
    sink_grid = sink_logits.reshape(KV_HEADS, group_size)
    columns = jnp.arange(LENGTH, dtype=jnp.int32)

    def one_block(block_index):
        begin_row = block_index * QBLOCK
        block_queries = lax.dynamic_slice_in_dim(grouped, begin_row, QBLOCK, 0)
        scores = low_back(jnp.einsum('qgrd,kgd->grqk', block_queries, key_rows, precision=PRECISE) * score_scale)
        row_ids = begin_row + jnp.arange(QBLOCK, dtype=jnp.int32)
        allowed = (row_ids[:, None] >= columns[None, :])[None, None]
        scores = jnp.where(allowed, scores, -1e+30)
        row_peak = jnp.maximum(lax.optimization_barrier(jnp.max(scores, axis=-1)), sink_grid[:, :, None])
        weights = jnp.where(allowed, jnp.exp(scores - row_peak[..., None]), 0.0)
        row_total = lax.optimization_barrier(jnp.sum(weights, axis=-1)) + jnp.exp(sink_grid[:, :, None] - row_peak)
        weights_low = low(weights / row_total[..., None])
        mixed = jnp.einsum('grqk,kgd->qgrd', weights_low, value_rows, precision=PRECISE)
        return mixed.reshape(QBLOCK, HEADS * HD)
    blocks = lax.map(jax.checkpoint(one_block), jnp.arange(LENGTH // QBLOCK, dtype=jnp.int32))
    return blocks.reshape(LENGTH, HEADS * HD)

def slot_places(flat_routes):
    blocks = flat_routes.reshape(SEQS * N_SEQ, TOK_DEV * TOPK)
    one_hot = (blocks[..., None] == jnp.arange(EXPERTS, dtype=jnp.int32)).astype(jnp.int32)
    earlier = jnp.cumsum(one_hot, axis=1) - one_hot
    slot_ids = lax.optimization_barrier(jnp.sum(earlier * one_hot, axis=-1))
    owners = jnp.arange(SEQS * N_SEQ, dtype=jnp.int32)[:, None]
    places = (owners * EXPERTS + blocks) * CAP + slot_ids
    return places.reshape(SEQS * LENGTH, TOPK).astype(jnp.int32)

def run_expert(expert_pack):
    expert_rows, joined_weight, joined_bias, down_part, down_shift = expert_pack
    joined = low_back(jnp.dot(expert_rows, joined_weight, precision=PRECISE) + joined_bias)
    activated = low(clamped_glu(joined, FF))
    return jnp.dot(activated, down_part, precision=PRECISE) + down_shift

def forward(hidden, norm1_gain, qkv_weight, qkv_bias, sink_logits, out_weight, out_bias, norm2_gain, router_weight, router_bias, gate_up_weight, gate_up_bias, down_weight, down_bias, routes):
    normed = low(rms_scale(hidden, norm1_gain))
    projected = low_back(jnp.einsum('bld,de->ble', normed, qkv_weight, precision=PRECISE) + qkv_bias)
    query_width = HEADS * HD
    pair_width = KV_HEADS * HD
    queries = projected[..., :query_width].reshape(SEQS, LENGTH, HEADS, HD)
    key_rows = projected[..., query_width:query_width + pair_width].reshape(SEQS, LENGTH, KV_HEADS, HD)
    value_rows = projected[..., query_width + pair_width:].reshape(SEQS, LENGTH, KV_HEADS, HD)
    cosine_table, sine_table = rope_tables(jnp.arange(LENGTH, dtype=jnp.int32), HD)
    queries = low_back(low(rotate(queries, cosine_table, sine_table)))
    key_rows = low_back(low(rotate(key_rows, cosine_table, sine_table)))
    value_rows = low_back(low(value_rows))
    attended = lax.map(lambda triple: attend_sequence(triple[0], triple[1], triple[2], sink_logits), (queries, key_rows, value_rows))
    attended = low_back(low(attended))
    branch = low_back(jnp.einsum('ble,ed->bld', attended, out_weight, precision=PRECISE) + out_bias)
    middle = hidden + branch
    second_normed = low(rms_scale(middle, norm2_gain))
    logits = jnp.einsum('bld,de->ble', second_normed, router_weight, precision=PRECISE) + router_bias
    flat_rows = second_normed.reshape(SEQS * LENGTH, D)
    flat_routes = routes.reshape(SEQS * LENGTH, TOPK)
    places = slot_places(flat_routes)
    buffer_rows = jnp.zeros((SEQS * N_SEQ * EXPERTS * CAP, D), jnp.float32)
    buffer_rows = buffer_rows.at[places.reshape(-1)].add(jnp.repeat(flat_rows, TOPK, axis=0))
    buffer_rows = low_back(buffer_rows)
    by_expert = buffer_rows.reshape(SEQS * N_SEQ, EXPERTS, CAP, D).transpose(1, 0, 2, 3)
    by_expert = by_expert.reshape(EXPERTS, SEQS * N_SEQ * CAP, D)
    expert_out = lax.map(jax.checkpoint(run_expert), (by_expert, gate_up_weight, gate_up_bias, down_weight, down_bias))
    expert_out = low_back(low(expert_out))
    back_rows = expert_out.reshape(EXPERTS, SEQS * N_SEQ, CAP, D).transpose(1, 0, 2, 3).reshape(-1, D)
    picked = jnp.take(back_rows, places, axis=0)
    chosen = jnp.take_along_axis(logits.reshape(SEQS * LENGTH, EXPERTS), flat_routes, axis=1)
    mixing = jax.nn.softmax(chosen, axis=-1)
    combined = lax.optimization_barrier(jnp.sum(mixing[..., None] * picked, axis=1))
    return middle + combined.reshape(SEQS, LENGTH, D)

def reference(hidden, out_grad, routes, norm1_gain, qkv_weight, qkv_bias, sink_logits, out_weight, out_bias, norm2_gain, router_weight, router_bias, gate_up_weight, gate_up_bias, down_weight, down_bias):
    floats = tuple((member.astype(jnp.float32) for member in (hidden, norm1_gain, qkv_weight, qkv_bias, sink_logits, out_weight, out_bias, norm2_gain, router_weight, router_bias, gate_up_weight, gate_up_bias, down_weight, down_bias)))

    def routed_forward(*params):
        return forward(*params, routes)
    result, pullback = jax.vjp(routed_forward, *floats)
    gradients = pullback(out_grad.astype(jnp.float32))
    return (result.astype(jnp.bfloat16), gradients[0].astype(jnp.bfloat16), gradients[1], gradients[2], gradients[3], gradients[4], gradients[5], gradients[6], gradients[7], gradients[8], gradients[9], gradients[10], gradients[11], gradients[12], gradients[13])
```

```python
import functools
import math

import jax
import jax.numpy as jnp
import numpy as np
from jax import lax
from jax.experimental.layout import Layout, with_layout_constraint
from jax.experimental import pallas as pl
from jax.experimental.pallas import tpu as pltpu
from jax.sharding import PartitionSpec as P

KV_HEADS = 8
HD = 64
TOPK = 4

ROPE_BASE = 150000.0
SWIGLU_SLOPE = 1.702
CLAMP_LIMIT = 7.0
NORM_EPSILON = 1e-05
PRECISE = lax.Precision.HIGHEST
BOTH = ("fsdp", "seq")
LOW = jnp.bfloat16
WIDE = jnp.float32
NN = (((1,), (0,)), ((), ()))
NT = (((1,), (1,)), ((), ()))
TN = (((0,), (0,)), ((), ()))


def mul(left, right, dims=NN):
    return lax.dot_general(left, right, dims, preferred_element_type=WIDE)


def straight(values):
    return with_layout_constraint(values, Layout(major_to_minor=tuple(range(values.ndim))))


def blank(shape, dtype):
    return pl.pallas_call(
        lambda out: None,
        out_specs=pl.BlockSpec(memory_space=pl.ANY),
        out_shape=jax.ShapeDtypeStruct(shape, dtype),
        name="blank",
    )()


def ring_order(count):
    return list(range(0, count, 2)) + list(range(1, count, 2))[::-1]


def ring_pairs(count):
    order = ring_order(count)
    ahead = [(order[i], order[(i + 1) % count]) for i in range(count)]
    return ahead, [(b, a) for a, b in ahead]


def ring_ids():
    count = lax.axis_size("seq")
    order = ring_order(count)
    rank = {p: i for i, p in enumerate(order)}
    table = [[order[(rank[p] + j) % count] for j in range(count)] for p in range(count)]
    return jnp.asarray(np.array(table, np.int32))[lax.axis_index("seq")]


def send(values, axis, pairs):
    if values.ndim == 2 and values.shape[0] % 16 == 0:
        blocks = straight(values.reshape(values.shape[0] // 16, 16, values.shape[1]))
        return straight(lax.ppermute(blocks, axis, pairs)).reshape(values.shape)
    return straight(lax.ppermute(straight(values), axis, pairs))


def swap(values, axis, bit):
    return send(values, axis, [(i, i ^ bit) for i in range(lax.axis_size(axis))])


class Freight:
    def __init__(self):
        self.hurried, self.flying, self.pending = [], [], []
        self.now = 0

    def load(self, values, sizes, land, when, lags, start=0):
        for size, delay, lag in zip(sizes, when, lags):
            piece = values[start : start + size]
            start += size
            self.after(delay, piece, functools.partial(self.hurry, land=land, lag=lag))

    def hurry(self, values, land, lag=1):
        self.hurried.append((values, land, lag))

    def need(self, values, use):
        self.pending.append((values, use))

    def __call__(self, *values):
        self.now += 1
        due = self.pending + [(array, use) for array, use, when in self.flying if when <= self.now]
        self.flying = [flight for flight in self.flying if flight[2] > self.now]
        self.pending = []
        if due:
            out = lax.optimization_barrier((*values, *(array for array, _ in due)))
            values = out[: len(values)]
            for array, (_, use) in zip(out[len(values) :], due):
                use(array)
        going, self.hurried = self.hurried, []
        for fresh, use, lag in going:
            self.flying.append((swap(fresh, "fsdp", 2), use, self.now + lag))
        return values

    def after(self, events, values, use):
        if events == 0:
            return use(values)
        self.need(values, lambda held: self.after(events - 1, held, use))

    def chain(self, values, steps, use):
        if not steps:
            return use(values)
        self.need(values, lambda held: self.chain(steps[0](held), steps[1:], use))

    def blocks(self, terms, use):
        def near_there(near):
            away = straight((terms[2].astype(WIDE) + near[0].astype(WIDE)).astype(LOW))
            own = terms[0].astype(WIDE) + near[1].astype(WIDE)
            self.hurry(away, lambda far: use(own + far.astype(WIDE)), 2)

        self.need(swap(straight(jnp.stack([terms[3], terms[1]])), "fsdp", 1), near_there)

    def settle(self):
        while self.pending:
            due, self.pending = self.pending, []
            for array, use in due:
                use(array)

    def finish(self):
        self.settle()
        while self.flying or self.hurried:
            self.flying += [(swap(fresh, "fsdp", 2), use, 0) for fresh, use, _ in self.hurried]
            due, self.flying, self.hurried = self.flying, [], []
            for array, use, _ in due:
                use(array)
            self.settle()


def alone(*values):
    return values


def ring_gather_steps(rows, ids, beside=alone, after=None):
    count = lax.axis_size("seq")
    ahead, behind = ring_pairs(count)
    tokens = rows.shape[0]
    half = tokens // 2

    def put(full, part, index, offset=0):
        return straight(lax.dynamic_update_slice(full, part, (index * tokens + offset, 0)))

    rows = straight(rows)
    if after is not None:
        rows, _ = lax.optimization_barrier((rows, after))
    full = put(blank((count * tokens, rows.shape[1]), rows.dtype), rows, ids[0])
    up = down = rows
    for hop in range(1, (count + 1) // 2):
        up, down = beside(up, down)
        up, down = send(up, "seq", ahead), send(down, "seq", behind)
        landed = yield up, down
        if landed is not None:
            up, down = landed
            yield None
        full = put(put(full, up, ids[count - hop]), down, ids[hop])
    if count % 2 == 0:
        up, down = beside(straight(up[:half]), straight(down[half:]))
        up, down = send(up, "seq", ahead), send(down, "seq", behind)
        yield up, down
        full = put(put(full, up, ids[count // 2]), down, ids[count // 2], half)
    yield full, (up, down)


def ring_gather(rows, ids, beside=alone):
    for out in ring_gather_steps(rows, ids, beside):
        pass
    return out


def ring_reduce(term, ids, beside=alone):
    count = lax.axis_size("seq")
    ahead, behind = ring_pairs(count)
    middle = count // 2
    if count == 1:
        return term(ids[0])
    up = down = None
    if count % 2 == 0:
        whole = straight(term(ids[middle]).astype(LOW))
        half = whole.shape[0] // 2
        up, down = beside(straight(whole[:half]), straight(whole[half:]))
        up = send(up, "seq", ahead).astype(WIDE)
        down = send(down, "seq", behind).astype(WIDE)
        up = jnp.pad(up, ((0, half), (0, 0)))
        down = jnp.pad(down, ((half, 0), (0, 0)))
    for hop in range((count - 1) // 2, 0, -1):
        send_up = term(ids[hop])
        send_down = term(ids[count - hop])
        if up is not None:
            send_up, send_down = send_up + up, send_down + down
        send_up, send_down = beside(straight(send_up.astype(LOW)), straight(send_down.astype(LOW)))
        up = send(send_up, "seq", ahead).astype(WIDE)
        down = send(send_down, "seq", behind).astype(WIDE)
    return straight(term(ids[0]) + up + down)


def xor_steps(axis):
    def step(held, bit):
        return jnp.concatenate([held, swap(held, axis, bit)])

    bits = [1 << i for i in range((lax.axis_size(axis) - 1).bit_length())]
    return [functools.partial(step, bit=bit) for bit in bits]


def straighten(parts, axis):
    count = parts.shape[0]
    me = lax.axis_index(axis)
    bit = 1
    while bit < count:
        other = jnp.stack([parts[j ^ bit] for j in range(count)])
        parts = jnp.where((me & bit) != 0, other, parts)
        bit *= 2
    return parts


def sum_steps(axes):
    def step(values, axis, bit):
        return values + swap(values, axis, bit)

    return [
        functools.partial(step, axis=axis, bit=1 << i)
        for axis in axes
        for i in range((lax.axis_size(axis) - 1).bit_length())
    ]


def spread(total, parts):
    ends = [round(total * sum(parts[: i + 1]) / sum(parts) / 16) * 16 for i in range(len(parts))]
    ends[-1] = total
    return [end - start for start, end in zip([0] + ends, ends)]


def add_pieces(kept, pieces):
    total, sums = kept
    start = 0
    for piece in pieces:
        size = min(piece.shape[0], total.shape[0] - start)
        rows = total[start : start + size] + piece[:size].astype(WIDE)
        total = straight(lax.dynamic_update_slice(total, rows, (start, 0)))
        start += size
    return total, sums[0] + pieces[-1][-1].astype(WIDE)


UNIT_PARTS = [
    3, 1, 2, 1, 0, 1, 3, 2, 1, 0, 0, 1, 2, 0, 0, 3, 3, 3, 1, 2, 0, 0, 1, 1, 0, 1, 2, 1, 0, 3, 0, 3,
    0, 2, 0, 2, 0, 2, 0, 1, 1, 2, 0, 1, 1, 3, 1, 3, 3, 3, 0, 1, 2, 1, 0, 1, 1, 0, 1, 0, 2, 2, 0, 2,
    2, 0, 3, 0, 3, 3, 0, 0, 2, 1, 3, 3, 1, 2, 0, 1, 3, 0, 1, 0, 2, 2, 2, 1, 3, 3, 3, 2, 2, 3, 1, 0,
    0, 3, 3, 3, 0, 1, 2, 2, 3, 2, 2, 2, 1, 0, 0, 1, 1, 3, 3, 2, 1, 1, 1, 1, 2, 0, 3, 2, 0, 3, 0, 0,
    3, 2, 2, 2, 3, 3, 3, 3, 1, 1, 1, 0, 0, 3, 2, 2, 2, 3, 2, 3, 3, 2, 2, 3, 2, 2, 0, 1, 1, 1, 0, 3,
]
BLOCK_PARTS = [
    0, 3, 1, 2, 2, 3, 0, 1, 1, 2, 3, 0, 3, 0, 1, 2, 3, 0, 1, 2, 1, 0, 2, 3, 1, 2, 3, 0, 2, 3, 1, 0,
]


def group_places(groups):
    return [1, 4, 6, 3, 2, 0, 5, 7] if groups == 8 else list(range(groups))


@functools.lru_cache(None)
def unit_plan(fsdp, groups, query_width, pair_width):
    columns = query_width + 2 * pair_width
    per_device = columns // (fsdp * groups)
    group_query, group_pair = query_width // groups, pair_width // groups
    unit = math.gcd(math.gcd(per_device, group_query), group_pair)
    rounds = per_device // unit
    total = fsdp * groups
    wanted = []
    for index in range(columns // unit):
        column = index * unit
        if column < query_width:
            group, place = divmod(column, group_query)
        elif column < query_width + pair_width:
            group, place = divmod(column - query_width, group_pair)
            place += group_query
        else:
            group, place = divmod(column - query_width - pair_width, group_pair)
            place += group_query + group_pair
        wanted.append((index // rounds, index % rounds, group, place // unit))
    filled = {}
    edges = []
    near = UNIT_PARTS if groups == 8 and len(wanted) == len(UNIT_PARTS) else None
    spots = group_places(groups)
    for index, (source, slot, group, place) in enumerate(wanted):
        own = near[index] if near else source // groups
        for turn in (0, 1, 2, 3):
            part = own ^ turn
            if filled.get((part, group), 0) < rounds:
                filled[(part, group)] = filled.get((part, group), 0) + 1
                edges.append((source, slot, part * groups + spots[group], place))
                break
    steps = []
    for _ in range(rounds):
        taken = {}

        def find(source, seen):
            for edge in edges:
                if edge[0] != source or edge[2] in seen:
                    continue
                seen.add(edge[2])
                if edge[2] not in taken or find(taken[edge[2]][0], seen):
                    taken[edge[2]] = edge
                    return True
            return False

        for source in range(total):
            find(source, set())
        steps.append(sorted(taken.values()))
        for edge in taken.values():
            edges.remove(edge)
    send = np.zeros((rounds, total), np.int32)
    place_at = np.zeros((rounds, total), np.int32)
    pairs = []
    for i, step in enumerate(steps):
        pairs.append([(edge[0], edge[2]) for edge in step])
        for source, slot, target, place in step:
            send[i, source] = slot
            place_at[i, target] = place
    count = fsdp * rounds
    order = np.zeros((total, count), np.int32)
    back = np.zeros((total, count), np.int32)
    for device in range(total):
        part, group = divmod(device, groups)
        for j in range(fsdp):
            for i in range(rounds):
                place = place_at[i, (part ^ j) * groups + group]
                order[device, place] = j * rounds + i
                back[device, j * rounds + i] = place
    home = np.argsort(send, axis=0).astype(np.int32)
    return unit, rounds, pairs, send, order, back, home


def out_pairs(fsdp, groups):
    total = fsdp * groups
    parts = BLOCK_PARTS if (fsdp, groups) == (4, 8) else [b % fsdp for b in range(total)]
    spots = group_places(groups)
    moves = [(b, parts[b] * groups + spots[b // fsdp]) for b in range(total)]
    found = np.zeros((total, fsdp), np.int32)
    for b, target in moves:
        part, spot = divmod(target, groups)
        for turn in range(fsdp):
            found[(part ^ turn) * groups + spot, b % fsdp] = turn
    return moves, found


def turn(front, back, cosine, sine):
    return front * cosine - back * sine, back * cosine + front * sine


def forward_kernel(
    at_ref, sink_ref, front_ref, back_ref, key_front, key_back, value_front, value_back,
    query_bias, pair_bias, cos_ref, sin_ref,
    turned_ref, pairs_ref, out_ref, total_ref, keys,
    *, block, scale,
):
    head = pl.program_id(0)
    length = front_ref.shape[1]
    half = HD // 2
    cosine, sine = cos_ref[...], sin_ref[...]

    @pl.when(head == 0)
    def _():
        front, back = turn(
            key_front[...] + pair_bias[:half], key_back[...] + pair_bias[half:HD], cosine, sine
        )
        key = jnp.concatenate([front, back], axis=0)
        pairs_ref[:HD, :] = key.astype(LOW)
        pairs_ref[HD : HD + half, :] = (value_front[...] + pair_bias[HD : HD + half]).astype(LOW)
        pairs_ref[HD + half :, :] = (value_back[...] + pair_bias[HD + half :]).astype(LOW)
        keys[...] = key.T.astype(LOW)

    front, back = turn(
        front_ref[...] + query_bias[:half], back_ref[...] + query_bias[half:], cosine, sine
    )
    turned_ref[:half, :] = (front.astype(LOW).astype(WIDE) * scale).astype(LOW)
    turned_ref[half:, :] = (back.astype(LOW).astype(WIDE) * scale).astype(LOW)
    sink = sink_ref[head]
    count = length // block
    below = lax.broadcasted_iota(jnp.int32, (block, block), 0) > lax.broadcasted_iota(
        jnp.int32, (block, block), 1
    )
    for index in range(count):
        columns = pl.ds(index * block, block)
        query = turned_ref[:, columns]

        def scores(rows):
            return mul(keys[rows, :], query)

        def step(start, carry, masked):
            peak, total, mixed = carry
            rows = pl.ds(start, block)
            tile = scores(rows)
            if masked:
                tile = jnp.where(below, -1e30, tile)
            top = jnp.maximum(peak, jnp.max(tile, axis=0, keepdims=True))
            weights = jnp.exp(tile - top)
            shrink = jnp.exp(peak - top)
            total = total * shrink + jnp.sum(weights, axis=0, keepdims=True)
            mixed = mixed * shrink + mul(pairs_ref[HD:, rows], weights.astype(LOW))
            return top, total, mixed

        carry = (
            jnp.full((1, block), sink, WIDE),
            jnp.ones((1, block), WIDE),
            jnp.zeros((HD, block), WIDE),
        )
        if count <= 4:
            for earlier in range(index):
                carry = step(earlier * block, carry, False)
        elif index:
            carry = lax.fori_loop(
                0, index, lambda i, c: step(pl.multiple_of(i * block, block), c, False), carry
            )
        peak, total, mixed = step(index * block, carry, True)
        out_ref[:, columns] = (mixed / total).astype(LOW)
        total_ref[0, :, columns] = peak + jnp.log(total)


def attend(at, projected, bias, sinks, cosine, sine, heads):
    length = projected.shape[1]
    rows = heads * HD
    half = HD // 2
    block = min(256, length)
    last = rows // (2 * HD)

    def piece(place):
        return pl.BlockSpec((half, length), lambda h, at: (at[place], 0))

    return pl.pallas_call(
        functools.partial(forward_kernel, block=block, scale=HD**-0.5),
        grid_spec=pltpu.PrefetchScalarGridSpec(
            num_scalar_prefetch=1,
            grid=(heads,),
            in_specs=[
                pl.BlockSpec(memory_space=pltpu.SMEM),
                pl.BlockSpec((half, length), lambda h, at: (at[2 * h], 0)),
                pl.BlockSpec((half, length), lambda h, at: (at[2 * h + 1], 0)),
                piece(2 * heads),
                piece(2 * heads + 1),
                piece(2 * heads + 2),
                piece(2 * heads + 3),
                pl.BlockSpec((HD, 1), lambda h, at: (h, 0)),
                pl.BlockSpec((2 * HD, 1), lambda h, at: (last, 0)),
                pl.BlockSpec((half, length), lambda h, at: (0, 0)),
                pl.BlockSpec((half, length), lambda h, at: (0, 0)),
            ],
            out_specs=[
                pl.BlockSpec((HD, length), lambda h, at: (h, 0)),
                pl.BlockSpec((2 * HD, length), lambda h, at: (0, 0)),
                pl.BlockSpec((HD, length), lambda h, at: (at[2 * heads + 4 + h], 0)),
                pl.BlockSpec((1, 1, length), lambda h, at: (h, 0, 0)),
            ],
            scratch_shapes=[pltpu.VMEM((length, HD), LOW)],
        ),
        out_shape=[
            jax.ShapeDtypeStruct((rows, length), LOW),
            jax.ShapeDtypeStruct((2 * HD, length), LOW),
            jax.ShapeDtypeStruct((rows, length), LOW),
            jax.ShapeDtypeStruct((heads, 1, length), WIDE),
        ],
        compiler_params=pltpu.CompilerParams(
            dimension_semantics=("arbitrary",), vmem_limit_bytes=40 * 2**20
        ),
        cost_estimate=pl.CostEstimate(
            flops=0, bytes_accessed=0, transcendentals=0
        ),
        name="attend",
    )(at, sinks, *[projected] * 6, bias, bias, cosine, sine)


def backward_kernel(
    at_ref, sink_ref, turned_ref, pairs_ref, out_ref, grad_ref, total_ref, cos_ref, sin_ref,
    query_ref, pair_ref, sink_grad_ref, keys, values, key_sum, value_sum, query_rows, grad_rows,
    *, block, scale,
):
    head = pl.program_id(0)
    length = turned_ref.shape[1]
    half = HD // 2
    count = length // block

    @pl.when(head == 0)
    def _():
        keys[...] = pairs_ref[:HD, :].astype(WIDE).T.astype(LOW)
        values[...] = pairs_ref[HD:, :].astype(WIDE).T.astype(LOW)
        key_sum[...] = jnp.zeros_like(key_sum)
        value_sum[...] = jnp.zeros_like(value_sum)

    query_rows[...] = turned_ref[...].astype(WIDE).T.astype(LOW)
    grad_rows[...] = grad_ref[...].astype(WIDE).T.astype(LOW)
    below = lax.broadcasted_iota(jnp.int32, (block, block), 0) > lax.broadcasted_iota(
        jnp.int32, (block, block), 1
    )
    deltas = jnp.sum(grad_ref[...].astype(WIDE) * out_ref[...].astype(WIDE), axis=0, keepdims=True)
    totals = total_ref[0]
    sink_term = -jnp.sum(jnp.exp(sink_ref[head] - totals) * deltas, axis=1, keepdims=True)
    sink_grad_ref[0] = jnp.broadcast_to(sink_term, (1, 128))
    for index in range(count):
        columns = pl.ds(index * block, block)
        query = turned_ref[:, columns]
        grad = grad_ref[:, columns]
        total = totals[:, index * block : (index + 1) * block]
        delta = deltas[:, index * block : (index + 1) * block]

        def step(start, query_sum, masked):
            rows = pl.ds(start, block)
            weights = jnp.exp(mul(keys[rows, :], query) - total)
            if masked:
                weights = jnp.where(below, 0.0, weights)
            inner = (weights * (mul(values[rows, :], grad) - delta)).astype(LOW)
            key_sum[rows, :] += mul(inner, query_rows[columns, :])
            value_sum[rows, :] += mul(weights.astype(LOW), grad_rows[columns, :])
            return query_sum + mul(pairs_ref[:HD, rows], inner)

        query_sum = jnp.zeros((HD, block), WIDE)
        if count <= 4:
            for earlier in range(index):
                query_sum = step(earlier * block, query_sum, False)
        elif index:
            query_sum = lax.fori_loop(
                0, index, lambda i, c: step(pl.multiple_of(i * block, block), c, False), query_sum
            )
        query_sum = step(index * block, query_sum, True)
        rounded = (query_sum * scale).astype(LOW).astype(WIDE)
        cosine, sine = cos_ref[:, columns], sin_ref[:, columns]
        front, back = turn(rounded[:half], rounded[half:], cosine, -sine)
        query_ref[:half, columns] = front.astype(LOW)
        query_ref[half:, columns] = back.astype(LOW)

    @pl.when(head == pl.num_programs(0) - 1)
    def _():
        rounded = key_sum[...].T.astype(LOW).astype(WIDE)
        front, back = turn(rounded[:half], rounded[half:], cos_ref[...], -sin_ref[...])
        pair_ref[:half, :] = front.astype(LOW)
        pair_ref[half:HD, :] = back.astype(LOW)
        pair_ref[HD:, :] = value_sum[...].T.astype(LOW)


def attend_back(at, sinks, turned, pairs, attended, upstream, totals, cosine, sine):
    heads, _, length = totals.shape
    rows = heads * HD
    block = min(256, length)
    by_head = pl.BlockSpec((HD, length), lambda h, at: (h, 0))
    moved = pl.BlockSpec((HD, length), lambda h, at: (at[2 * heads + 4 + h], 0))
    table = pl.BlockSpec((HD // 2, length), lambda h, at: (0, 0))
    whole = pl.BlockSpec((2 * HD, length), lambda h, at: (0, 0))
    return pl.pallas_call(
        functools.partial(backward_kernel, block=block, scale=HD**-0.5),
        grid_spec=pltpu.PrefetchScalarGridSpec(
            num_scalar_prefetch=1,
            grid=(heads,),
            in_specs=[
                pl.BlockSpec(memory_space=pltpu.SMEM),
                by_head,
                whole,
                moved,
                moved,
                pl.BlockSpec((1, 1, length), lambda h, at: (h, 0, 0)),
                table,
                table,
            ],
            out_specs=[by_head, whole, pl.BlockSpec((1, 1, 128), lambda h, at: (h, 0, 0))],
            scratch_shapes=[
                pltpu.VMEM((length, HD), LOW),
                pltpu.VMEM((length, HD), LOW),
                pltpu.VMEM((length, HD), WIDE),
                pltpu.VMEM((length, HD), WIDE),
                pltpu.VMEM((length, HD), LOW),
                pltpu.VMEM((length, HD), LOW),
            ],
        ),
        out_shape=[
            jax.ShapeDtypeStruct((rows, length), LOW),
            jax.ShapeDtypeStruct((2 * HD, length), LOW),
            jax.ShapeDtypeStruct((heads, 1, 128), WIDE),
        ],
        compiler_params=pltpu.CompilerParams(
            dimension_semantics=("arbitrary",), vmem_limit_bytes=40 * 2**20
        ),
        cost_estimate=pl.CostEstimate(
            flops=0, bytes_accessed=0, transcendentals=0
        ),
        name="attend_back",
    )(at, sinks, turned, pairs, attended, upstream, totals, cosine, sine)


EXTRA = 16


def term_kernel(at_ref, left_ref, right_ref, *refs, others):
    size = left_ref.shape[0]
    total = mul(left_ref[...], right_ref[...])
    sums = jnp.sum(right_ref[...].astype(WIDE), axis=0, keepdims=True)
    sums = jnp.broadcast_to(sums, (EXTRA, sums.shape[1]))
    for other in refs[:others]:
        total = total + other[:size, :].astype(WIDE)
        sums = sums + other[size:, :].astype(WIDE)
    if len(refs) > others + 1:
        refs[-2][...], refs[-1][...] = total, sums
    else:
        refs[-1][:size, :] = total.astype(LOW)
        refs[-1][size:, :] = sums.astype(LOW)


def weight_term(left, right, index, size, *others, final=False):
    depth, width = right.shape
    block = min(640, width)
    at = jnp.full((1,), index, jnp.int32)

    def tile(rows):
        return pl.BlockSpec((rows, block), lambda n, at: (0, n))

    low = jax.ShapeDtypeStruct((size + EXTRA, width), LOW)
    split = [jax.ShapeDtypeStruct((rows, width), WIDE) for rows in (size, EXTRA)]
    return pl.pallas_call(
        functools.partial(term_kernel, others=len(others)),
        grid_spec=pltpu.PrefetchScalarGridSpec(
            num_scalar_prefetch=1,
            grid=(pl.cdiv(width, block),),
            in_specs=[
                pl.BlockSpec((size, depth), lambda n, at: (at[0], 0)),
                pl.BlockSpec((depth, block), lambda n, at: (0, n)),
                *[tile(size + EXTRA)] * len(others),
            ],
            out_specs=[tile(size), tile(EXTRA)] if final else tile(size + EXTRA),
        ),
        out_shape=split if final else low,
        compiler_params=pltpu.CompilerParams(
            dimension_semantics=("arbitrary",), vmem_limit_bytes=32 * 2**20
        ),
        cost_estimate=pl.CostEstimate(
            flops=2 * size * depth * width,
            bytes_accessed=2 * (depth * (size + width) + (2 + len(others)) * size * width),
            transcendentals=0,
        ),
        name="weight_term",
    )(at, left, right, *others)


def rms_scale(values, norm_gain):
    factor = lax.rsqrt(jnp.mean(values * values, axis=-1, keepdims=True) + NORM_EPSILON)
    return (values * factor * norm_gain, factor)


def rms_back(values, factor, norm_gain, upstream):
    scaled = upstream * norm_gain
    value_grad = factor * scaled - values * factor * factor * factor * jnp.mean(
        scaled * values, axis=-1, keepdims=True
    )
    gain_grad = jnp.sum(upstream * values * factor, axis=0)
    return (value_grad, gain_grad)


def clamped_glu(joined, expert_width):
    gate_part = jnp.minimum(joined[:, :expert_width], CLAMP_LIMIT)
    linear_part = jnp.clip(joined[:, expert_width:], -CLAMP_LIMIT, CLAMP_LIMIT)
    return (linear_part + 1.0) * gate_part * jax.nn.sigmoid(SWIGLU_SLOPE * gate_part)


def glu_back(joined, expert_width, upstream):
    raw_gate = joined[:, :expert_width]
    raw_linear = joined[:, expert_width:]
    gate_part = jnp.minimum(raw_gate, CLAMP_LIMIT)
    linear_part = jnp.clip(raw_linear, -CLAMP_LIMIT, CLAMP_LIMIT)
    sigmoid_part = jax.nn.sigmoid(SWIGLU_SLOPE * gate_part)
    gate_open = (raw_gate < CLAMP_LIMIT).astype(jnp.float32)
    linear_open = (jnp.abs(raw_linear) < CLAMP_LIMIT).astype(jnp.float32)
    slope_part = sigmoid_part + gate_part * SWIGLU_SLOPE * sigmoid_part * (1.0 - sigmoid_part)
    gate_grad = upstream * (linear_part + 1.0) * slope_part * gate_open
    linear_grad = upstream * gate_part * sigmoid_part * linear_open
    return jnp.concatenate([gate_grad, linear_grad], axis=1)


def mixing_of(rows, routes, router_weight, router_bias):
    logits = mul(rows, router_weight) + router_bias
    experts = jnp.arange(router_bias.shape[0], dtype=jnp.int32)
    chosen = jnp.any(routes[:, :, None] == experts, axis=1)
    logits = jnp.where(chosen, logits, -jnp.inf)
    weights = jnp.exp(logits - jnp.max(logits, axis=1, keepdims=True))
    return weights / jnp.sum(weights, axis=1, keepdims=True)


def rows_of(values, index, size):
    return lax.dynamic_slice_in_dim(values, index * size, size, axis=0)


def columns_of(values, index, size):
    return lax.dynamic_slice_in_dim(values, index * size, size, axis=1)


def body(
    hidden,
    out_grad,
    routes,
    norm1_gain,
    qkv_weight,
    qkv_bias,
    sink_logits,
    out_weight,
    out_bias,
    norm2_gain,
    router_weight,
    router_bias,
    gate_up_weight,
    gate_up_bias,
    down_weight,
    down_bias,
):
    tokens = hidden.shape[1]
    groups = lax.axis_size("seq")
    position = lax.axis_index("seq")
    spots = np.argsort(np.array(group_places(lax.axis_size("seq")))).astype(np.int32)
    group = jnp.asarray(spots)[position]
    fsdp = lax.axis_size("fsdp")
    part = lax.axis_index("fsdp")
    device = part * groups + position
    head_count = sink_logits.shape[0]
    group_heads = head_count // groups
    expert_width = down_weight.shape[1] * fsdp
    capacity = tokens * TOPK * 9 // (8 * groups)
    slot_count = groups * capacity
    length = tokens * groups
    query_width = head_count * HD
    pair_width = KV_HEADS * HD
    group_query = group_heads * HD
    ids = ring_ids()

    planned = groups == KV_HEADS and fsdp == 4 and qkv_weight.shape[1] % (HD // 2) == 0
    qkv_rows = straight(qkv_weight.T)
    held = {}
    freight = Freight()
    out_moves, out_found = out_pairs(fsdp, groups)

    def keep(name):
        return lambda values: held.__setitem__(name, values)

    def gather_parts(name):
        def land(far):
            mine = held[name]

            def near(other):
                held[name] = jnp.stack([mine, other[0], far, other[1]])

            freight.need(swap(jnp.stack([mine, far]), "fsdp", 1), near)

        return land

    def arrived(name, lag=1):
        def use(block):
            held[name] = block
            freight.hurry(block, gather_parts(name), lag)

        return use

    if planned:
        unit, rounds, pairs, send_slots, order, back, home = unit_plan(
            fsdp, groups, query_width, pair_width
        )
        slots = jnp.asarray(send_slots)[:, device]
        bias_at = (group, group, group)
        head_units = jnp.asarray(order)[device]
        units = qkv_rows.reshape(rounds, unit, -1)
        blocks = [
            send(lax.dynamic_index_in_dim(units, slots[i], 0, keepdims=False), BOTH, pairs[i])
            for i in range(rounds)
        ]
        freight.after(1, straight(jnp.stack(blocks)), arrived("qkv"))
    else:
        pair_index = group * KV_HEADS // groups
        bias_at = (group, pair_index, pair_index)
        head_units = jnp.arange(2 * group_heads + 4, dtype=jnp.int32)
    bias_group = jnp.concatenate(
        [
            rows_of(qkv_bias[:query_width], bias_at[0], group_query),
            rows_of(qkv_bias[query_width : query_width + pair_width], bias_at[1], HD),
            rows_of(qkv_bias[query_width + pair_width :], bias_at[2], HD),
        ]
    )
    block_heads = out_weight.shape[0] // HD
    by_block = out_weight.shape[0] % HD == 0
    head_ids = jnp.arange(group_heads, dtype=jnp.int32)
    if by_block:
        turns = jnp.asarray(np.repeat(out_found, block_heads, axis=1))[device]
        head_ids = turns * block_heads + head_ids % block_heads
    places_at = jnp.concatenate([head_units, head_ids])

    def open_out(weight):
        freight.need(send(weight, BOTH, out_moves), arrived("out", 2))

    def open_expert(name):
        def use(shard):
            held[name] = lax.all_gather(shard, "fsdp", axis=0, tiled=True)

        return use

    freight.need(out_weight, open_out)
    freight.after(4, gate_up_weight[0], open_expert("gate_up"))
    freight.after(4, down_weight[0], open_expert("down"))

    inputs = hidden[0].astype(WIDE)
    first_normed, first_factor = rms_scale(inputs, norm1_gain)
    first_full, first_last = ring_gather(first_normed.astype(LOW), ids, freight)
    frequency = ROPE_BASE ** (-(jnp.arange(HD // 2, dtype=WIDE) * 2.0) / HD)
    angles = jnp.arange(length, dtype=jnp.int32).astype(WIDE)[None, :] * frequency[:, None]
    cosine, sine = jnp.cos(angles), jnp.sin(angles)
    sink_part = rows_of(sink_logits, group, group_heads)
    gather = ring_gather_steps(out_grad[0], ids, freight, first_last)
    next(gather)
    if planned:
        qkv_group = straight(held["qkv"]).reshape(fsdp * rounds * unit, -1)
    else:
        qkv_full = lax.all_gather(qkv_rows, BOTH, axis=0, tiled=True)
        qkv_group = jnp.concatenate(
            [
                rows_of(qkv_full[:query_width], group, group_query),
                rows_of(qkv_full[query_width : query_width + pair_width], pair_index, HD),
                rows_of(qkv_full[query_width + pair_width :], pair_index, HD),
            ]
        )
    freight.need(mul(qkv_group, first_full, NT), keep("projected"))
    hop = next(gather)
    out_group = straight(held["out"])
    if not by_block:
        out_group = straight(straighten(out_group, "fsdp"))
    out_group = out_group.reshape(fsdp * out_weight.shape[0], -1)
    held["projected"], out_group = lax.optimization_barrier((held["projected"], out_group))
    turned, pair_rows, attended, log_totals = attend(
        places_at, held["projected"], bias_group[:, None], sink_part, cosine, sine, group_heads
    )

    freight.need(hop, gather.send)
    freight.chain(routes, xor_steps("seq"), keep("routes"))
    biases = jnp.concatenate([gate_up_bias, down_bias], axis=1)
    freight.chain(biases, xor_steps("fsdp"), keep("biases"))
    branch = ring_reduce(
        lambda index: mul(columns_of(attended, index, tokens), out_group, TN), ids, freight
    )
    middle = inputs + (branch + out_bias)
    second_normed, second_factor = rms_scale(middle, norm2_gain)
    second_low = second_normed.astype(LOW)

    second_full, last = ring_gather(second_low, ids, freight)
    freight.need(last[0], lambda values: None)
    next(gather)
    freight.settle()
    joined_weight, down_full = held["gate_up"], held["down"]
    all_routes = straighten(held["routes"], "seq").reshape(length, TOPK)
    biases = straighten(held["biases"], "fsdp")
    joined_bias = biases[:, : gate_up_bias.shape[1]].reshape(-1).astype(WIDE)
    down_shift = biases[:, gate_up_bias.shape[1] :].reshape(-1).astype(WIDE)
    mine = jnp.any(all_routes == position, axis=1)
    counted = mine.astype(jnp.int32)
    earlier = jnp.cumsum(counted) - counted
    places = jnp.where(mine, earlier, -1)
    slots_here = jnp.arange(slot_count, dtype=jnp.int32)
    into = slots_here[:, None] == places[None, :]
    back_to = places[:, None] == slots_here[None, :]
    into_low, back_low = into.astype(LOW), back_to.astype(LOW)
    mixing_all = mixing_of(second_full, all_routes, router_weight, router_bias)
    expert_ids = jnp.arange(groups, dtype=jnp.int32)
    mixing_mine = jnp.sum(jnp.where(expert_ids == position, mixing_all, 0.0), axis=1)
    mixing_rows = jnp.sum(jnp.where(into, mixing_mine[None, :], 0.0), axis=1)[:, None]
    expert_rows = mul(into_low, second_full).astype(LOW)
    joined = mul(expert_rows, joined_weight) + joined_bias
    activated = lax.optimization_barrier(clamped_glu(joined, expert_width).astype(LOW))
    expert_columns = expert_rows.T
    activated_rows = activated.T
    upstream_full = None
    for upstream_full in gather:
        pass
    upstream_full = upstream_full[0]
    freight.finish()
    freight = Freight()
    landed = {"down": [], "joined": []}
    down_rows = expert_width // fsdp
    joined_rows = hidden.shape[2] // fsdp

    def down_term(j, *others, final=False):
        return weight_term(activated_rows, rows_grad, part ^ j, down_rows, *others, final=final)

    def joined_term(j, *others, final=False):
        grad = held["joined_grad"]
        return weight_term(expert_columns, grad, part ^ j, joined_rows, *others, final=final)

    upstream_rows = mul(into_low, upstream_full)
    rows_grad = (upstream_rows * mixing_rows).astype(LOW)
    near = swap(down_term(3), "fsdp", 1)
    down_away = down_term(2, near)
    down_close = swap(down_term(1), "fsdp", 1)
    freight.load(down_away, [down_away.shape[0]], landed["down"].append, [1], [4])
    expert_out = (mul(activated, down_full) + down_shift).astype(LOW).astype(WIDE)
    weighted = (expert_out * mixing_rows).astype(LOW)
    mixing_grad_rows = jnp.sum(upstream_rows * expert_out, axis=1)

    def back_first(upstream):
        activated_grad = mul(upstream, down_full, NT)
        joined_grad = glu_back(joined, expert_width, activated_grad).astype(LOW)
        freight.need(joined_grad, back_second)

    def back_second(joined_grad):
        held["joined_grad"] = joined_grad
        near = swap(joined_term(3), "fsdp", 1)
        freight.need(joined_term(1), keep("joined_one"))
        freight.need(near, back_third)

    def back_third(near):
        held["joined_close"] = swap(held["joined_one"], "fsdp", 1)
        freight.need(held["joined_grad"], keep("joined_grad"))
        freight.need(joined_term(2, near), back_fourth)

    def back_fourth(away):
        sizes = spread(away.shape[0], [1, 1, 1])
        freight.load(away, sizes, landed["joined"].append, [1, 4, 7], [3, 3, 3])
        rows = mul(held["joined_grad"], joined_weight, NT).astype(LOW)
        held["input_rows_grad"] = rows

    freight.need(rows_grad, back_first)
    combined = ring_reduce(lambda index: mul(rows_of(back_low, index, tokens), weighted), ids, freight)
    outputs = middle + combined
    mixing_grad = jnp.sum(jnp.where(back_to, mixing_grad_rows[None, :], 0.0), axis=1)
    mixing_grad = lax.all_to_all(
        mixing_grad.reshape(groups, tokens), "seq", split_axis=0, concat_axis=0, tiled=True
    ).T
    if "input_rows_grad" not in held:
        freight.settle()
    joined_grad, input_rows_grad = held["joined_grad"], held["input_rows_grad"]
    def down_last(close):
        freight.need(down_term(0, close, final=True), keep("down_keep"))

    def joined_last(close):
        freight.need(joined_term(0, close, final=True), keep("joined_keep"))

    freight.after(2, down_close, down_last)
    freight.after(5, held["joined_close"], joined_last)
    second_grad = ring_reduce(
        lambda index: mul(rows_of(back_low, index, tokens), input_rows_grad), ids, freight
    )
    mixing = mixing_of(second_low, routes[0], router_weight, router_bias)
    logits_grad = mixing * (
        mixing_grad - jnp.sum(mixing * mixing_grad, axis=-1, keepdims=True)
    )
    second_grad = second_grad + jnp.dot(
        logits_grad, router_weight.astype(WIDE).T, precision=PRECISE
    )
    upstream = out_grad[0].astype(WIDE)
    middle_part, gain2_grad = rms_back(middle, second_factor, norm2_gain, second_grad)
    middle_grad = upstream + middle_part
    branch_low = middle_grad.astype(LOW)

    width = hidden.shape[2]

    router_weight_grad = jnp.dot(second_low.astype(WIDE).T, logits_grad, precision=PRECISE)
    router_bias_grad = jnp.sum(logits_grad, axis=0)
    out_bias_grad = jnp.sum(branch_low.astype(WIDE), axis=0)
    early = [out_bias_grad, gain2_grad, router_weight_grad.T.reshape(-1), router_bias_grad]
    early = jnp.concatenate(early)
    branch_full, _ = ring_gather(branch_low, ids, freight)
    heads_grad = mul(out_group, branch_full, NT).astype(LOW)
    query_grad, pair_grad, sink_grad = attend_back(
        places_at, sink_part, turned, pair_rows, attended, heads_grad, log_totals, cosine, sine
    )
    projected_grad = jnp.concatenate([query_grad, pair_grad])
    bias_term = jnp.sum(projected_grad.astype(WIDE), axis=1)
    if planned:
        projected_grad = jnp.take(
            projected_grad.reshape(fsdp * rounds, unit, -1),
            jnp.asarray(back)[device],
            axis=0,
            mode="clip",
        ).reshape(projected_grad.shape)

    bias_full = jnp.zeros((query_width + 2 * pair_width,), WIDE)
    bias_full = lax.dynamic_update_slice(
        bias_full, bias_term[:group_query], (bias_at[0] * group_query,)
    )
    bias_full = lax.dynamic_update_slice(
        bias_full, bias_term[group_query : group_query + HD], (query_width + bias_at[1] * HD,)
    )
    bias_full = lax.dynamic_update_slice(
        bias_full,
        bias_term[group_query + HD :],
        (query_width + pair_width + bias_at[2] * HD,),
    )
    sink_full = lax.dynamic_update_slice_in_dim(
        jnp.zeros((head_count,), WIDE), sink_grad[:, 0, 0], group * group_heads, 0
    )

    def out_first(grad):
        terms = straight(mul(attended, grad).astype(LOW)).reshape(fsdp, out_weight.shape[0], -1)
        if not by_block:
            terms = straight(straighten(terms, "fsdp"))

        def use(total):
            back = [(b, a) for a, b in out_moves]
            freight.need(send(total.astype(LOW), BOTH, back), keep("out_shard"))

        freight.blocks(terms, use)

    def qkv_first(grad):
        terms = mul(grad, first_full)
        low = straight(terms.astype(LOW))
        sums = jnp.sum(low.astype(WIDE) * qkv_group.astype(WIDE), axis=0) / norm1_gain
        values = jnp.concatenate([sums, bias_full, sink_full, early])
        for step in sum_steps(BOTH):
            values = step(values)
        held["late"] = values
        if not planned:
            held["qkv_term"] = terms
            return

        def use(total):
            total = total.astype(LOW)
            returned = [
                send(total[i], BOTH, [(b, a) for a, b in pairs[i]]) for i in range(rounds)
            ]
            freight.need(straight(jnp.stack(returned)), keep("returned"))

        freight.blocks(low.reshape(fsdp, rounds, unit, -1), use)

    freight.need(projected_grad, qkv_first)
    freight.need(branch_full, out_first)
    first_grad = ring_reduce(
        lambda index: mul(columns_of(projected_grad, index, tokens), qkv_group, TN), ids, freight
    )
    freight.finish()
    down_shard, bias_sums = add_pieces(held["down_keep"], landed["down"])
    down_bias_shard = rows_of(bias_sums, part, down_bias.shape[1])
    joined_shard, bias_sums = add_pieces(held["joined_keep"], landed["joined"])
    joined_bias_shard = rows_of(bias_sums, part, gate_up_bias.shape[1])
    out_shard = held["out_shard"].astype(WIDE)
    if planned:
        qkv_shard = jnp.take(held["returned"], jnp.asarray(home)[:, device], axis=0, mode="clip")
        qkv_shard = qkv_shard.reshape(rounds * unit, -1).T.astype(WIDE)
    else:
        qkv_term = held["qkv_term"]
        scattered = jnp.zeros((query_width + 2 * pair_width, width), WIDE)
        for start, stop, row in (
            (0, group_query, group * group_query),
            (group_query, group_query + HD, query_width + pair_index * HD),
            (group_query + HD, group_query + 2 * HD, query_width + pair_width + pair_index * HD),
        ):
            scattered = lax.dynamic_update_slice(scattered, qkv_term[start:stop], (row, 0))
        qkv_shard = lax.psum_scatter(scattered, BOTH, scatter_dimension=0, tiled=True).T
    input_part, _ = rms_back(inputs, first_factor, norm1_gain, first_grad)
    input_grad = middle_grad + input_part

    late = held["late"]
    early = late[width + qkv_bias.shape[0] + head_count :]
    router_sums = early[2 * width : 2 * width + width * groups].reshape(groups, width).T
    return (
        outputs.astype(LOW)[None],
        input_grad.astype(LOW)[None],
        late[:width],
        qkv_shard,
        late[width : width + qkv_bias.shape[0]],
        late[width + qkv_bias.shape[0] : width + qkv_bias.shape[0] + head_count],
        out_shard,
        early[:width],
        early[width : 2 * width],
        router_sums,
        early[2 * width + width * groups : 2 * width + (width + 1) * groups],
        joined_shard[None],
        joined_bias_shard[None],
        down_shard[None],
        down_bias_shard[None],
    )


def solution(mesh):
    tokens = P("fsdp", "seq", None)
    by_expert = P("seq", "fsdp", None)
    return jax.shard_map(
        body,
        mesh=mesh,
        in_specs=(
            tokens, tokens, tokens, P(), P(None, BOTH), P(), P(), P(BOTH, None), P(), P(), P(), P(),
            by_expert, P("seq", "fsdp"), by_expert, P("seq", "fsdp"),
        ),
        out_specs=(
            tokens, tokens, P(), P(None, BOTH), P(), P(), P(BOTH, None), P(), P(), P(), P(),
            by_expert, P("seq", "fsdp"), by_expert, P("seq", "fsdp"),
        ),
        check_vma=False,
    )
```

```python
import functools
import math

import jax
import jax.numpy as jnp
import numpy as np
from jax import lax
from jax.experimental.layout import Layout, with_layout_constraint
from jax.experimental import pallas as pl
from jax.experimental.pallas import tpu as pltpu
from jax.sharding import PartitionSpec as P

KV_HEADS = 8
HD = 64
TOPK = 4

ROPE_BASE = 150000.0
SWIGLU_SLOPE = 1.702
CLAMP_LIMIT = 7.0
NORM_EPSILON = 1e-05
PRECISE = lax.Precision.HIGHEST
BOTH = ("fsdp", "seq")
LOW = jnp.bfloat16
WIDE = jnp.float32
NN = (((1,), (0,)), ((), ()))
NT = (((1,), (1,)), ((), ()))
TN = (((0,), (0,)), ((), ()))


def mul(left, right, dims=NN):
    return lax.dot_general(left, right, dims, preferred_element_type=WIDE)


def straight(values):
    return with_layout_constraint(values, Layout(major_to_minor=tuple(range(values.ndim))))


def blank(shape, dtype):
    return pl.pallas_call(
        lambda out: None,
        out_specs=pl.BlockSpec(memory_space=pl.ANY),
        out_shape=jax.ShapeDtypeStruct(shape, dtype),
        name="blank",
    )()


def free():
    return pl.CostEstimate(flops=0, bytes_accessed=0, transcendentals=0)


def pick_kernel(*refs, count):
    out = refs[-1]
    for i in range(count):

        @pl.when(pl.program_id(0) == i)
        def _(i=i):
            out[...] = refs[i][...].reshape(out.shape)


def lay(*parts):
    arrays, specs = [], []
    for part in parts:
        array, index = part if isinstance(part, tuple) else (part[None], 0)
        arrays.append(array)
        zeros = (0,) * (array.ndim - 1)
        specs.append(
            pl.BlockSpec((1, *array.shape[1:]), lambda n, at=(index, *zeros): at)
        )
    block = arrays[0].shape[1:]
    zeros = (0,) * len(block)
    return pl.pallas_call(
        functools.partial(pick_kernel, count=len(parts)),
        grid=(len(parts),),
        in_specs=specs,
        out_specs=pl.BlockSpec((1, *block), lambda n: (n, *zeros)),
        out_shape=jax.ShapeDtypeStruct((len(parts), *block), arrays[0].dtype),
        compiler_params=pltpu.CompilerParams(
            dimension_semantics=("arbitrary",), vmem_limit_bytes=32 * 2**20
        ),
        cost_estimate=free(),
        name="lay",
    )(*arrays)


def picked_kernel(at_ref, source_ref, out_ref):
    out_ref[...] = source_ref[...]


def picked(array, at):
    block = (1, *array.shape[1:])
    zeros = (0,) * (array.ndim - 1)
    return pl.pallas_call(
        picked_kernel,
        grid_spec=pltpu.PrefetchScalarGridSpec(
            num_scalar_prefetch=1,
            grid=(at.shape[0],),
            in_specs=[pl.BlockSpec(block, lambda n, at: (at[n], *zeros))],
            out_specs=pl.BlockSpec(block, lambda n, at: (n, *zeros)),
        ),
        out_shape=jax.ShapeDtypeStruct((at.shape[0], *array.shape[1:]), array.dtype),
        compiler_params=pltpu.CompilerParams(
            dimension_semantics=("arbitrary",), vmem_limit_bytes=32 * 2**20
        ),
        cost_estimate=free(),
        name="picked",
    )(at, array)


def ring_order(count):
    return list(range(0, count, 2)) + list(range(1, count, 2))[::-1]


def ring_pairs(count):
    order = ring_order(count)
    ahead = [(order[i], order[(i + 1) % count]) for i in range(count)]
    return ahead, [(b, a) for a, b in ahead]


def ring_ids():
    count = lax.axis_size("seq")
    order = ring_order(count)
    rank = {p: i for i, p in enumerate(order)}
    table = [[order[(rank[p] + j) % count] for j in range(count)] for p in range(count)]
    return jnp.asarray(np.array(table, np.int32))[lax.axis_index("seq")]


def send(values, axis, pairs):
    if values.ndim == 2 and values.shape[0] % 16 == 0:
        blocks = straight(values.reshape(values.shape[0] // 16, 16, values.shape[1]))
        return straight(lax.ppermute(blocks, axis, pairs)).reshape(values.shape)
    return straight(lax.ppermute(straight(values), axis, pairs))


def swap(values, axis, bit):
    return send(values, axis, [(i, i ^ bit) for i in range(lax.axis_size(axis))])


class Freight:
    def __init__(self):
        self.pending, self.now = [], 0

    def at(self, event, values, use):
        self.pending.append((max(event, self.now + 1), values, use))

    def after(self, events, values, use):
        self.at(self.now + events, values, use)

    def need(self, values, use):
        self.after(1, values, use)

    def carry(self, values, land, lag=1):
        self.after(lag, swap(values, "fsdp", 2), land)

    def blocks(self, terms, near_at, far_at, use):
        part = lax.axis_index("fsdp")
        terms = picked(terms, part ^ jnp.array([3, 1, 2, 0], jnp.int32))

        def near_there(near):
            away = straight((terms[2].astype(WIDE) + near[0].astype(WIDE)).astype(LOW))
            own = terms[3].astype(WIDE) + near[1].astype(WIDE)
            self.at(far_at, swap(away, "fsdp", 2), lambda far: use(own + far.astype(WIDE)))

        self.at(near_at, swap(straight(terms[:2]), "fsdp", 1), near_there)

    def chain(self, values, steps, use):
        if not steps:
            return use(values)
        self.need(values, lambda held: self.chain(steps[0](held), steps[1:], use))

    def __call__(self, *values):
        self.now += 1
        due = [(array, use) for event, array, use in self.pending if event <= self.now]
        self.pending = [item for item in self.pending if item[0] > self.now]
        out = lax.optimization_barrier((*values, *(array for array, _ in due)))
        for array, (_, use) in zip(out[len(values) :], due):
            use(array)
        return out[: len(values)]

    def finish(self):
        while self.pending:
            due, self.pending = self.pending, []
            for _, array, use in due:
                use(array)


def alone(*values):
    return values


def ring_gather_steps(rows, ids, beside=alone, after=None):
    count = lax.axis_size("seq")
    ahead, behind = ring_pairs(count)
    tokens = rows.shape[0]
    half = tokens // 2

    def put(full, part, index, offset=0):
        return straight(lax.dynamic_update_slice(full, part, (index * tokens + offset, 0)))

    rows = straight(rows)
    if after is not None:
        rows, _ = lax.optimization_barrier((rows, after))
    full = put(blank((count * tokens, rows.shape[1]), rows.dtype), rows, ids[0])
    up = down = rows
    for hop in range(1, (count + 1) // 2):
        up, down = beside(up, down)
        up, down = send(up, "seq", ahead), send(down, "seq", behind)
        landed = yield up, down
        if landed is not None:
            up, down = landed
            yield None
        full = put(put(full, up, ids[count - hop]), down, ids[hop])
    if count % 2 == 0:
        up, down = beside(straight(up[:half]), straight(down[half:]))
        up, down = send(up, "seq", ahead), send(down, "seq", behind)
        yield up, down
        full = put(put(full, up, ids[count // 2]), down, ids[count // 2], half)
    yield full, (up, down)


def ring_gather(rows, ids, beside=alone):
    for out in ring_gather_steps(rows, ids, beside):
        pass
    return out


def ring_reduce(term, ids, beside=alone):
    count = lax.axis_size("seq")
    ahead, behind = ring_pairs(count)
    middle = count // 2
    if count == 1:
        return term(ids[0])
    up = down = None
    if count % 2 == 0:
        whole = straight(term(ids[middle]).astype(LOW))
        half = whole.shape[0] // 2
        up, down = beside(straight(whole[:half]), straight(whole[half:]))
        up = send(up, "seq", ahead).astype(WIDE)
        down = send(down, "seq", behind).astype(WIDE)
        up = jnp.pad(up, ((0, half), (0, 0)))
        down = jnp.pad(down, ((half, 0), (0, 0)))
    for hop in range((count - 1) // 2, 0, -1):
        send_up = term(ids[hop])
        send_down = term(ids[count - hop])
        if up is not None:
            send_up, send_down = send_up + up, send_down + down
        send_up, send_down = beside(straight(send_up.astype(LOW)), straight(send_down.astype(LOW)))
        up = send(send_up, "seq", ahead).astype(WIDE)
        down = send(send_down, "seq", behind).astype(WIDE)
    return straight(term(ids[0]) + up + down)


def xor_steps(axis):
    def step(held, bit):
        return jnp.concatenate([held, swap(held, axis, bit)])

    bits = [1 << i for i in range((lax.axis_size(axis) - 1).bit_length())]
    return [functools.partial(step, bit=bit) for bit in bits]


def straighten(parts, axis):
    count = parts.shape[0]
    me = lax.axis_index(axis)
    bit = 1
    while bit < count:
        other = jnp.stack([parts[j ^ bit] for j in range(count)])
        parts = jnp.where((me & bit) != 0, other, parts)
        bit *= 2
    return parts


def sum_steps(axes):
    def step(values, axis, bit):
        return values + swap(values, axis, bit)

    return [
        functools.partial(step, axis=axis, bit=1 << i)
        for axis in axes
        for i in range((lax.axis_size(axis) - 1).bit_length())
    ]


UNIT_PARTS = [
    3, 1, 2, 1, 0, 1, 3, 2, 1, 0, 0, 1, 2, 0, 0, 3, 3, 3, 1, 2, 0, 0, 1, 1, 0, 1, 2, 1, 0, 3, 0, 3,
    0, 2, 0, 2, 0, 2, 0, 1, 1, 2, 0, 1, 1, 3, 1, 3, 3, 3, 0, 1, 2, 1, 0, 1, 1, 0, 1, 0, 2, 2, 0, 2,
    2, 0, 3, 0, 3, 3, 0, 0, 2, 1, 3, 3, 1, 2, 0, 1, 3, 0, 1, 0, 2, 2, 2, 1, 3, 3, 3, 2, 2, 3, 1, 0,
    0, 3, 3, 3, 0, 1, 2, 2, 3, 2, 2, 2, 1, 0, 0, 1, 1, 3, 3, 2, 1, 1, 1, 1, 2, 0, 3, 2, 0, 3, 0, 0,
    3, 2, 2, 2, 3, 3, 3, 3, 1, 1, 1, 0, 0, 3, 2, 2, 2, 3, 2, 3, 3, 2, 2, 3, 2, 2, 0, 1, 1, 1, 0, 3,
]
BLOCK_PARTS = [
    0, 3, 1, 2, 2, 3, 0, 1, 1, 2, 3, 0, 3, 0, 1, 2, 3, 0, 1, 2, 1, 0, 2, 3, 1, 2, 3, 0, 2, 3, 1, 0,
]


def group_places(groups):
    return [1, 4, 6, 3, 2, 0, 5, 7] if groups == 8 else list(range(groups))


@functools.lru_cache(None)
def unit_plan(fsdp, groups, query_width, pair_width):
    columns = query_width + 2 * pair_width
    per_device = columns // (fsdp * groups)
    group_query, group_pair = query_width // groups, pair_width // groups
    unit = math.gcd(math.gcd(per_device, group_query), group_pair)
    rounds = per_device // unit
    total = fsdp * groups
    wanted = []
    for index in range(columns // unit):
        column = index * unit
        if column < query_width:
            group, place = divmod(column, group_query)
        elif column < query_width + pair_width:
            group, place = divmod(column - query_width, group_pair)
            place += group_query
        else:
            group, place = divmod(column - query_width - pair_width, group_pair)
            place += group_query + group_pair
        wanted.append((index // rounds, index % rounds, group, place // unit))
    filled = {}
    edges = []
    near = UNIT_PARTS if groups == 8 and len(wanted) == len(UNIT_PARTS) else None
    spots = group_places(groups)
    for index, (source, slot, group, place) in enumerate(wanted):
        own = near[index] if near else source // groups
        for turn in (0, 1, 2, 3):
            part = own ^ turn
            if filled.get((part, group), 0) < rounds:
                filled[(part, group)] = filled.get((part, group), 0) + 1
                edges.append((source, slot, part * groups + spots[group], place))
                break
    steps = []
    for _ in range(rounds):
        taken = {}

        def find(source, seen):
            for edge in edges:
                if edge[0] != source or edge[2] in seen:
                    continue
                seen.add(edge[2])
                if edge[2] not in taken or find(taken[edge[2]][0], seen):
                    taken[edge[2]] = edge
                    return True
            return False

        for source in range(total):
            find(source, set())
        steps.append(sorted(taken.values()))
        for edge in taken.values():
            edges.remove(edge)
    send = np.zeros((rounds, total), np.int32)
    place_at = np.zeros((rounds, total), np.int32)
    pairs = []
    for i, step in enumerate(steps):
        pairs.append([(edge[0], edge[2]) for edge in step])
        for source, slot, target, place in step:
            send[i, source] = slot
            place_at[i, target] = place
    count = fsdp * rounds
    order = np.zeros((total, count), np.int32)
    back = np.zeros((total, count), np.int32)
    for device in range(total):
        group = device % groups
        for part in range(fsdp):
            for i in range(rounds):
                place = place_at[i, part * groups + group]
                order[device, place] = part * rounds + i
                back[device, part * rounds + i] = place
    home = np.argsort(send, axis=0).astype(np.int32)
    return unit, rounds, pairs, send, order, back, home


def out_pairs(fsdp, groups):
    total = fsdp * groups
    parts = BLOCK_PARTS if (fsdp, groups) == (4, 8) else [b % fsdp for b in range(total)]
    spots = group_places(groups)
    moves = [(b, parts[b] * groups + spots[b // fsdp]) for b in range(total)]
    found = np.zeros((total, fsdp), np.int32)
    for b, target in moves:
        found[target % groups :: groups, b % fsdp] = target // groups
    return moves, found


def turn(front, back, cosine, sine):
    return front * cosine - back * sine, back * cosine + front * sine


def forward_kernel(
    at_ref, sink_ref, front_ref, back_ref, key_front, key_back, value_front, value_back,
    query_bias, pair_bias, cos_ref, sin_ref,
    turned_ref, pairs_ref, out_ref, total_ref, keys,
    *, block, scale,
):
    head = pl.program_id(0)
    length = front_ref.shape[1]
    half = HD // 2
    cosine, sine = cos_ref[...], sin_ref[...]

    @pl.when(head == 0)
    def _():
        front, back = turn(
            key_front[...] + pair_bias[:half], key_back[...] + pair_bias[half:HD], cosine, sine
        )
        key = jnp.concatenate([front, back], axis=0)
        pairs_ref[:HD, :] = key.astype(LOW)
        pairs_ref[HD : HD + half, :] = (value_front[...] + pair_bias[HD : HD + half]).astype(LOW)
        pairs_ref[HD + half :, :] = (value_back[...] + pair_bias[HD + half :]).astype(LOW)
        keys[...] = key.T.astype(LOW)

    front, back = turn(
        front_ref[...] + query_bias[:half], back_ref[...] + query_bias[half:], cosine, sine
    )
    turned_ref[:half, :] = (front.astype(LOW).astype(WIDE) * scale).astype(LOW)
    turned_ref[half:, :] = (back.astype(LOW).astype(WIDE) * scale).astype(LOW)
    sink = sink_ref[head]
    count = length // block
    below = lax.broadcasted_iota(jnp.int32, (block, block), 0) > lax.broadcasted_iota(
        jnp.int32, (block, block), 1
    )
    for index in range(count):
        columns = pl.ds(index * block, block)
        query = turned_ref[:, columns]

        def scores(rows):
            return mul(keys[rows, :], query)

        def step(start, carry, masked):
            peak, total, mixed = carry
            rows = pl.ds(start, block)
            tile = scores(rows)
            if masked:
                tile = jnp.where(below, -1e30, tile)
            top = jnp.maximum(peak, jnp.max(tile, axis=0, keepdims=True))
            weights = jnp.exp(tile - top)
            shrink = jnp.exp(peak - top)
            total = total * shrink + jnp.sum(weights, axis=0, keepdims=True)
            mixed = mixed * shrink + mul(pairs_ref[HD:, rows], weights.astype(LOW))
            return top, total, mixed

        carry = (
            jnp.full((1, block), sink, WIDE),
            jnp.ones((1, block), WIDE),
            jnp.zeros((HD, block), WIDE),
        )
        if count <= 4:
            for earlier in range(index):
                carry = step(earlier * block, carry, False)
        elif index:
            carry = lax.fori_loop(
                0, index, lambda i, c: step(pl.multiple_of(i * block, block), c, False), carry
            )
        peak, total, mixed = step(index * block, carry, True)
        out_ref[:, columns] = (mixed / total).astype(LOW)
        total_ref[0, :, columns] = peak + jnp.log(total)


def attend(at, projected, bias, sinks, cosine, sine, heads):
    length = projected.shape[1]
    rows = heads * HD
    half = HD // 2
    block = min(256, length)
    last = rows // (2 * HD)

    def piece(place):
        return pl.BlockSpec((half, length), lambda h, at: (at[place], 0))

    return pl.pallas_call(
        functools.partial(forward_kernel, block=block, scale=HD**-0.5),
        grid_spec=pltpu.PrefetchScalarGridSpec(
            num_scalar_prefetch=1,
            grid=(heads,),
            in_specs=[
                pl.BlockSpec(memory_space=pltpu.SMEM),
                pl.BlockSpec((half, length), lambda h, at: (at[2 * h], 0)),
                pl.BlockSpec((half, length), lambda h, at: (at[2 * h + 1], 0)),
                piece(2 * heads),
                piece(2 * heads + 1),
                piece(2 * heads + 2),
                piece(2 * heads + 3),
                pl.BlockSpec((HD, 1), lambda h, at: (h, 0)),
                pl.BlockSpec((2 * HD, 1), lambda h, at: (last, 0)),
                pl.BlockSpec((half, length), lambda h, at: (0, 0)),
                pl.BlockSpec((half, length), lambda h, at: (0, 0)),
            ],
            out_specs=[
                pl.BlockSpec((HD, length), lambda h, at: (h, 0)),
                pl.BlockSpec((2 * HD, length), lambda h, at: (0, 0)),
                pl.BlockSpec((HD, length), lambda h, at: (at[2 * heads + 4 + h], 0)),
                pl.BlockSpec((1, 1, length), lambda h, at: (h, 0, 0)),
            ],
            scratch_shapes=[pltpu.VMEM((length, HD), LOW)],
        ),
        out_shape=[
            jax.ShapeDtypeStruct((rows, length), LOW),
            jax.ShapeDtypeStruct((2 * HD, length), LOW),
            jax.ShapeDtypeStruct((rows, length), LOW),
            jax.ShapeDtypeStruct((heads, 1, length), WIDE),
        ],
        compiler_params=pltpu.CompilerParams(
            dimension_semantics=("arbitrary",), vmem_limit_bytes=40 * 2**20
        ),
        cost_estimate=pl.CostEstimate(
            flops=0, bytes_accessed=0, transcendentals=0
        ),
        name="attend",
    )(at, sinks, *[projected] * 6, bias, bias, cosine, sine)


def backward_kernel(
    at_ref, sink_ref, turned_ref, pairs_ref, out_ref, grad_ref, total_ref, cos_ref, sin_ref,
    query_ref, pair_ref, sink_grad_ref, keys, values, key_sum, value_sum, query_rows, grad_rows,
    *, block, scale,
):
    head = pl.program_id(0)
    length = turned_ref.shape[1]
    half = HD // 2
    count = length // block

    @pl.when(head == 0)
    def _():
        keys[...] = pairs_ref[:HD, :].astype(WIDE).T.astype(LOW)
        values[...] = pairs_ref[HD:, :].astype(WIDE).T.astype(LOW)
        key_sum[...] = jnp.zeros_like(key_sum)
        value_sum[...] = jnp.zeros_like(value_sum)

    query_rows[...] = turned_ref[...].astype(WIDE).T.astype(LOW)
    grad_rows[...] = grad_ref[...].astype(WIDE).T.astype(LOW)
    below = lax.broadcasted_iota(jnp.int32, (block, block), 0) > lax.broadcasted_iota(
        jnp.int32, (block, block), 1
    )
    deltas = jnp.sum(grad_ref[...].astype(WIDE) * out_ref[...].astype(WIDE), axis=0, keepdims=True)
    totals = total_ref[0]
    sink_term = -jnp.sum(jnp.exp(sink_ref[head] - totals) * deltas, axis=1, keepdims=True)
    sink_grad_ref[0] = jnp.broadcast_to(sink_term, (1, 128))
    for index in range(count):
        columns = pl.ds(index * block, block)
        query = turned_ref[:, columns]
        grad = grad_ref[:, columns]
        total = totals[:, index * block : (index + 1) * block]
        delta = deltas[:, index * block : (index + 1) * block]

        def step(start, query_sum, masked):
            rows = pl.ds(start, block)
            weights = jnp.exp(mul(keys[rows, :], query) - total)
            if masked:
                weights = jnp.where(below, 0.0, weights)
            inner = (weights * (mul(values[rows, :], grad) - delta)).astype(LOW)
            key_sum[rows, :] += mul(inner, query_rows[columns, :])
            value_sum[rows, :] += mul(weights.astype(LOW), grad_rows[columns, :])
            return query_sum + mul(pairs_ref[:HD, rows], inner)

        query_sum = jnp.zeros((HD, block), WIDE)
        if count <= 4:
            for earlier in range(index):
                query_sum = step(earlier * block, query_sum, False)
        elif index:
            query_sum = lax.fori_loop(
                0, index, lambda i, c: step(pl.multiple_of(i * block, block), c, False), query_sum
            )
        query_sum = step(index * block, query_sum, True)
        rounded = (query_sum * scale).astype(LOW).astype(WIDE)
        cosine, sine = cos_ref[:, columns], sin_ref[:, columns]
        front, back = turn(rounded[:half], rounded[half:], cosine, -sine)
        query_ref[:half, columns] = front.astype(LOW)
        query_ref[half:, columns] = back.astype(LOW)

    @pl.when(head == pl.num_programs(0) - 1)
    def _():
        rounded = key_sum[...].T.astype(LOW).astype(WIDE)
        front, back = turn(rounded[:half], rounded[half:], cos_ref[...], -sin_ref[...])
        pair_ref[:half, :] = front.astype(LOW)
        pair_ref[half:HD, :] = back.astype(LOW)
        pair_ref[HD:, :] = value_sum[...].T.astype(LOW)


def attend_back(at, sinks, turned, pairs, attended, upstream, totals, cosine, sine):
    heads, _, length = totals.shape
    rows = heads * HD
    block = min(256, length)
    by_head = pl.BlockSpec((HD, length), lambda h, at: (h, 0))
    moved = pl.BlockSpec((HD, length), lambda h, at: (at[2 * heads + 4 + h], 0))
    table = pl.BlockSpec((HD // 2, length), lambda h, at: (0, 0))
    whole = pl.BlockSpec((2 * HD, length), lambda h, at: (0, 0))
    return pl.pallas_call(
        functools.partial(backward_kernel, block=block, scale=HD**-0.5),
        grid_spec=pltpu.PrefetchScalarGridSpec(
            num_scalar_prefetch=1,
            grid=(heads,),
            in_specs=[
                pl.BlockSpec(memory_space=pltpu.SMEM),
                by_head,
                whole,
                moved,
                moved,
                pl.BlockSpec((1, 1, length), lambda h, at: (h, 0, 0)),
                table,
                table,
            ],
            out_specs=[by_head, whole, pl.BlockSpec((1, 1, 128), lambda h, at: (h, 0, 0))],
            scratch_shapes=[
                pltpu.VMEM((length, HD), LOW),
                pltpu.VMEM((length, HD), LOW),
                pltpu.VMEM((length, HD), WIDE),
                pltpu.VMEM((length, HD), WIDE),
                pltpu.VMEM((length, HD), LOW),
                pltpu.VMEM((length, HD), LOW),
            ],
        ),
        out_shape=[
            jax.ShapeDtypeStruct((rows, length), LOW),
            jax.ShapeDtypeStruct((2 * HD, length), LOW),
            jax.ShapeDtypeStruct((heads, 1, 128), WIDE),
        ],
        compiler_params=pltpu.CompilerParams(
            dimension_semantics=("arbitrary",), vmem_limit_bytes=40 * 2**20
        ),
        cost_estimate=pl.CostEstimate(
            flops=0, bytes_accessed=0, transcendentals=0
        ),
        name="attend_back",
    )(at, sinks, turned, pairs, attended, upstream, totals, cosine, sine)


EXTRA = 16


def term_kernel(left_ref, right_ref, extra_ref, out_ref):
    size = left_ref.shape[0]
    out_ref[:size, :] = mul(left_ref[...], right_ref[...]).astype(LOW)
    out_ref[size:, :] = extra_ref[...].astype(LOW)


def column_parts(width, count):
    block = min(640, width)
    tiles = pl.cdiv(width, block)
    ends = [round(tiles * i / count) for i in range(count + 1)]
    return block, [(a, b - a) for a, b in zip(ends, ends[1:]) if b > a]


def weight_term(left, right, extra, size, block, tiles):
    depth, width = right.shape
    first, count = tiles
    shards = left.shape[0] // size
    columns = min(width, (first + count) * block) - first * block
    return pl.pallas_call(
        term_kernel,
        grid=(shards, count),
        in_specs=[
            pl.BlockSpec((size, depth), lambda m, n: (m, 0)),
            pl.BlockSpec((depth, block), lambda m, n: (0, n + first)),
            pl.BlockSpec((EXTRA, block), lambda m, n: (0, n + first)),
        ],
        out_specs=pl.BlockSpec((size + EXTRA, block), lambda m, n: (m, n)),
        out_shape=jax.ShapeDtypeStruct((shards * (size + EXTRA), columns), LOW),
        compiler_params=pltpu.CompilerParams(
            dimension_semantics=("arbitrary", "arbitrary"), vmem_limit_bytes=56 * 2**20
        ),
        cost_estimate=free(),
        name="weight_term",
    )(left, right, extra)


def rms_scale(values, norm_gain):
    factor = lax.rsqrt(jnp.mean(values * values, axis=-1, keepdims=True) + NORM_EPSILON)
    return (values * factor * norm_gain, factor)


def rms_back(values, factor, norm_gain, upstream):
    scaled = upstream * norm_gain
    value_grad = factor * scaled - values * factor * factor * factor * jnp.mean(
        scaled * values, axis=-1, keepdims=True
    )
    gain_grad = jnp.sum(upstream * values * factor, axis=0)
    return (value_grad, gain_grad)


def clamped_glu(joined, expert_width):
    gate_part = jnp.minimum(joined[:, :expert_width], CLAMP_LIMIT)
    linear_part = jnp.clip(joined[:, expert_width:], -CLAMP_LIMIT, CLAMP_LIMIT)
    return (linear_part + 1.0) * gate_part * jax.nn.sigmoid(SWIGLU_SLOPE * gate_part)


def glu_back(joined, expert_width, upstream):
    raw_gate = joined[:, :expert_width]
    raw_linear = joined[:, expert_width:]
    gate_part = jnp.minimum(raw_gate, CLAMP_LIMIT)
    linear_part = jnp.clip(raw_linear, -CLAMP_LIMIT, CLAMP_LIMIT)
    sigmoid_part = jax.nn.sigmoid(SWIGLU_SLOPE * gate_part)
    gate_open = (raw_gate < CLAMP_LIMIT).astype(jnp.float32)
    linear_open = (jnp.abs(raw_linear) < CLAMP_LIMIT).astype(jnp.float32)
    slope_part = sigmoid_part + gate_part * SWIGLU_SLOPE * sigmoid_part * (1.0 - sigmoid_part)
    gate_grad = upstream * (linear_part + 1.0) * slope_part * gate_open
    linear_grad = upstream * gate_part * sigmoid_part * linear_open
    return jnp.concatenate([gate_grad, linear_grad], axis=1)


def mixing_of(rows, routes, router_weight, router_bias):
    logits = mul(rows, router_weight) + router_bias
    experts = jnp.arange(router_bias.shape[0], dtype=jnp.int32)
    chosen = jnp.any(routes[:, :, None] == experts, axis=1)
    logits = jnp.where(chosen, logits, -jnp.inf)
    weights = jnp.exp(logits - jnp.max(logits, axis=1, keepdims=True))
    return weights / jnp.sum(weights, axis=1, keepdims=True)


def rows_of(values, index, size):
    return lax.dynamic_slice_in_dim(values, index * size, size, axis=0)


def columns_of(values, index, size):
    return lax.dynamic_slice_in_dim(values, index * size, size, axis=1)


def body(
    hidden,
    out_grad,
    routes,
    norm1_gain,
    qkv_weight,
    qkv_bias,
    sink_logits,
    out_weight,
    out_bias,
    norm2_gain,
    router_weight,
    router_bias,
    gate_up_weight,
    gate_up_bias,
    down_weight,
    down_bias,
):
    tokens = hidden.shape[1]
    groups = lax.axis_size("seq")
    position = lax.axis_index("seq")
    spots = np.argsort(np.array(group_places(lax.axis_size("seq")))).astype(np.int32)
    group = jnp.asarray(spots)[position]
    fsdp = lax.axis_size("fsdp")
    part = lax.axis_index("fsdp")
    device = part * groups + position
    head_count = sink_logits.shape[0]
    group_heads = head_count // groups
    expert_width = down_weight.shape[1] * fsdp
    capacity = tokens * TOPK * 9 // (8 * groups)
    slot_count = groups * capacity
    length = tokens * groups
    query_width = head_count * HD
    pair_width = KV_HEADS * HD
    group_query = group_heads * HD
    ids = ring_ids()

    planned = groups == KV_HEADS and fsdp == 4 and qkv_weight.shape[1] % (HD // 2) == 0
    qkv_rows = straight(qkv_weight.T)
    held = {}
    freight = Freight()
    out_moves, out_found = out_pairs(fsdp, groups)

    def keep(name):
        return lambda values: held.__setitem__(name, values)

    def gathered(name):
        return lambda block: held.__setitem__(name, lax.all_gather(block, "fsdp", axis=0))

    if planned:
        unit, rounds, pairs, send_slots, order, back, home = unit_plan(
            fsdp, groups, query_width, pair_width
        )
        slots = jnp.asarray(send_slots)[:, device]
        bias_at = (group, group, group)
        head_units = jnp.asarray(order)[device]

        def open_units(weight):
            units = weight.reshape(rounds, unit, -1)
            blocks = [
                send(lax.dynamic_index_in_dim(units, slots[i], 0, keepdims=False), BOTH, pairs[i])
                for i in range(rounds)
            ]
            freight.need(lay(*blocks).reshape(rounds * unit, -1), gathered("qkv"))

        freight.need(qkv_rows, open_units)
    else:
        pair_index = group * KV_HEADS // groups
        bias_at = (group, pair_index, pair_index)
        head_units = jnp.arange(2 * group_heads + 4, dtype=jnp.int32)
    bias_group = jnp.concatenate(
        [
            rows_of(qkv_bias[:query_width], bias_at[0], group_query),
            rows_of(qkv_bias[query_width : query_width + pair_width], bias_at[1], HD),
            rows_of(qkv_bias[query_width + pair_width :], bias_at[2], HD),
        ]
    )
    block_heads = out_weight.shape[0] // HD
    by_block = out_weight.shape[0] % HD == 0
    head_ids = jnp.arange(group_heads, dtype=jnp.int32)
    if by_block:
        turns = jnp.asarray(np.repeat(out_found, block_heads, axis=1))[device]
        head_ids = turns * block_heads + head_ids % block_heads
    places_at = jnp.concatenate([head_units, head_ids])

    def open_out(weight):
        mine = send(weight, BOTH, out_moves)
        held["out"] = lax.all_gather(mine, "fsdp", axis=0)
        gate_up, down, _ = lax.optimization_barrier((gate_up_weight[0], down_weight[0], mine))
        held["gate_up"] = lax.all_gather(gate_up, "fsdp", axis=0, tiled=True)
        held["down"] = lax.all_gather(down, "fsdp", axis=0, tiled=True)

    freight.after(4, out_weight, open_out)

    def open_routes(own):
        own = jnp.broadcast_to(own.reshape(1, -1), (groups, tokens * TOPK))
        held["routes"] = lax.all_to_all(own, "seq", split_axis=0, concat_axis=0, tiled=True)

    freight.after(4, routes, open_routes)

    inputs = hidden[0].astype(WIDE)
    first_normed, first_factor = rms_scale(inputs, norm1_gain)
    first_full, first_last = ring_gather(first_normed.astype(LOW), ids, freight)
    frequency = ROPE_BASE ** (-(jnp.arange(HD // 2, dtype=WIDE) * 2.0) / HD)
    angles = jnp.arange(length, dtype=jnp.int32).astype(WIDE)[None, :] * frequency[:, None]
    cosine, sine = jnp.cos(angles), jnp.sin(angles)
    sink_part = rows_of(sink_logits, group, group_heads)
    gather = ring_gather_steps(out_grad[0], ids, freight, first_last)
    hop = next(gather)
    if planned:
        qkv_group = straight(held["qkv"].reshape(fsdp * rounds * unit, -1))
    else:
        qkv_full = lax.all_gather(qkv_rows, BOTH, axis=0, tiled=True)
        qkv_group = jnp.concatenate(
            [
                rows_of(qkv_full[:query_width], group, group_query),
                rows_of(qkv_full[query_width : query_width + pair_width], pair_index, HD),
                rows_of(qkv_full[query_width + pair_width :], pair_index, HD),
            ]
        )
    projected, held["routes"] = lax.optimization_barrier(
        (mul(qkv_group, first_full, NT), held["routes"])
    )
    out_group = straight(held["out"].reshape(fsdp * out_weight.shape[0], -1))
    turned, pair_rows, attended, log_totals = attend(
        places_at, projected, bias_group[:, None], sink_part, cosine, sine, group_heads
    )

    freight.need(hop, gather.send)
    biases = jnp.concatenate([gate_up_bias, down_bias], axis=1)
    freight.chain(biases, xor_steps("fsdp"), keep("biases"))
    branch = ring_reduce(
        lambda index: mul(columns_of(attended, index, tokens), out_group, TN), ids, freight
    )
    middle = inputs + (branch + out_bias)
    second_normed, second_factor = rms_scale(middle, norm2_gain)
    second_low = second_normed.astype(LOW)

    second_full, last = ring_gather(second_low, ids, freight)
    freight.need(last[0], lambda values: None)
    next(gather)
    freight.finish()
    joined_weight, down_full = held["gate_up"], held["down"]
    all_routes = held["routes"].reshape(length, TOPK)
    biases = straighten(held["biases"], "fsdp")
    joined_bias = biases[:, : gate_up_bias.shape[1]].reshape(-1).astype(WIDE)
    down_shift = biases[:, gate_up_bias.shape[1] :].reshape(-1).astype(WIDE)
    mine = jnp.any(all_routes == position, axis=1)
    counted = mine.astype(jnp.int32)
    earlier = jnp.cumsum(counted) - counted
    places = jnp.where(mine, earlier, -1)
    slots_here = jnp.arange(slot_count, dtype=jnp.int32)
    into = slots_here[:, None] == places[None, :]
    back_to = places[:, None] == slots_here[None, :]
    into_low, back_low = into.astype(LOW), back_to.astype(LOW)
    mixing_all = mixing_of(second_full, all_routes, router_weight, router_bias)
    expert_ids = jnp.arange(groups, dtype=jnp.int32)
    mixing_mine = jnp.sum(jnp.where(expert_ids == position, mixing_all, 0.0), axis=1)
    mixing_rows = jnp.sum(jnp.where(into, mixing_mine[None, :], 0.0), axis=1)[:, None]
    next(gather)
    expert_rows = mul(into_low, second_full).astype(LOW)
    freight.need(straight(mul(expert_rows, joined_weight) + joined_bias), keep("joined"))
    next(gather)
    joined = held["joined"]
    activated = lax.optimization_barrier(clamped_glu(joined, expert_width).astype(LOW))
    expert_columns = expert_rows.T
    upstream_full = None
    for upstream_full in gather:
        pass
    upstream_full = upstream_full[0]
    freight.finish()
    freight = Freight()
    upstream_rows = mul(into_low, upstream_full)
    rows_grad = (upstream_rows * mixing_rows).astype(LOW)
    down_term = straight(mul(activated, rows_grad, TN).astype(LOW))
    down_total = lax.psum_scatter(down_term, "fsdp", scatter_dimension=0, tiled=True)
    freight.at(9, down_total, lambda total: freight.need(total.astype(WIDE), keep("down_shard")))
    activated, _ = lax.optimization_barrier((activated, down_term))
    expert_out = (mul(activated, down_full) + down_shift).astype(LOW).astype(WIDE)
    weighted = (expert_out * mixing_rows).astype(LOW)
    mixing_grad_rows = jnp.sum(upstream_rows * expert_out, axis=1)
    down_sums = jnp.sum(rows_grad.astype(WIDE), axis=0, keepdims=True)


    def back_first(upstream):
        activated_grad = mul(upstream, down_full, NT)
        grad = straight(glu_back(joined, expert_width, activated_grad).astype(LOW))
        freight.need(grad, back_second)

    def back_second(grad):
        held["input_rows_grad"] = straight(mul(grad, joined_weight, NT).astype(LOW))
        back_third(grad)

    def back_third(grad):
        sums = jnp.sum(grad.astype(WIDE), axis=0, keepdims=True)
        extra = jnp.concatenate([sums, jnp.pad(down_sums, ((0, 0), (0, expert_width)))])
        extra = jnp.pad(extra, ((0, EXTRA - 2), (0, 0)))
        block, split = column_parts(grad.shape[1], 3)
        held["joined_parts"] = [None] * len(split)
        held["joined_shard"] = blank((hidden.shape[2] // fsdp, grad.shape[1]), WIDE)

        def part_there(i, term):
            total = lax.psum_scatter(term, "fsdp", scatter_dimension=0, tiled=True)
            freight.at([11, 13, 16][i], total, functools.partial(part_kept, i))

        def part_kept(i, total):
            own_rows = hidden.shape[2] // fsdp
            rows = total[:own_rows].astype(WIDE)
            start = split[i][0] * block
            held["joined_shard"] = lax.dynamic_update_slice(held["joined_shard"], rows, (0, start))
            held["joined_parts"][i] = total[own_rows : own_rows + 2].astype(WIDE)
            if i + 1 < len(split):
                freight.need(held["joined_shard"], keep("joined_shard"))

        def begin(i, held_here):
            grad, extra = held_here
            size = hidden.shape[2] // fsdp
            term = weight_term(expert_columns, grad, extra, size, block, split[i])
            freight.need(term, functools.partial(part_there, i))

        begin(0, (grad, extra))
        for i in range(1, len(split)):
            freight.at([2, 5, 7][i], (grad, extra), functools.partial(begin, i))

    def mixing_back(rows):
        tokens_grad = jnp.sum(jnp.where(back_to, rows[None, :], 0.0), axis=1)
        by_device = lax.all_to_all(
            tokens_grad.reshape(groups, tokens), "seq", split_axis=0, concat_axis=0, tiled=True
        )
        freight.need(by_device, keep("mixing_grad"))

    freight.need(mixing_grad_rows, mixing_back)
    freight.need(rows_grad, back_first)
    combined = ring_reduce(lambda index: mul(rows_of(back_low, index, tokens), weighted), ids, freight)
    freight.need((middle + combined).astype(LOW), keep("outputs"))
    if "input_rows_grad" not in held:
        freight.finish()
    input_rows_grad = held["input_rows_grad"]
    second_grad = ring_reduce(
        lambda index: mul(rows_of(back_low, index, tokens), input_rows_grad), ids, freight
    )
    mixing = mixing_of(second_low, routes[0], router_weight, router_bias)
    mixing_grad = held["mixing_grad"].T
    logits_grad = mixing * (
        mixing_grad - jnp.sum(mixing * mixing_grad, axis=-1, keepdims=True)
    )
    second_grad = second_grad + jnp.dot(
        logits_grad, router_weight.astype(WIDE).T, precision=PRECISE
    )
    upstream = out_grad[0].astype(WIDE)
    middle_part, gain2_grad = rms_back(middle, second_factor, norm2_gain, second_grad)
    middle_grad = upstream + middle_part
    branch_low = middle_grad.astype(LOW)

    width = hidden.shape[2]

    router_weight_grad = jnp.dot(second_low.astype(WIDE).T, logits_grad, precision=PRECISE)
    router_bias_grad = jnp.sum(logits_grad, axis=0)
    out_bias_grad = jnp.sum(branch_low.astype(WIDE), axis=0)
    early = [out_bias_grad, gain2_grad, router_weight_grad.T.reshape(-1), router_bias_grad]
    branch_full, _ = ring_gather(branch_low, ids, freight)
    heads_grad = mul(out_group, branch_full, NT).astype(LOW)
    query_grad, pair_grad, sink_grad = attend_back(
        places_at, sink_part, turned, pair_rows, attended, heads_grad, log_totals, cosine, sine
    )
    projected_grad = jnp.concatenate([query_grad, pair_grad])
    bias_term = jnp.sum(projected_grad.astype(WIDE), axis=1)
    if planned:
        projected_grad = jnp.take(
            projected_grad.reshape(fsdp * rounds, unit, -1),
            jnp.asarray(back)[device],
            axis=0,
            mode="clip",
        ).reshape(projected_grad.shape)

    bias_full = jnp.zeros((query_width + 2 * pair_width,), WIDE)
    bias_full = lax.dynamic_update_slice(
        bias_full, bias_term[:group_query], (bias_at[0] * group_query,)
    )
    bias_full = lax.dynamic_update_slice(
        bias_full, bias_term[group_query : group_query + HD], (query_width + bias_at[1] * HD,)
    )
    bias_full = lax.dynamic_update_slice(
        bias_full,
        bias_term[group_query + HD :],
        (query_width + pair_width + bias_at[2] * HD,),
    )
    sink_full = lax.dynamic_update_slice_in_dim(
        jnp.zeros((head_count,), WIDE), sink_grad[:, 0, 0], group * group_heads, 0
    )

    def out_first(grad):
        terms = straight(mul(attended, grad).astype(LOW))

        def use(total):
            held["out_shard"] = send(total.astype(LOW), BOTH, [(b, a) for a, b in out_moves])

        freight.blocks(terms.reshape(fsdp, out_weight.shape[0], -1), 15, 16, use)

    def qkv_first(grad):
        terms = mul(grad, first_full)
        low = straight(terms.astype(LOW))
        sums = jnp.sum(low.astype(WIDE) * qkv_group.astype(WIDE), axis=0) / norm1_gain
        held["late"] = jnp.concatenate([sums, bias_full, sink_full, *early])
        if not planned:
            held["qkv_term"] = terms
            return

        def come_back(total):
            total = straight(total.astype(LOW))
            returned = [
                send(total[i], BOTH, [(b, a) for a, b in pairs[i]]) for i in range(rounds)
            ]
            held["returned"] = lay(*returned)

        freight.blocks(low.reshape(fsdp, rounds, unit, -1), 14, 15, come_back)

    freight.need(projected_grad, qkv_first)
    freight.at(14, branch_full, out_first)
    first_grad = ring_reduce(
        lambda index: mul(columns_of(projected_grad, index, tokens), qkv_group, TN), ids, freight
    )
    freight.finish()
    joined_sums = jnp.concatenate(held["joined_parts"], axis=1)
    joined_shard = held["joined_shard"]
    joined_bias_shard = rows_of(joined_sums[0], part, gate_up_bias.shape[1])
    down_bias_shard = rows_of(joined_sums[1, :width], part, down_bias.shape[1])
    down_shard = held["down_shard"]
    out_shard = held["out_shard"].astype(WIDE)
    if planned:
        qkv_shard = jnp.take(held["returned"], jnp.asarray(home)[:, device], axis=0, mode="clip")
        qkv_shard = qkv_shard.reshape(rounds * unit, -1).T.astype(WIDE)
    else:
        qkv_term = held["qkv_term"]
        scattered = jnp.zeros((query_width + 2 * pair_width, width), WIDE)
        for start, stop, row in (
            (0, group_query, group * group_query),
            (group_query, group_query + HD, query_width + pair_index * HD),
            (group_query + HD, group_query + 2 * HD, query_width + pair_width + pair_index * HD),
        ):
            scattered = lax.dynamic_update_slice(scattered, qkv_term[start:stop], (row, 0))
        qkv_shard = lax.psum_scatter(scattered, BOTH, scatter_dimension=0, tiled=True).T
    late, first_grad = lax.optimization_barrier((held["late"], first_grad))
    for step in sum_steps(BOTH):
        late = step(late)
    input_part, _ = rms_back(inputs, first_factor, norm1_gain, first_grad)
    input_grad = middle_grad + input_part

    early = late[width + qkv_bias.shape[0] + head_count :]
    router_sums = early[2 * width : 2 * width + width * groups].reshape(groups, width).T
    return (
        held["outputs"][None],
        input_grad.astype(LOW)[None],
        late[:width],
        qkv_shard,
        late[width : width + qkv_bias.shape[0]],
        late[width + qkv_bias.shape[0] : width + qkv_bias.shape[0] + head_count],
        out_shard,
        early[:width],
        early[width : 2 * width],
        router_sums,
        early[2 * width + width * groups : 2 * width + (width + 1) * groups],
        joined_shard[None],
        joined_bias_shard[None],
        down_shard[None],
        down_bias_shard[None],
    )


def solution(mesh):
    tokens = P("fsdp", "seq", None)
    by_expert = P("seq", "fsdp", None)
    return jax.shard_map(
        body,
        mesh=mesh,
        in_specs=(
            tokens, tokens, tokens, P(), P(None, BOTH), P(), P(), P(BOTH, None), P(), P(), P(), P(),
            by_expert, P("seq", "fsdp"), by_expert, P("seq", "fsdp"),
        ),
        out_specs=(
            tokens, tokens, P(), P(None, BOTH), P(), P(), P(BOTH, None), P(), P(), P(), P(),
            by_expert, P("seq", "fsdp"), by_expert, P("seq", "fsdp"),
        ),
        check_vma=False,
    )
```

```python
import functools
import math

import jax
import jax.numpy as jnp
import numpy as np
from jax import lax
from jax.experimental.layout import Layout, with_layout_constraint
from jax.experimental import pallas as pl
from jax.experimental.pallas import tpu as pltpu
from jax.sharding import PartitionSpec as P

KV_HEADS = 8
HD = 64
TOPK = 4

ROPE_BASE = 150000.0
SWIGLU_SLOPE = 1.702
CLAMP_LIMIT = 7.0
NORM_EPSILON = 1e-05
PRECISE = lax.Precision.HIGHEST
BOTH = ("fsdp", "seq")
LOW = jnp.bfloat16
WIDE = jnp.float32
NN = (((1,), (0,)), ((), ()))
NT = (((1,), (1,)), ((), ()))
TN = (((0,), (0,)), ((), ()))


def mul(left, right, dims=NN):
    return lax.dot_general(left, right, dims, preferred_element_type=WIDE)


def straight(values):
    return with_layout_constraint(values, Layout(major_to_minor=tuple(range(values.ndim))))


def blank(shape, dtype):
    return pl.pallas_call(
        lambda out: None,
        out_specs=pl.BlockSpec(memory_space=pl.ANY),
        out_shape=jax.ShapeDtypeStruct(shape, dtype),
        name="blank",
    )()


def free():
    return pl.CostEstimate(flops=0, bytes_accessed=0, transcendentals=0)


def pick_kernel(*refs, count):
    out = refs[-1]
    for i in range(count):

        @pl.when(pl.program_id(0) == i)
        def _(i=i):
            out[...] = refs[i][...].reshape(out.shape)


def lay_kernel(at_ref, *refs, count):
    pick_kernel(*refs, count=count)


def lay(*parts, at=None):
    arrays, specs = [], []
    for part in parts:
        array, index = part if isinstance(part, tuple) else (part[None], 0)
        arrays.append(array)
        place = (index,) + (0,) * (array.ndim - 1)
        specs.append(pl.BlockSpec((1, *array.shape[1:]), lambda n, at, place=place: place))
    block = arrays[0].shape[1:]
    zeros = (0,) * len(block)
    at = jnp.arange(len(parts), dtype=jnp.int32) if at is None else at
    return pl.pallas_call(
        functools.partial(lay_kernel, count=len(parts)),
        grid_spec=pltpu.PrefetchScalarGridSpec(
            num_scalar_prefetch=1,
            grid=(len(parts),),
            in_specs=specs,
            out_specs=pl.BlockSpec((1, *block), lambda n, at: (at[n], *zeros)),
        ),
        out_shape=jax.ShapeDtypeStruct((len(parts), *block), arrays[0].dtype),
        compiler_params=pltpu.CompilerParams(
            dimension_semantics=("arbitrary",), vmem_limit_bytes=32 * 2**20
        ),
        cost_estimate=free(),
        name="lay",
    )(at, *arrays)


def picked_kernel(at_ref, source_ref, out_ref):
    out_ref[...] = source_ref[...]


def picked(array, at):
    block = (1, *array.shape[1:])
    zeros = (0,) * (array.ndim - 1)
    return pl.pallas_call(
        picked_kernel,
        grid_spec=pltpu.PrefetchScalarGridSpec(
            num_scalar_prefetch=1,
            grid=(at.shape[0],),
            in_specs=[pl.BlockSpec(block, lambda n, at: (at[n], *zeros))],
            out_specs=pl.BlockSpec(block, lambda n, at: (n, *zeros)),
        ),
        out_shape=jax.ShapeDtypeStruct((at.shape[0], *array.shape[1:]), array.dtype),
        compiler_params=pltpu.CompilerParams(
            dimension_semantics=("arbitrary",), vmem_limit_bytes=32 * 2**20
        ),
        cost_estimate=free(),
        name="picked",
    )(at, array)


def ring_order(count):
    return list(range(0, count, 2)) + list(range(1, count, 2))[::-1]


def ring_pairs(count):
    order = ring_order(count)
    ahead = [(order[i], order[(i + 1) % count]) for i in range(count)]
    return ahead, [(b, a) for a, b in ahead]


def ring_ids():
    count = lax.axis_size("seq")
    order = ring_order(count)
    rank = {p: i for i, p in enumerate(order)}
    table = [[order[(rank[p] + j) % count] for j in range(count)] for p in range(count)]
    return jnp.asarray(np.array(table, np.int32))[lax.axis_index("seq")]


def send(values, axis, pairs):
    if values.ndim == 2 and values.shape[0] % 16 == 0:
        blocks = straight(values.reshape(values.shape[0] // 16, 16, values.shape[1]))
        return straight(lax.ppermute(blocks, axis, pairs)).reshape(values.shape)
    return straight(lax.ppermute(straight(values), axis, pairs))


def swap(values, axis, bit):
    return send(values, axis, [(i, i ^ bit) for i in range(lax.axis_size(axis))])


class Freight:
    def __init__(self):
        self.pending, self.now = [], 0

    def at(self, event, values, use):
        self.pending.append((max(event, self.now + 1), values, use))

    def after(self, events, values, use):
        self.at(self.now + events, values, use)

    def need(self, values, use):
        self.after(1, values, use)

    def carry(self, values, land, lag=1):
        self.after(lag, swap(values, "fsdp", 2), land)

    def blocks(self, terms, near_at, far_at, use):
        part = lax.axis_index("fsdp")
        terms = picked(terms, part ^ jnp.array([3, 1, 2, 0], jnp.int32))

        def near_there(near):
            away = straight((terms[2].astype(WIDE) + near[0].astype(WIDE)).astype(LOW))
            own = terms[3].astype(WIDE) + near[1].astype(WIDE)
            self.at(far_at, swap(away, "fsdp", 2), lambda far: use(own + far.astype(WIDE)))

        self.at(near_at, swap(straight(terms[:2]), "fsdp", 1), near_there)

    def chain(self, values, steps, use):
        if not steps:
            return use(values)
        self.need(values, lambda held: self.chain(steps[0](held), steps[1:], use))

    def __call__(self, *values):
        self.now += 1
        due = [(array, use) for event, array, use in self.pending if event <= self.now]
        self.pending = [item for item in self.pending if item[0] > self.now]
        out = lax.optimization_barrier((*values, *(array for array, _ in due)))
        for array, (_, use) in zip(out[len(values) :], due):
            use(array)
        return out[: len(values)]

    def finish(self):
        while self.pending:
            due, self.pending = self.pending, []
            for _, array, use in due:
                use(array)


def alone(*values):
    return values


def ring_gather_steps(rows, ids, beside=alone, after=None):
    count = lax.axis_size("seq")
    ahead, behind = ring_pairs(count)
    tokens = rows.shape[0]
    half = tokens // 2

    def put(full, part, index, offset=0):
        return straight(lax.dynamic_update_slice(full, part, (index * tokens + offset, 0)))

    rows = straight(rows)
    if after is not None:
        rows, _ = lax.optimization_barrier((rows, after))
    full = put(blank((count * tokens, rows.shape[1]), rows.dtype), rows, ids[0])
    up = down = rows
    for hop in range(1, (count + 1) // 2):
        up, down = beside(up, down)
        up, down = send(up, "seq", ahead), send(down, "seq", behind)
        landed = yield up, down
        if landed is not None:
            up, down = landed
            yield None
        full = put(put(full, up, ids[count - hop]), down, ids[hop])
    if count % 2 == 0:
        up, down = beside(straight(up[:half]), straight(down[half:]))
        up, down = send(up, "seq", ahead), send(down, "seq", behind)
        yield up, down
        full = put(put(full, up, ids[count // 2]), down, ids[count // 2], half)
    yield full, (up, down)


def ring_gather(rows, ids, beside=alone):
    for out in ring_gather_steps(rows, ids, beside):
        pass
    return out


def ring_reduce(term, ids, beside=alone):
    count = lax.axis_size("seq")
    ahead, behind = ring_pairs(count)
    middle = count // 2
    if count == 1:
        return term(ids[0])
    up = down = None
    if count % 2 == 0:
        whole = straight(term(ids[middle]).astype(LOW))
        half = whole.shape[0] // 2
        up, down = beside(straight(whole[:half]), straight(whole[half:]))
        up = send(up, "seq", ahead).astype(WIDE)
        down = send(down, "seq", behind).astype(WIDE)
        up = jnp.pad(up, ((0, half), (0, 0)))
        down = jnp.pad(down, ((half, 0), (0, 0)))
    for hop in range((count - 1) // 2, 0, -1):
        send_up = term(ids[hop])
        send_down = term(ids[count - hop])
        if up is not None:
            send_up, send_down = send_up + up, send_down + down
        send_up, send_down = beside(straight(send_up.astype(LOW)), straight(send_down.astype(LOW)))
        up = send(send_up, "seq", ahead).astype(WIDE)
        down = send(send_down, "seq", behind).astype(WIDE)
    return straight(term(ids[0]) + up + down)


def xor_steps(axis):
    def step(held, bit):
        return jnp.concatenate([held, swap(held, axis, bit)])

    bits = [1 << i for i in range((lax.axis_size(axis) - 1).bit_length())]
    return [functools.partial(step, bit=bit) for bit in bits]


def straighten(parts, axis):
    count = parts.shape[0]
    me = lax.axis_index(axis)
    bit = 1
    while bit < count:
        other = jnp.stack([parts[j ^ bit] for j in range(count)])
        parts = jnp.where((me & bit) != 0, other, parts)
        bit *= 2
    return parts


def sum_steps(axes):
    def step(values, axis, bit):
        return values + swap(values, axis, bit)

    return [
        functools.partial(step, axis=axis, bit=1 << i)
        for axis in axes
        for i in range((lax.axis_size(axis) - 1).bit_length())
    ]


UNIT_PARTS = [
    3, 1, 2, 1, 0, 1, 3, 2, 1, 0, 0, 1, 2, 0, 0, 3, 3, 3, 1, 2, 0, 0, 1, 1, 0, 1, 2, 1, 0, 3, 0, 3,
    0, 2, 0, 2, 0, 2, 0, 1, 1, 2, 0, 1, 1, 3, 1, 3, 3, 3, 0, 1, 2, 1, 0, 1, 1, 0, 1, 0, 2, 2, 0, 2,
    2, 0, 3, 0, 3, 3, 0, 0, 2, 1, 3, 3, 1, 2, 0, 1, 3, 0, 1, 0, 2, 2, 2, 1, 3, 3, 3, 2, 2, 3, 1, 0,
    0, 3, 3, 3, 0, 1, 2, 2, 3, 2, 2, 2, 1, 0, 0, 1, 1, 3, 3, 2, 1, 1, 1, 1, 2, 0, 3, 2, 0, 3, 0, 0,
    3, 2, 2, 2, 3, 3, 3, 3, 1, 1, 1, 0, 0, 3, 2, 2, 2, 3, 2, 3, 3, 2, 2, 3, 2, 2, 0, 1, 1, 1, 0, 3,
]
BLOCK_PARTS = [
    0, 3, 1, 2, 2, 3, 0, 1, 1, 2, 3, 0, 3, 0, 1, 2, 3, 0, 1, 2, 1, 0, 2, 3, 1, 2, 3, 0, 2, 3, 1, 0,
]


def group_places(groups):
    return [1, 4, 6, 3, 2, 0, 5, 7] if groups == 8 else list(range(groups))


@functools.lru_cache(None)
def unit_plan(fsdp, groups, query_width, pair_width):
    columns = query_width + 2 * pair_width
    per_device = columns // (fsdp * groups)
    group_query, group_pair = query_width // groups, pair_width // groups
    unit = math.gcd(math.gcd(per_device, group_query), group_pair)
    rounds = per_device // unit
    total = fsdp * groups
    wanted = []
    for index in range(columns // unit):
        column = index * unit
        if column < query_width:
            group, place = divmod(column, group_query)
        elif column < query_width + pair_width:
            group, place = divmod(column - query_width, group_pair)
            place += group_query
        else:
            group, place = divmod(column - query_width - pair_width, group_pair)
            place += group_query + group_pair
        wanted.append((index // rounds, index % rounds, group, place // unit))
    filled = {}
    edges = []
    near = UNIT_PARTS if groups == 8 and len(wanted) == len(UNIT_PARTS) else None
    spots = group_places(groups)
    for index, (source, slot, group, place) in enumerate(wanted):
        own = near[index] if near else source // groups
        for turn in (0, 1, 2, 3):
            part = own ^ turn
            if filled.get((part, group), 0) < rounds:
                filled[(part, group)] = filled.get((part, group), 0) + 1
                edges.append((source, slot, part * groups + spots[group], place))
                break
    steps = []
    for _ in range(rounds):
        taken = {}

        def find(source, seen):
            for edge in edges:
                if edge[0] != source or edge[2] in seen:
                    continue
                seen.add(edge[2])
                if edge[2] not in taken or find(taken[edge[2]][0], seen):
                    taken[edge[2]] = edge
                    return True
            return False

        for source in range(total):
            find(source, set())
        steps.append(sorted(taken.values()))
        for edge in taken.values():
            edges.remove(edge)
    send = np.zeros((rounds, total), np.int32)
    place_at = np.zeros((rounds, total), np.int32)
    pairs = []
    for i, step in enumerate(steps):
        pairs.append([(edge[0], edge[2]) for edge in step])
        for source, slot, target, place in step:
            send[i, source] = slot
            place_at[i, target] = place
    count = fsdp * rounds
    order = np.zeros((total, count), np.int32)
    back = np.zeros((total, count), np.int32)
    for device in range(total):
        group = device % groups
        for part in range(fsdp):
            for i in range(rounds):
                place = place_at[i, part * groups + group]
                order[device, place] = part * rounds + i
                back[device, part * rounds + i] = place
    home = np.argsort(send, axis=0).astype(np.int32)
    return unit, rounds, pairs, send, order, back, home


def out_pairs(fsdp, groups):
    total = fsdp * groups
    parts = BLOCK_PARTS if (fsdp, groups) == (4, 8) else [b % fsdp for b in range(total)]
    spots = group_places(groups)
    moves = [(b, parts[b] * groups + spots[b // fsdp]) for b in range(total)]
    found = np.zeros((total, fsdp), np.int32)
    for b, target in moves:
        found[target % groups :: groups, b % fsdp] = target // groups
    return moves, found


def turn(front, back, cosine, sine):
    return front * cosine - back * sine, back * cosine + front * sine


def forward_kernel(
    at_ref, sink_ref, front_ref, back_ref, key_front, key_back, value_front, value_back,
    query_bias, pair_bias, cos_ref, sin_ref,
    turned_ref, pairs_ref, out_ref, total_ref, keys,
    *, block, scale,
):
    head = pl.program_id(0)
    length = front_ref.shape[1]
    half = HD // 2
    cosine, sine = cos_ref[...], sin_ref[...]

    @pl.when(head == 0)
    def _():
        front, back = turn(
            key_front[...] + pair_bias[:half], key_back[...] + pair_bias[half:HD], cosine, sine
        )
        key = jnp.concatenate([front, back], axis=0)
        pairs_ref[:HD, :] = key.astype(LOW)
        pairs_ref[HD : HD + half, :] = (value_front[...] + pair_bias[HD : HD + half]).astype(LOW)
        pairs_ref[HD + half :, :] = (value_back[...] + pair_bias[HD + half :]).astype(LOW)
        keys[...] = key.T.astype(LOW)

    front, back = turn(
        front_ref[...] + query_bias[:half], back_ref[...] + query_bias[half:], cosine, sine
    )
    turned_ref[:half, :] = (front.astype(LOW).astype(WIDE) * scale).astype(LOW)
    turned_ref[half:, :] = (back.astype(LOW).astype(WIDE) * scale).astype(LOW)
    sink = sink_ref[head]
    count = length // block
    below = lax.broadcasted_iota(jnp.int32, (block, block), 0) > lax.broadcasted_iota(
        jnp.int32, (block, block), 1
    )
    for index in range(count):
        columns = pl.ds(index * block, block)
        query = turned_ref[:, columns]

        def scores(rows):
            return mul(keys[rows, :], query)

        def step(start, carry, masked):
            peak, total, mixed = carry
            rows = pl.ds(start, block)
            tile = scores(rows)
            if masked:
                tile = jnp.where(below, -1e30, tile)
            top = jnp.maximum(peak, jnp.max(tile, axis=0, keepdims=True))
            weights = jnp.exp(tile - top)
            shrink = jnp.exp(peak - top)
            total = total * shrink + jnp.sum(weights, axis=0, keepdims=True)
            mixed = mixed * shrink + mul(pairs_ref[HD:, rows], weights.astype(LOW))
            return top, total, mixed

        carry = (
            jnp.full((1, block), sink, WIDE),
            jnp.ones((1, block), WIDE),
            jnp.zeros((HD, block), WIDE),
        )
        if count <= 4:
            for earlier in range(index):
                carry = step(earlier * block, carry, False)
        elif index:
            carry = lax.fori_loop(
                0, index, lambda i, c: step(pl.multiple_of(i * block, block), c, False), carry
            )
        peak, total, mixed = step(index * block, carry, True)
        out_ref[:, columns] = (mixed / total).astype(LOW)
        total_ref[0, :, columns] = peak + jnp.log(total)


def attend(at, projected, bias, sinks, cosine, sine, heads):
    length = projected.shape[1]
    rows = heads * HD
    half = HD // 2
    block = min(256, length)
    last = rows // (2 * HD)

    def piece(place):
        return pl.BlockSpec((half, length), lambda h, at: (at[place], 0))

    return pl.pallas_call(
        functools.partial(forward_kernel, block=block, scale=HD**-0.5),
        grid_spec=pltpu.PrefetchScalarGridSpec(
            num_scalar_prefetch=1,
            grid=(heads,),
            in_specs=[
                pl.BlockSpec(memory_space=pltpu.SMEM),
                pl.BlockSpec((half, length), lambda h, at: (at[2 * h], 0)),
                pl.BlockSpec((half, length), lambda h, at: (at[2 * h + 1], 0)),
                piece(2 * heads),
                piece(2 * heads + 1),
                piece(2 * heads + 2),
                piece(2 * heads + 3),
                pl.BlockSpec((HD, 1), lambda h, at: (h, 0)),
                pl.BlockSpec((2 * HD, 1), lambda h, at: (last, 0)),
                pl.BlockSpec((half, length), lambda h, at: (0, 0)),
                pl.BlockSpec((half, length), lambda h, at: (0, 0)),
            ],
            out_specs=[
                pl.BlockSpec((HD, length), lambda h, at: (h, 0)),
                pl.BlockSpec((2 * HD, length), lambda h, at: (0, 0)),
                pl.BlockSpec((HD, length), lambda h, at: (at[2 * heads + 4 + h], 0)),
                pl.BlockSpec((1, 1, length), lambda h, at: (h, 0, 0)),
            ],
            scratch_shapes=[pltpu.VMEM((length, HD), LOW)],
        ),
        out_shape=[
            jax.ShapeDtypeStruct((rows, length), LOW),
            jax.ShapeDtypeStruct((2 * HD, length), LOW),
            jax.ShapeDtypeStruct((rows, length), LOW),
            jax.ShapeDtypeStruct((heads, 1, length), WIDE),
        ],
        compiler_params=pltpu.CompilerParams(
            dimension_semantics=("arbitrary",), vmem_limit_bytes=40 * 2**20
        ),
        cost_estimate=pl.CostEstimate(
            flops=0, bytes_accessed=22 * rows * length * 8, transcendentals=0
        ),
        name="attend",
    )(at, sinks, *[projected] * 6, bias, bias, cosine, sine)


def backward_kernel(
    at_ref, sink_ref, turned_ref, pairs_ref, out_ref, grad_ref, total_ref, cos_ref, sin_ref,
    query_ref, pair_ref, sink_grad_ref, keys, values, key_sum, value_sum, query_rows, grad_rows,
    *, block, scale,
):
    head = pl.program_id(0)
    length = turned_ref.shape[1]
    half = HD // 2
    count = length // block

    @pl.when(head == 0)
    def _():
        keys[...] = pairs_ref[:HD, :].astype(WIDE).T.astype(LOW)
        values[...] = pairs_ref[HD:, :].astype(WIDE).T.astype(LOW)
        key_sum[...] = jnp.zeros_like(key_sum)
        value_sum[...] = jnp.zeros_like(value_sum)

    query_rows[...] = turned_ref[...].astype(WIDE).T.astype(LOW)
    grad_rows[...] = grad_ref[...].astype(WIDE).T.astype(LOW)
    below = lax.broadcasted_iota(jnp.int32, (block, block), 0) > lax.broadcasted_iota(
        jnp.int32, (block, block), 1
    )
    deltas = jnp.sum(grad_ref[...].astype(WIDE) * out_ref[...].astype(WIDE), axis=0, keepdims=True)
    totals = total_ref[0]
    sink_term = -jnp.sum(jnp.exp(sink_ref[head] - totals) * deltas, axis=1, keepdims=True)
    sink_grad_ref[0] = jnp.broadcast_to(sink_term, (1, 128))
    for index in range(count):
        columns = pl.ds(index * block, block)
        query = turned_ref[:, columns]
        grad = grad_ref[:, columns]
        total = totals[:, index * block : (index + 1) * block]
        delta = deltas[:, index * block : (index + 1) * block]

        def step(start, query_sum, masked):
            rows = pl.ds(start, block)
            weights = jnp.exp(mul(keys[rows, :], query) - total)
            if masked:
                weights = jnp.where(below, 0.0, weights)
            inner = (weights * (mul(values[rows, :], grad) - delta)).astype(LOW)
            key_sum[rows, :] += mul(inner, query_rows[columns, :])
            value_sum[rows, :] += mul(weights.astype(LOW), grad_rows[columns, :])
            return query_sum + mul(pairs_ref[:HD, rows], inner)

        query_sum = jnp.zeros((HD, block), WIDE)
        if count <= 4:
            for earlier in range(index):
                query_sum = step(earlier * block, query_sum, False)
        elif index:
            query_sum = lax.fori_loop(
                0, index, lambda i, c: step(pl.multiple_of(i * block, block), c, False), query_sum
            )
        query_sum = step(index * block, query_sum, True)
        rounded = (query_sum * scale).astype(LOW).astype(WIDE)
        cosine, sine = cos_ref[:, columns], sin_ref[:, columns]
        front, back = turn(rounded[:half], rounded[half:], cosine, -sine)
        query_ref[:half, columns] = front.astype(LOW)
        query_ref[half:, columns] = back.astype(LOW)

    @pl.when(head == pl.num_programs(0) - 1)
    def _():
        rounded = key_sum[...].T.astype(LOW).astype(WIDE)
        front, back = turn(rounded[:half], rounded[half:], cos_ref[...], -sin_ref[...])
        pair_ref[:half, :] = front.astype(LOW)
        pair_ref[half:HD, :] = back.astype(LOW)
        pair_ref[HD:, :] = value_sum[...].T.astype(LOW)


def attend_back(at, sinks, turned, pairs, attended, upstream, totals, cosine, sine):
    heads, _, length = totals.shape
    rows = heads * HD
    block = min(256, length)
    by_head = pl.BlockSpec((HD, length), lambda h, at: (h, 0))
    moved = pl.BlockSpec((HD, length), lambda h, at: (at[2 * heads + 4 + h], 0))
    table = pl.BlockSpec((HD // 2, length), lambda h, at: (0, 0))
    whole = pl.BlockSpec((2 * HD, length), lambda h, at: (0, 0))
    return pl.pallas_call(
        functools.partial(backward_kernel, block=block, scale=HD**-0.5),
        grid_spec=pltpu.PrefetchScalarGridSpec(
            num_scalar_prefetch=1,
            grid=(heads,),
            in_specs=[
                pl.BlockSpec(memory_space=pltpu.SMEM),
                by_head,
                whole,
                moved,
                moved,
                pl.BlockSpec((1, 1, length), lambda h, at: (h, 0, 0)),
                table,
                table,
            ],
            out_specs=[by_head, whole, pl.BlockSpec((1, 1, 128), lambda h, at: (h, 0, 0))],
            scratch_shapes=[
                pltpu.VMEM((length, HD), LOW),
                pltpu.VMEM((length, HD), LOW),
                pltpu.VMEM((length, HD), WIDE),
                pltpu.VMEM((length, HD), WIDE),
                pltpu.VMEM((length, HD), LOW),
                pltpu.VMEM((length, HD), LOW),
            ],
        ),
        out_shape=[
            jax.ShapeDtypeStruct((rows, length), LOW),
            jax.ShapeDtypeStruct((2 * HD, length), LOW),
            jax.ShapeDtypeStruct((heads, 1, 128), WIDE),
        ],
        compiler_params=pltpu.CompilerParams(
            dimension_semantics=("arbitrary",), vmem_limit_bytes=40 * 2**20
        ),
        cost_estimate=pl.CostEstimate(
            flops=0, bytes_accessed=0, transcendentals=0
        ),
        name="attend_back",
    )(at, sinks, turned, pairs, attended, upstream, totals, cosine, sine)


EXTRA = 16


def term_kernel(left_ref, right_ref, extra_ref, out_ref):
    size = left_ref.shape[0]
    out_ref[:size, :] = mul(left_ref[...], right_ref[...]).astype(LOW)
    out_ref[size:, :] = extra_ref[...].astype(LOW)


def column_parts(width, count):
    block = min(640, width)
    tiles = pl.cdiv(width, block)
    ends = [round(tiles * i / count) for i in range(count + 1)]
    return block, [(a, b - a) for a, b in zip(ends, ends[1:]) if b > a]


def weight_term(left, right, extra, size, block, tiles):
    depth, width = right.shape
    first, count = tiles
    shards = left.shape[0] // size
    columns = min(width, (first + count) * block) - first * block
    return pl.pallas_call(
        term_kernel,
        grid=(shards, count),
        in_specs=[
            pl.BlockSpec((size, depth), lambda m, n: (m, 0)),
            pl.BlockSpec((depth, block), lambda m, n: (0, n + first)),
            pl.BlockSpec((EXTRA, block), lambda m, n: (0, n + first)),
        ],
        out_specs=pl.BlockSpec((size + EXTRA, block), lambda m, n: (m, n)),
        out_shape=jax.ShapeDtypeStruct((shards * (size + EXTRA), columns), LOW),
        compiler_params=pltpu.CompilerParams(
            dimension_semantics=("arbitrary", "arbitrary"), vmem_limit_bytes=56 * 2**20
        ),
        cost_estimate=free(),
        name="weight_term",
    )(left, right, extra)


def rms_scale(values, norm_gain):
    factor = lax.rsqrt(jnp.mean(values * values, axis=-1, keepdims=True) + NORM_EPSILON)
    return (values * factor * norm_gain, factor)


def rms_back(values, factor, norm_gain, upstream):
    scaled = upstream * norm_gain
    value_grad = factor * scaled - values * factor * factor * factor * jnp.mean(
        scaled * values, axis=-1, keepdims=True
    )
    gain_grad = jnp.sum(upstream * values * factor, axis=0)
    return (value_grad, gain_grad)


def clamped_glu(joined, expert_width):
    gate_part = jnp.minimum(joined[:, :expert_width], CLAMP_LIMIT)
    linear_part = jnp.clip(joined[:, expert_width:], -CLAMP_LIMIT, CLAMP_LIMIT)
    return (linear_part + 1.0) * gate_part * jax.nn.sigmoid(SWIGLU_SLOPE * gate_part)


def glu_back(joined, expert_width, upstream):
    raw_gate = joined[:, :expert_width]
    raw_linear = joined[:, expert_width:]
    gate_part = jnp.minimum(raw_gate, CLAMP_LIMIT)
    linear_part = jnp.clip(raw_linear, -CLAMP_LIMIT, CLAMP_LIMIT)
    sigmoid_part = jax.nn.sigmoid(SWIGLU_SLOPE * gate_part)
    gate_open = (raw_gate < CLAMP_LIMIT).astype(jnp.float32)
    linear_open = (jnp.abs(raw_linear) < CLAMP_LIMIT).astype(jnp.float32)
    slope_part = sigmoid_part + gate_part * SWIGLU_SLOPE * sigmoid_part * (1.0 - sigmoid_part)
    gate_grad = upstream * (linear_part + 1.0) * slope_part * gate_open
    linear_grad = upstream * gate_part * sigmoid_part * linear_open
    return jnp.concatenate([gate_grad, linear_grad], axis=1)


def mixing_of(rows, routes, router_weight, router_bias):
    logits = mul(rows, router_weight) + router_bias
    experts = jnp.arange(router_bias.shape[0], dtype=jnp.int32)
    chosen = jnp.any(routes[:, :, None] == experts, axis=1)
    logits = jnp.where(chosen, logits, -jnp.inf)
    weights = jnp.exp(logits - jnp.max(logits, axis=1, keepdims=True))
    return weights / jnp.sum(weights, axis=1, keepdims=True)


def rows_of(values, index, size):
    return lax.dynamic_slice_in_dim(values, index * size, size, axis=0)


def columns_of(values, index, size):
    return lax.dynamic_slice_in_dim(values, index * size, size, axis=1)


def body(
    hidden,
    out_grad,
    routes,
    norm1_gain,
    qkv_weight,
    qkv_bias,
    sink_logits,
    out_weight,
    out_bias,
    norm2_gain,
    router_weight,
    router_bias,
    gate_up_weight,
    gate_up_bias,
    down_weight,
    down_bias,
):
    tokens = hidden.shape[1]
    groups = lax.axis_size("seq")
    position = lax.axis_index("seq")
    spots = np.argsort(np.array(group_places(lax.axis_size("seq")))).astype(np.int32)
    group = jnp.asarray(spots)[position]
    fsdp = lax.axis_size("fsdp")
    part = lax.axis_index("fsdp")
    device = part * groups + position
    head_count = sink_logits.shape[0]
    group_heads = head_count // groups
    expert_width = down_weight.shape[1] * fsdp
    capacity = tokens * TOPK * 9 // (8 * groups)
    slot_count = groups * capacity
    length = tokens * groups
    query_width = head_count * HD
    pair_width = KV_HEADS * HD
    group_query = group_heads * HD
    ids = ring_ids()

    planned = groups == KV_HEADS and fsdp == 4 and qkv_weight.shape[1] % (HD // 2) == 0
    qkv_rows = straight(qkv_weight.T)
    held = {}
    freight = Freight()
    out_moves, out_found = out_pairs(fsdp, groups)

    def keep(name):
        return lambda values: held.__setitem__(name, values)

    if planned:
        unit, rounds, pairs, send_slots, order, back, home = unit_plan(
            fsdp, groups, query_width, pair_width
        )
        slots = jnp.asarray(send_slots)[:, device]
        bias_at = (group, group, group)
        head_units = jnp.asarray(order)[device]

        def open_units(weight):
            units = weight.reshape(rounds, unit, -1)
            blocks = [
                send(lax.dynamic_index_in_dim(units, slots[i], 0, keepdims=False), BOTH, pairs[i])
                for i in range(rounds)
            ]
            freight.need(lay(*blocks).reshape(rounds * unit, -1), units_there)

        def units_there(mine):
            held["qkv"] = lax.all_gather(mine, "fsdp", axis=0, tiled=True)

        freight.need(qkv_rows, open_units)
    else:
        pair_index = group * KV_HEADS // groups
        bias_at = (group, pair_index, pair_index)
        head_units = jnp.arange(2 * group_heads + 4, dtype=jnp.int32)
    bias_group = jnp.concatenate(
        [
            rows_of(qkv_bias[:query_width], bias_at[0], group_query),
            rows_of(qkv_bias[query_width : query_width + pair_width], bias_at[1], HD),
            rows_of(qkv_bias[query_width + pair_width :], bias_at[2], HD),
        ]
    )
    block_heads = out_weight.shape[0] // HD
    by_block = out_weight.shape[0] % HD == 0
    head_ids = jnp.arange(group_heads, dtype=jnp.int32)
    if by_block:
        turns = jnp.asarray(np.repeat(out_found, block_heads, axis=1))[device]
        head_ids = turns * block_heads + head_ids % block_heads
    places_at = jnp.concatenate([head_units, head_ids])

    def open_out(weight):
        freight.after(2, send(weight, BOTH, out_moves), out_there)

    def out_there(mine):
        held["out_mine"], held["out_far"] = mine, swap(mine, "fsdp", 2)

    def open_gate_up(shard):
        held["gate_up"] = lax.all_gather(shard, "fsdp", axis=0, tiled=True)

    held["down"] = lax.all_gather(down_weight[0], "fsdp", axis=0, tiled=True)
    freight.after(2, out_weight, open_out)
    freight.after(3, gate_up_weight[0], open_gate_up)

    def open_routes(own):
        own = jnp.broadcast_to(own.reshape(1, -1), (groups, tokens * TOPK))
        held["routes"] = lax.all_to_all(own, "seq", split_axis=0, concat_axis=0, tiled=True)

    freight.after(4, routes, open_routes)

    inputs = hidden[0].astype(WIDE)
    first_normed, first_factor = rms_scale(inputs, norm1_gain)
    first_full, first_last = ring_gather(first_normed.astype(LOW), ids, freight)
    frequency = ROPE_BASE ** (-(jnp.arange(HD // 2, dtype=WIDE) * 2.0) / HD)
    angles = jnp.arange(length, dtype=jnp.int32).astype(WIDE)[None, :] * frequency[:, None]
    cosine, sine = jnp.cos(angles), jnp.sin(angles)
    sink_part = rows_of(sink_logits, group, group_heads)
    gather = ring_gather_steps(out_grad[0], ids, freight, first_last)
    hop = next(gather)
    if planned:
        qkv_group = held["qkv"]
    else:
        qkv_full = lax.all_gather(qkv_rows, BOTH, axis=0, tiled=True)
        qkv_group = jnp.concatenate(
            [
                rows_of(qkv_full[:query_width], group, group_query),
                rows_of(qkv_full[query_width : query_width + pair_width], pair_index, HD),
                rows_of(qkv_full[query_width + pair_width :], pair_index, HD),
            ]
        )
    projected, held["routes"] = lax.optimization_barrier(
        (mul(qkv_group, first_full, NT), held["routes"])
    )
    turned, pair_rows, attended, log_totals = attend(
        places_at, projected, bias_group[:, None], sink_part, cosine, sine, group_heads
    )
    mine, far, attended = lax.optimization_barrier((held["out_mine"], held["out_far"], attended))
    near = swap(lay(mine, far), "fsdp", 1)
    parts = part ^ jnp.arange(fsdp, dtype=jnp.int32)
    out_group = lay(mine, (near, 0), far, (near, 1), at=parts).reshape(fsdp * mine.shape[0], -1)

    freight.need(hop, gather.send)
    biases = jnp.concatenate([gate_up_bias, down_bias], axis=1)
    freight.chain(biases, xor_steps("fsdp"), keep("biases"))
    branch = ring_reduce(
        lambda index: mul(columns_of(attended, index, tokens), out_group, TN), ids, freight
    )
    middle = inputs + (branch + out_bias)
    second_normed, second_factor = rms_scale(middle, norm2_gain)
    second_low = second_normed.astype(LOW)

    second_full, last = ring_gather(second_low, ids, freight)
    freight.need(last[0], lambda values: None)
    next(gather)
    freight.finish()
    joined_weight, down_full = held["gate_up"], held["down"]
    all_routes = held["routes"].reshape(length, TOPK)
    biases = straighten(held["biases"], "fsdp")
    joined_bias = biases[:, : gate_up_bias.shape[1]].reshape(-1).astype(WIDE)
    down_shift = biases[:, gate_up_bias.shape[1] :].reshape(-1).astype(WIDE)
    mine = jnp.any(all_routes == position, axis=1)
    counted = mine.astype(jnp.int32)
    earlier = jnp.cumsum(counted) - counted
    places = jnp.where(mine, earlier, -1)
    slots_here = jnp.arange(slot_count, dtype=jnp.int32)
    into = slots_here[:, None] == places[None, :]
    back_to = places[:, None] == slots_here[None, :]
    into_low, back_low = into.astype(LOW), back_to.astype(LOW)
    mixing_all = mixing_of(second_full, all_routes, router_weight, router_bias)
    expert_ids = jnp.arange(groups, dtype=jnp.int32)
    mixing_mine = jnp.sum(jnp.where(expert_ids == position, mixing_all, 0.0), axis=1)
    mixing_rows = jnp.sum(jnp.where(into, mixing_mine[None, :], 0.0), axis=1)[:, None]
    next(gather)
    expert_rows = mul(into_low, second_full).astype(LOW)
    freight.need(straight(mul(expert_rows, joined_weight) + joined_bias), keep("joined"))
    next(gather)
    joined = held["joined"]
    activated = lax.optimization_barrier(clamped_glu(joined, expert_width).astype(LOW))
    expert_columns = expert_rows.T
    upstream_full = None
    for upstream_full in gather:
        pass
    upstream_full = upstream_full[0]
    freight.finish()
    freight = Freight()
    upstream_rows = mul(into_low, upstream_full)
    rows_grad = (upstream_rows * mixing_rows).astype(LOW)
    down_term = straight(mul(activated, rows_grad, TN).astype(LOW))
    down_total = lax.psum_scatter(down_term, "fsdp", scatter_dimension=0, tiled=True)
    freight.at(9, down_total, lambda total: freight.need(total.astype(WIDE), keep("down_shard")))
    activated, _ = lax.optimization_barrier((activated, down_term))
    expert_out = (mul(activated, down_full) + down_shift).astype(LOW).astype(WIDE)
    weighted = (expert_out * mixing_rows).astype(LOW)
    mixing_grad_rows = jnp.sum(upstream_rows * expert_out, axis=1)
    down_sums = jnp.sum(rows_grad.astype(WIDE), axis=0, keepdims=True)


    def back_first(upstream):
        activated_grad = mul(upstream, down_full, NT)
        grad = straight(glu_back(joined, expert_width, activated_grad).astype(LOW))
        freight.need(grad, back_second)

    def back_second(grad):
        held["input_rows_grad"] = straight(mul(grad, joined_weight, NT).astype(LOW))
        back_third(grad)

    def back_third(grad):
        sums = jnp.sum(grad.astype(WIDE), axis=0, keepdims=True)
        extra = jnp.concatenate([sums, jnp.pad(down_sums, ((0, 0), (0, expert_width)))])
        extra = jnp.pad(extra, ((0, EXTRA - 2), (0, 0)))
        block, split = column_parts(grad.shape[1], 3)
        held["joined_parts"] = [None] * len(split)
        held["joined_shard"] = blank((hidden.shape[2] // fsdp, grad.shape[1]), WIDE)

        def part_there(i, term):
            total = lax.psum_scatter(term, "fsdp", scatter_dimension=0, tiled=True)
            freight.at([11, 14, 16][i], total, functools.partial(part_kept, i))

        def part_kept(i, total):
            own_rows = hidden.shape[2] // fsdp
            rows = total[:own_rows].astype(WIDE)
            start = split[i][0] * block
            held["joined_shard"] = lax.dynamic_update_slice(held["joined_shard"], rows, (0, start))
            held["joined_parts"][i] = total[own_rows : own_rows + 2].astype(WIDE)
            if i + 1 < len(split):
                freight.need(held["joined_shard"], keep("joined_shard"))

        def begin(i, held_here):
            grad, extra = held_here
            size = hidden.shape[2] // fsdp
            term = weight_term(expert_columns, grad, extra, size, block, split[i])
            freight.need(term, functools.partial(part_there, i))

        begin(0, (grad, extra))
        for i in range(1, len(split)):
            freight.at([2, 5, 7][i], (grad, extra), functools.partial(begin, i))

    def mixing_back(rows):
        tokens_grad = jnp.sum(jnp.where(back_to, rows[None, :], 0.0), axis=1)
        by_device = lax.all_to_all(
            tokens_grad.reshape(groups, tokens), "seq", split_axis=0, concat_axis=0, tiled=True
        )
        freight.need(by_device, keep("mixing_grad"))

    freight.need(mixing_grad_rows, mixing_back)
    freight.need(rows_grad, back_first)
    combined = ring_reduce(lambda index: mul(rows_of(back_low, index, tokens), weighted), ids, freight)
    freight.need((middle + combined).astype(LOW), keep("outputs"))
    if "input_rows_grad" not in held:
        freight.finish()
    input_rows_grad = held["input_rows_grad"]
    second_grad = ring_reduce(
        lambda index: mul(rows_of(back_low, index, tokens), input_rows_grad), ids, freight
    )
    mixing = mixing_of(second_low, routes[0], router_weight, router_bias)
    mixing_grad = held["mixing_grad"].T
    logits_grad = mixing * (
        mixing_grad - jnp.sum(mixing * mixing_grad, axis=-1, keepdims=True)
    )
    second_grad = second_grad + jnp.dot(
        logits_grad, router_weight.astype(WIDE).T, precision=PRECISE
    )
    upstream = out_grad[0].astype(WIDE)
    middle_part, gain2_grad = rms_back(middle, second_factor, norm2_gain, second_grad)
    middle_grad = upstream + middle_part
    branch_low = middle_grad.astype(LOW)

    width = hidden.shape[2]

    router_weight_grad = jnp.dot(second_low.astype(WIDE).T, logits_grad, precision=PRECISE)
    router_bias_grad = jnp.sum(logits_grad, axis=0)
    out_bias_grad = jnp.sum(branch_low.astype(WIDE), axis=0)
    early = [out_bias_grad, gain2_grad, router_weight_grad.T.reshape(-1), router_bias_grad]
    branch_full, _ = ring_gather(branch_low, ids, freight)
    heads_grad = mul(out_group, branch_full, NT).astype(LOW)
    query_grad, pair_grad, sink_grad = attend_back(
        places_at, sink_part, turned, pair_rows, attended, heads_grad, log_totals, cosine, sine
    )
    projected_grad = jnp.concatenate([query_grad, pair_grad])
    bias_term = jnp.sum(projected_grad.astype(WIDE), axis=1)
    if planned:
        projected_grad = jnp.take(
            projected_grad.reshape(fsdp * rounds, unit, -1),
            jnp.asarray(back)[device],
            axis=0,
            mode="clip",
        ).reshape(projected_grad.shape)

    bias_full = jnp.zeros((query_width + 2 * pair_width,), WIDE)
    bias_full = lax.dynamic_update_slice(
        bias_full, bias_term[:group_query], (bias_at[0] * group_query,)
    )
    bias_full = lax.dynamic_update_slice(
        bias_full, bias_term[group_query : group_query + HD], (query_width + bias_at[1] * HD,)
    )
    bias_full = lax.dynamic_update_slice(
        bias_full,
        bias_term[group_query + HD :],
        (query_width + pair_width + bias_at[2] * HD,),
    )
    sink_full = lax.dynamic_update_slice_in_dim(
        jnp.zeros((head_count,), WIDE), sink_grad[:, 0, 0], group * group_heads, 0
    )

    def out_first(grad):
        terms = straight(mul(attended, grad).astype(LOW))

        def use(total):
            held["out_total"] = total.astype(LOW)

        freight.blocks(terms.reshape(fsdp, out_weight.shape[0], -1), 15, 16, use)

    def qkv_first(grad):
        terms = mul(grad, first_full)
        low = straight(terms.astype(LOW))
        sums = jnp.sum(low.astype(WIDE) * qkv_group.astype(WIDE), axis=0) / norm1_gain
        late = jnp.concatenate([sums, bias_full, sink_full, *early])
        freight.chain(late, sum_steps(["seq"]), keep("late"))
        if not planned:
            held["qkv_term"] = terms
            return

        def come_back(total):
            held["qkv_total"] = straight(total.astype(LOW))

        freight.blocks(low.reshape(fsdp, rounds, unit, -1), 14, 16, come_back)

    freight.need(projected_grad, qkv_first)
    freight.at(14, branch_full, out_first)
    first_grad = ring_reduce(
        lambda index: mul(columns_of(projected_grad, index, tokens), qkv_group, TN), ids, freight
    )
    freight.finish()
    joined_sums = jnp.concatenate(held["joined_parts"], axis=1)
    joined_shard = held["joined_shard"]
    joined_bias_shard = rows_of(joined_sums[0], part, gate_up_bias.shape[1])
    down_bias_shard = rows_of(joined_sums[1, :width], part, down_bias.shape[1])
    down_shard = held["down_shard"]
    qkv_total = held.get("qkv_total", held["out_total"])
    late, first_grad, out_total, qkv_total = lax.optimization_barrier(
        (held["late"], first_grad, held["out_total"], qkv_total)
    )
    if planned:
        returned = lay(
            *[
                send(qkv_total[i], BOTH, [(b, a) for a, b in pairs[i]])
                for i in range(rounds)
            ]
        )
    if planned:
        qkv_shard = jnp.take(returned, jnp.asarray(home)[:, device], axis=0, mode="clip")
        qkv_shard = qkv_shard.reshape(rounds * unit, -1).T.astype(WIDE)
    else:
        qkv_term = held["qkv_term"]
        scattered = jnp.zeros((query_width + 2 * pair_width, width), WIDE)
        for start, stop, row in (
            (0, group_query, group * group_query),
            (group_query, group_query + HD, query_width + pair_index * HD),
            (group_query + HD, group_query + 2 * HD, query_width + pair_width + pair_index * HD),
        ):
            scattered = lax.dynamic_update_slice(scattered, qkv_term[start:stop], (row, 0))
        qkv_shard = lax.psum_scatter(scattered, BOTH, scatter_dimension=0, tiled=True).T
    out_shard = send(out_total, BOTH, [(b, a) for a, b in out_moves]).astype(WIDE)
    for step in sum_steps(["fsdp"]):
        late = step(late)
    input_part, _ = rms_back(inputs, first_factor, norm1_gain, first_grad)
    input_grad = middle_grad + input_part

    early = late[width + qkv_bias.shape[0] + head_count :]
    router_sums = early[2 * width : 2 * width + width * groups].reshape(groups, width).T
    return (
        held["outputs"][None],
        input_grad.astype(LOW)[None],
        late[:width],
        qkv_shard,
        late[width : width + qkv_bias.shape[0]],
        late[width + qkv_bias.shape[0] : width + qkv_bias.shape[0] + head_count],
        out_shard,
        early[:width],
        early[width : 2 * width],
        router_sums,
        early[2 * width + width * groups : 2 * width + (width + 1) * groups],
        joined_shard[None],
        joined_bias_shard[None],
        down_shard[None],
        down_bias_shard[None],
    )


def solution(mesh):
    tokens = P("fsdp", "seq", None)
    by_expert = P("seq", "fsdp", None)
    return jax.shard_map(
        body,
        mesh=mesh,
        in_specs=(
            tokens, tokens, tokens, P(), P(None, BOTH), P(), P(), P(BOTH, None), P(), P(), P(), P(),
            by_expert, P("seq", "fsdp"), by_expert, P("seq", "fsdp"),
        ),
        out_specs=(
            tokens, tokens, P(), P(None, BOTH), P(), P(), P(BOTH, None), P(), P(), P(), P(),
            by_expert, P("seq", "fsdp"), by_expert, P("seq", "fsdp"),
        ),
        check_vma=False,
    )
```

```python
import functools
import math

import jax
import jax.numpy as jnp
import numpy as np
from jax import lax
from jax.experimental.layout import Layout, with_layout_constraint
from jax.experimental import pallas as pl
from jax.experimental.pallas import tpu as pltpu
from jax.sharding import PartitionSpec as P

KV_HEADS = 8
HD = 64
TOPK = 4

ROPE_BASE = 150000.0
SWIGLU_SLOPE = 1.702
CLAMP_LIMIT = 7.0
NORM_EPSILON = 1e-05
PRECISE = lax.Precision.HIGHEST
BOTH = ("fsdp", "seq")
LOW = jnp.bfloat16
WIDE = jnp.float32
NN = (((1,), (0,)), ((), ()))
NT = (((1,), (1,)), ((), ()))
TN = (((0,), (0,)), ((), ()))


def mul(left, right, dims=NN):
    return lax.dot_general(left, right, dims, preferred_element_type=WIDE)


def straight(values):
    return with_layout_constraint(values, Layout(major_to_minor=tuple(range(values.ndim))))


def blank(shape, dtype):
    return pl.pallas_call(
        lambda out: None,
        out_specs=pl.BlockSpec(memory_space=pl.ANY),
        out_shape=jax.ShapeDtypeStruct(shape, dtype),
        name="blank",
    )()


def free():
    return pl.CostEstimate(flops=0, bytes_accessed=0, transcendentals=0)


def pick_kernel(*refs, count):
    out = refs[-1]
    for i in range(count):

        @pl.when(pl.program_id(0) == i)
        def _(i=i):
            out[...] = refs[i][...].reshape(out.shape)


def lay_kernel(at_ref, *refs, count):
    pick_kernel(*refs, count=count)


def lay(*parts, at=None):
    arrays, specs = [], []
    for part in parts:
        array, index = part if isinstance(part, tuple) else (part[None], 0)
        arrays.append(array)
        place = (index,) + (0,) * (array.ndim - 1)
        specs.append(pl.BlockSpec((1, *array.shape[1:]), lambda n, at, place=place: place))
    block = arrays[0].shape[1:]
    zeros = (0,) * len(block)
    at = jnp.arange(len(parts), dtype=jnp.int32) if at is None else at
    return pl.pallas_call(
        functools.partial(lay_kernel, count=len(parts)),
        grid_spec=pltpu.PrefetchScalarGridSpec(
            num_scalar_prefetch=1,
            grid=(len(parts),),
            in_specs=specs,
            out_specs=pl.BlockSpec((1, *block), lambda n, at: (at[n], *zeros)),
        ),
        out_shape=jax.ShapeDtypeStruct((len(parts), *block), arrays[0].dtype),
        compiler_params=pltpu.CompilerParams(
            dimension_semantics=("arbitrary",), vmem_limit_bytes=32 * 2**20
        ),
        cost_estimate=free(),
        name="lay",
    )(at, *arrays)


def picked_kernel(at_ref, source_ref, out_ref):
    out_ref[...] = source_ref[...]


def picked(array, at):
    block = (1, *array.shape[1:])
    zeros = (0,) * (array.ndim - 1)
    return pl.pallas_call(
        picked_kernel,
        grid_spec=pltpu.PrefetchScalarGridSpec(
            num_scalar_prefetch=1,
            grid=(at.shape[0],),
            in_specs=[pl.BlockSpec(block, lambda n, at: (at[n], *zeros))],
            out_specs=pl.BlockSpec(block, lambda n, at: (n, *zeros)),
        ),
        out_shape=jax.ShapeDtypeStruct((at.shape[0], *array.shape[1:]), array.dtype),
        compiler_params=pltpu.CompilerParams(
            dimension_semantics=("arbitrary",), vmem_limit_bytes=32 * 2**20
        ),
        cost_estimate=free(),
        name="picked",
    )(at, array)


def ring_order(count):
    return list(range(0, count, 2)) + list(range(1, count, 2))[::-1]


def ring_pairs(count):
    order = ring_order(count)
    ahead = [(order[i], order[(i + 1) % count]) for i in range(count)]
    return ahead, [(b, a) for a, b in ahead]


def ring_ids():
    count = lax.axis_size("seq")
    order = ring_order(count)
    rank = {p: i for i, p in enumerate(order)}
    table = [[order[(rank[p] + j) % count] for j in range(count)] for p in range(count)]
    return jnp.asarray(np.array(table, np.int32))[lax.axis_index("seq")]


def send(values, axis, pairs):
    if values.ndim == 2 and values.shape[0] % 16 == 0:
        blocks = straight(values.reshape(values.shape[0] // 16, 16, values.shape[1]))
        return straight(lax.ppermute(blocks, axis, pairs)).reshape(values.shape)
    return straight(lax.ppermute(straight(values), axis, pairs))


def swap(values, axis, bit):
    return send(values, axis, [(i, i ^ bit) for i in range(lax.axis_size(axis))])


class Freight:
    def __init__(self):
        self.pending, self.now = [], 0

    def at(self, event, values, use):
        self.pending.append((max(event, self.now + 1), values, use))

    def after(self, events, values, use):
        self.at(self.now + events, values, use)

    def need(self, values, use):
        self.after(1, values, use)

    def carry(self, values, land, lag=1):
        self.after(lag, swap(values, "fsdp", 2), land)

    def blocks(self, terms, near_at, far_at, use):
        part = lax.axis_index("fsdp")
        terms = picked(terms, part ^ jnp.array([3, 1, 2, 0], jnp.int32))

        def near_there(near):
            away = straight((terms[2].astype(WIDE) + near[0].astype(WIDE)).astype(LOW))
            own = terms[3].astype(WIDE) + near[1].astype(WIDE)
            self.at(far_at, swap(away, "fsdp", 2), lambda far: use(own + far.astype(WIDE)))

        self.at(near_at, swap(straight(terms[:2]), "fsdp", 1), near_there)

    def chain(self, values, steps, use):
        if not steps:
            return use(values)
        self.need(values, lambda held: self.chain(steps[0](held), steps[1:], use))

    def __call__(self, *values):
        self.now += 1
        due = [(array, use) for event, array, use in self.pending if event <= self.now]
        self.pending = [item for item in self.pending if item[0] > self.now]
        out = lax.optimization_barrier((*values, *(array for array, _ in due)))
        for array, (_, use) in zip(out[len(values) :], due):
            use(array)
        return out[: len(values)]

    def finish(self):
        while self.pending:
            due, self.pending = self.pending, []
            for _, array, use in due:
                use(array)


def alone(*values):
    return values


def ring_gather_steps(rows, ids, beside=alone, after=None):
    count = lax.axis_size("seq")
    ahead, behind = ring_pairs(count)
    tokens = rows.shape[0]
    half = tokens // 2

    def put(full, part, index, offset=0):
        return straight(lax.dynamic_update_slice(full, part, (index * tokens + offset, 0)))

    rows = straight(rows)
    if after is not None:
        rows, _ = lax.optimization_barrier((rows, after))
    full = put(blank((count * tokens, rows.shape[1]), rows.dtype), rows, ids[0])
    up = down = rows
    for hop in range(1, (count + 1) // 2):
        up, down = beside(up, down)
        up, down = send(up, "seq", ahead), send(down, "seq", behind)
        landed = yield up, down
        if landed is not None:
            up, down = landed
            yield None
        full = put(put(full, up, ids[count - hop]), down, ids[hop])
    if count % 2 == 0:
        up, down = beside(straight(up[:half]), straight(down[half:]))
        up, down = send(up, "seq", ahead), send(down, "seq", behind)
        yield up, down
        full = put(put(full, up, ids[count // 2]), down, ids[count // 2], half)
    yield full, (up, down)


def ring_gather(rows, ids, beside=alone):
    for out in ring_gather_steps(rows, ids, beside):
        pass
    return out


def ring_reduce(term, ids, beside=alone):
    count = lax.axis_size("seq")
    ahead, behind = ring_pairs(count)
    middle = count // 2
    if count == 1:
        return term(ids[0])
    up = down = None
    if count % 2 == 0:
        whole = straight(term(ids[middle]).astype(LOW))
        half = whole.shape[0] // 2
        up, down = beside(straight(whole[:half]), straight(whole[half:]))
        up = send(up, "seq", ahead).astype(WIDE)
        down = send(down, "seq", behind).astype(WIDE)
        up = jnp.pad(up, ((0, half), (0, 0)))
        down = jnp.pad(down, ((half, 0), (0, 0)))
    for hop in range((count - 1) // 2, 0, -1):
        send_up = term(ids[hop])
        send_down = term(ids[count - hop])
        if up is not None:
            send_up, send_down = send_up + up, send_down + down
        send_up, send_down = beside(straight(send_up.astype(LOW)), straight(send_down.astype(LOW)))
        up = send(send_up, "seq", ahead).astype(WIDE)
        down = send(send_down, "seq", behind).astype(WIDE)
    return straight(term(ids[0]) + up + down)


def xor_steps(axis):
    def step(held, bit):
        return jnp.concatenate([held, swap(held, axis, bit)])

    bits = [1 << i for i in range((lax.axis_size(axis) - 1).bit_length())]
    return [functools.partial(step, bit=bit) for bit in bits]


def straighten(parts, axis):
    count = parts.shape[0]
    me = lax.axis_index(axis)
    bit = 1
    while bit < count:
        other = jnp.stack([parts[j ^ bit] for j in range(count)])
        parts = jnp.where((me & bit) != 0, other, parts)
        bit *= 2
    return parts


def sum_steps(axes):
    def step(values, axis, bit):
        return values + swap(values, axis, bit)

    return [
        functools.partial(step, axis=axis, bit=1 << i)
        for axis in axes
        for i in range((lax.axis_size(axis) - 1).bit_length())
    ]


UNIT_PARTS = [
    3, 1, 2, 1, 0, 1, 3, 2, 1, 0, 0, 1, 2, 0, 0, 3, 3, 3, 1, 2, 0, 0, 1, 1, 0, 1, 2, 1, 0, 3, 0, 3,
    0, 2, 0, 2, 0, 2, 0, 1, 1, 2, 0, 1, 1, 3, 1, 3, 3, 3, 0, 1, 2, 1, 0, 1, 1, 0, 1, 0, 2, 2, 0, 2,
    2, 0, 3, 0, 3, 3, 0, 0, 2, 1, 3, 3, 1, 2, 0, 1, 3, 0, 1, 0, 2, 2, 2, 1, 3, 3, 3, 2, 2, 3, 1, 0,
    0, 3, 3, 3, 0, 1, 2, 2, 3, 2, 2, 2, 1, 0, 0, 1, 1, 3, 3, 2, 1, 1, 1, 1, 2, 0, 3, 2, 0, 3, 0, 0,
    3, 2, 2, 2, 3, 3, 3, 3, 1, 1, 1, 0, 0, 3, 2, 2, 2, 3, 2, 3, 3, 2, 2, 3, 2, 2, 0, 1, 1, 1, 0, 3,
]
BLOCK_PARTS = [
    0, 3, 1, 2, 2, 3, 0, 1, 1, 2, 3, 0, 3, 0, 1, 2, 3, 0, 1, 2, 1, 0, 2, 3, 1, 2, 3, 0, 2, 3, 1, 0,
]


def group_places(groups):
    return [1, 4, 6, 3, 2, 0, 5, 7] if groups == 8 else list(range(groups))


@functools.lru_cache(None)
def unit_plan(fsdp, groups, query_width, pair_width):
    columns = query_width + 2 * pair_width
    per_device = columns // (fsdp * groups)
    group_query, group_pair = query_width // groups, pair_width // groups
    unit = math.gcd(math.gcd(per_device, group_query), group_pair)
    rounds = per_device // unit
    total = fsdp * groups
    wanted = []
    for index in range(columns // unit):
        column = index * unit
        if column < query_width:
            group, place = divmod(column, group_query)
        elif column < query_width + pair_width:
            group, place = divmod(column - query_width, group_pair)
            place += group_query
        else:
            group, place = divmod(column - query_width - pair_width, group_pair)
            place += group_query + group_pair
        wanted.append((index // rounds, index % rounds, group, place // unit))
    filled = {}
    edges = []
    near = UNIT_PARTS if groups == 8 and len(wanted) == len(UNIT_PARTS) else None
    spots = group_places(groups)
    for index, (source, slot, group, place) in enumerate(wanted):
        own = near[index] if near else source // groups
        for turn in (0, 1, 2, 3):
            part = own ^ turn
            if filled.get((part, group), 0) < rounds:
                filled[(part, group)] = filled.get((part, group), 0) + 1
                edges.append((source, slot, part * groups + spots[group], place))
                break
    steps = []
    for _ in range(rounds):
        taken = {}

        def find(source, seen):
            for edge in edges:
                if edge[0] != source or edge[2] in seen:
                    continue
                seen.add(edge[2])
                if edge[2] not in taken or find(taken[edge[2]][0], seen):
                    taken[edge[2]] = edge
                    return True
            return False

        for source in range(total):
            find(source, set())
        steps.append(sorted(taken.values()))
        for edge in taken.values():
            edges.remove(edge)
    send = np.zeros((rounds, total), np.int32)
    place_at = np.zeros((rounds, total), np.int32)
    pairs = []
    for i, step in enumerate(steps):
        pairs.append([(edge[0], edge[2]) for edge in step])
        for source, slot, target, place in step:
            send[i, source] = slot
            place_at[i, target] = place
    count = fsdp * rounds
    order = np.zeros((total, count), np.int32)
    back = np.zeros((total, count), np.int32)
    for device in range(total):
        group = device % groups
        for part in range(fsdp):
            for i in range(rounds):
                place = place_at[i, part * groups + group]
                order[device, place] = part * rounds + i
                back[device, part * rounds + i] = place
    home = np.argsort(send, axis=0).astype(np.int32)
    return unit, rounds, pairs, send, order, back, home


def out_pairs(fsdp, groups):
    total = fsdp * groups
    parts = BLOCK_PARTS if (fsdp, groups) == (4, 8) else [b % fsdp for b in range(total)]
    spots = group_places(groups)
    moves = [(b, parts[b] * groups + spots[b // fsdp]) for b in range(total)]
    found = np.zeros((total, fsdp), np.int32)
    for b, target in moves:
        found[target % groups :: groups, b % fsdp] = target // groups
    return moves, found


def turn(front, back, cosine, sine):
    return front * cosine - back * sine, back * cosine + front * sine


def forward_kernel(
    at_ref, sink_ref, front_ref, back_ref, key_front, key_back, value_front, value_back,
    query_bias, pair_bias, cos_ref, sin_ref,
    turned_ref, pairs_ref, out_ref, total_ref, keys,
    *, block, scale,
):
    head = pl.program_id(0)
    length = front_ref.shape[1]
    half = HD // 2
    cosine, sine = cos_ref[...], sin_ref[...]

    @pl.when(head == 0)
    def _():
        front, back = turn(
            key_front[...] + pair_bias[:half], key_back[...] + pair_bias[half:HD], cosine, sine
        )
        key = jnp.concatenate([front, back], axis=0)
        pairs_ref[:HD, :] = key.astype(LOW)
        pairs_ref[HD : HD + half, :] = (value_front[...] + pair_bias[HD : HD + half]).astype(LOW)
        pairs_ref[HD + half :, :] = (value_back[...] + pair_bias[HD + half :]).astype(LOW)
        keys[...] = key.T.astype(LOW)

    front, back = turn(
        front_ref[...] + query_bias[:half], back_ref[...] + query_bias[half:], cosine, sine
    )
    turned_ref[:half, :] = (front.astype(LOW).astype(WIDE) * scale).astype(LOW)
    turned_ref[half:, :] = (back.astype(LOW).astype(WIDE) * scale).astype(LOW)
    sink = sink_ref[head]
    count = length // block
    below = lax.broadcasted_iota(jnp.int32, (block, block), 0) > lax.broadcasted_iota(
        jnp.int32, (block, block), 1
    )
    for index in range(count):
        columns = pl.ds(index * block, block)
        query = turned_ref[:, columns]

        def scores(rows):
            return mul(keys[rows, :], query)

        def step(start, carry, masked):
            peak, total, mixed = carry
            rows = pl.ds(start, block)
            tile = scores(rows)
            if masked:
                tile = jnp.where(below, -1e30, tile)
            top = jnp.maximum(peak, jnp.max(tile, axis=0, keepdims=True))
            weights = jnp.exp(tile - top)
            shrink = jnp.exp(peak - top)
            total = total * shrink + jnp.sum(weights, axis=0, keepdims=True)
            mixed = mixed * shrink + mul(pairs_ref[HD:, rows], weights.astype(LOW))
            return top, total, mixed

        carry = (
            jnp.full((1, block), sink, WIDE),
            jnp.ones((1, block), WIDE),
            jnp.zeros((HD, block), WIDE),
        )
        if count <= 4:
            for earlier in range(index):
                carry = step(earlier * block, carry, False)
        elif index:
            carry = lax.fori_loop(
                0, index, lambda i, c: step(pl.multiple_of(i * block, block), c, False), carry
            )
        peak, total, mixed = step(index * block, carry, True)
        out_ref[:, columns] = (mixed / total).astype(LOW)
        total_ref[0, :, columns] = peak + jnp.log(total)


def attend(at, projected, bias, sinks, cosine, sine, heads):
    length = projected.shape[1]
    rows = heads * HD
    half = HD // 2
    block = min(512, length)
    last = rows // (2 * HD)

    def piece(place):
        return pl.BlockSpec((half, length), lambda h, at: (at[place], 0))

    return pl.pallas_call(
        functools.partial(forward_kernel, block=block, scale=HD**-0.5),
        grid_spec=pltpu.PrefetchScalarGridSpec(
            num_scalar_prefetch=1,
            grid=(heads,),
            in_specs=[
                pl.BlockSpec(memory_space=pltpu.SMEM),
                pl.BlockSpec((half, length), lambda h, at: (at[2 * h], 0)),
                pl.BlockSpec((half, length), lambda h, at: (at[2 * h + 1], 0)),
                piece(2 * heads),
                piece(2 * heads + 1),
                piece(2 * heads + 2),
                piece(2 * heads + 3),
                pl.BlockSpec((HD, 1), lambda h, at: (h, 0)),
                pl.BlockSpec((2 * HD, 1), lambda h, at: (last, 0)),
                pl.BlockSpec((half, length), lambda h, at: (0, 0)),
                pl.BlockSpec((half, length), lambda h, at: (0, 0)),
            ],
            out_specs=[
                pl.BlockSpec((HD, length), lambda h, at: (h, 0)),
                pl.BlockSpec((2 * HD, length), lambda h, at: (0, 0)),
                pl.BlockSpec((HD, length), lambda h, at: (at[2 * heads + 4 + h], 0)),
                pl.BlockSpec((1, 1, length), lambda h, at: (h, 0, 0)),
            ],
            scratch_shapes=[pltpu.VMEM((length, HD), LOW)],
        ),
        out_shape=[
            jax.ShapeDtypeStruct((rows, length), LOW),
            jax.ShapeDtypeStruct((2 * HD, length), LOW),
            jax.ShapeDtypeStruct((rows, length), LOW),
            jax.ShapeDtypeStruct((heads, 1, length), WIDE),
        ],
        compiler_params=pltpu.CompilerParams(
            dimension_semantics=("arbitrary",), vmem_limit_bytes=40 * 2**20
        ),
        cost_estimate=pl.CostEstimate(
            flops=0, bytes_accessed=22 * rows * length * 8, transcendentals=0
        ),
        name="attend",
    )(at, sinks, *[projected] * 6, bias, bias, cosine, sine)


def backward_kernel(
    at_ref, sink_ref, turned_ref, pairs_ref, out_ref, grad_ref, total_ref, cos_ref, sin_ref,
    query_ref, pair_ref, sink_grad_ref, keys, values, key_sum, value_sum, query_rows, grad_rows,
    *, block, scale,
):
    head = pl.program_id(0)
    length = turned_ref.shape[1]
    half = HD // 2
    count = length // block

    @pl.when(head == 0)
    def _():
        keys[...] = pairs_ref[:HD, :].astype(WIDE).T.astype(LOW)
        values[...] = pairs_ref[HD:, :].astype(WIDE).T.astype(LOW)
        key_sum[...] = jnp.zeros_like(key_sum)
        value_sum[...] = jnp.zeros_like(value_sum)

    query_rows[...] = turned_ref[...].astype(WIDE).T.astype(LOW)
    grad_rows[...] = grad_ref[...].astype(WIDE).T.astype(LOW)
    below = lax.broadcasted_iota(jnp.int32, (block, block), 0) > lax.broadcasted_iota(
        jnp.int32, (block, block), 1
    )
    deltas = jnp.sum(grad_ref[...].astype(WIDE) * out_ref[...].astype(WIDE), axis=0, keepdims=True)
    totals = total_ref[0]
    sink_term = -jnp.sum(jnp.exp(sink_ref[head] - totals) * deltas, axis=1, keepdims=True)
    sink_grad_ref[0] = jnp.broadcast_to(sink_term, (1, 128))
    for index in range(count):
        columns = pl.ds(index * block, block)
        query = turned_ref[:, columns]
        grad = grad_ref[:, columns]
        total = totals[:, index * block : (index + 1) * block]
        delta = deltas[:, index * block : (index + 1) * block]

        def step(start, query_sum, masked):
            rows = pl.ds(start, block)
            weights = jnp.exp(mul(keys[rows, :], query) - total)
            if masked:
                weights = jnp.where(below, 0.0, weights)
            inner = (weights * (mul(values[rows, :], grad) - delta)).astype(LOW)
            key_sum[rows, :] += mul(inner, query_rows[columns, :])
            value_sum[rows, :] += mul(weights.astype(LOW), grad_rows[columns, :])
            return query_sum + mul(pairs_ref[:HD, rows], inner)

        query_sum = jnp.zeros((HD, block), WIDE)
        if count <= 4:
            for earlier in range(index):
                query_sum = step(earlier * block, query_sum, False)
        elif index:
            query_sum = lax.fori_loop(
                0, index, lambda i, c: step(pl.multiple_of(i * block, block), c, False), query_sum
            )
        query_sum = step(index * block, query_sum, True)
        rounded = (query_sum * scale).astype(LOW).astype(WIDE)
        cosine, sine = cos_ref[:, columns], sin_ref[:, columns]
        front, back = turn(rounded[:half], rounded[half:], cosine, -sine)
        query_ref[:half, columns] = front.astype(LOW)
        query_ref[half:, columns] = back.astype(LOW)

    @pl.when(head == pl.num_programs(0) - 1)
    def _():
        rounded = key_sum[...].T.astype(LOW).astype(WIDE)
        front, back = turn(rounded[:half], rounded[half:], cos_ref[...], -sin_ref[...])
        pair_ref[:half, :] = front.astype(LOW)
        pair_ref[half:HD, :] = back.astype(LOW)
        pair_ref[HD:, :] = value_sum[...].T.astype(LOW)


def attend_back(at, sinks, turned, pairs, attended, upstream, totals, cosine, sine):
    heads, _, length = totals.shape
    rows = heads * HD
    block = min(512, length)
    by_head = pl.BlockSpec((HD, length), lambda h, at: (h, 0))
    moved = pl.BlockSpec((HD, length), lambda h, at: (at[2 * heads + 4 + h], 0))
    table = pl.BlockSpec((HD // 2, length), lambda h, at: (0, 0))
    whole = pl.BlockSpec((2 * HD, length), lambda h, at: (0, 0))
    return pl.pallas_call(
        functools.partial(backward_kernel, block=block, scale=HD**-0.5),
        grid_spec=pltpu.PrefetchScalarGridSpec(
            num_scalar_prefetch=1,
            grid=(heads,),
            in_specs=[
                pl.BlockSpec(memory_space=pltpu.SMEM),
                by_head,
                whole,
                moved,
                moved,
                pl.BlockSpec((1, 1, length), lambda h, at: (h, 0, 0)),
                table,
                table,
            ],
            out_specs=[by_head, whole, pl.BlockSpec((1, 1, 128), lambda h, at: (h, 0, 0))],
            scratch_shapes=[
                pltpu.VMEM((length, HD), LOW),
                pltpu.VMEM((length, HD), LOW),
                pltpu.VMEM((length, HD), WIDE),
                pltpu.VMEM((length, HD), WIDE),
                pltpu.VMEM((length, HD), LOW),
                pltpu.VMEM((length, HD), LOW),
            ],
        ),
        out_shape=[
            jax.ShapeDtypeStruct((rows, length), LOW),
            jax.ShapeDtypeStruct((2 * HD, length), LOW),
            jax.ShapeDtypeStruct((heads, 1, 128), WIDE),
        ],
        compiler_params=pltpu.CompilerParams(
            dimension_semantics=("arbitrary",), vmem_limit_bytes=40 * 2**20
        ),
        cost_estimate=pl.CostEstimate(
            flops=0, bytes_accessed=0, transcendentals=0
        ),
        name="attend_back",
    )(at, sinks, turned, pairs, attended, upstream, totals, cosine, sine)


EXTRA = 16


def term_kernel(left_ref, right_ref, extra_ref, out_ref):
    size = left_ref.shape[0]
    out_ref[:size, :] = mul(left_ref[...], right_ref[...]).astype(LOW)
    out_ref[size:, :] = extra_ref[...].astype(LOW)


def column_parts(width, count):
    block = min(640, width)
    tiles = pl.cdiv(width, block)
    ends = [round(tiles * i / count) for i in range(count + 1)]
    return block, [(a, b - a) for a, b in zip(ends, ends[1:]) if b > a]


def weight_term(left, right, extra, size, block, tiles):
    depth, width = right.shape
    first, count = tiles
    shards = left.shape[0] // size
    columns = min(width, (first + count) * block) - first * block
    return pl.pallas_call(
        term_kernel,
        grid=(shards, count),
        in_specs=[
            pl.BlockSpec((size, depth), lambda m, n: (m, 0)),
            pl.BlockSpec((depth, block), lambda m, n: (0, n + first)),
            pl.BlockSpec((EXTRA, block), lambda m, n: (0, n + first)),
        ],
        out_specs=pl.BlockSpec((size + EXTRA, block), lambda m, n: (m, n)),
        out_shape=jax.ShapeDtypeStruct((shards * (size + EXTRA), columns), LOW),
        compiler_params=pltpu.CompilerParams(
            dimension_semantics=("arbitrary", "arbitrary"), vmem_limit_bytes=56 * 2**20
        ),
        cost_estimate=free(),
        name="weight_term",
    )(left, right, extra)


def rms_scale(values, norm_gain):
    factor = lax.rsqrt(jnp.mean(values * values, axis=-1, keepdims=True) + NORM_EPSILON)
    return (values * factor * norm_gain, factor)


def rms_back(values, factor, norm_gain, upstream):
    scaled = upstream * norm_gain
    value_grad = factor * scaled - values * factor * factor * factor * jnp.mean(
        scaled * values, axis=-1, keepdims=True
    )
    gain_grad = jnp.sum(upstream * values * factor, axis=0)
    return (value_grad, gain_grad)


def clamped_glu(joined, expert_width):
    gate_part = jnp.minimum(joined[:, :expert_width], CLAMP_LIMIT)
    linear_part = jnp.clip(joined[:, expert_width:], -CLAMP_LIMIT, CLAMP_LIMIT)
    return (linear_part + 1.0) * gate_part * jax.nn.sigmoid(SWIGLU_SLOPE * gate_part)


def glu_back(joined, expert_width, upstream):
    raw_gate = joined[:, :expert_width]
    raw_linear = joined[:, expert_width:]
    gate_part = jnp.minimum(raw_gate, CLAMP_LIMIT)
    linear_part = jnp.clip(raw_linear, -CLAMP_LIMIT, CLAMP_LIMIT)
    sigmoid_part = jax.nn.sigmoid(SWIGLU_SLOPE * gate_part)
    gate_open = (raw_gate < CLAMP_LIMIT).astype(jnp.float32)
    linear_open = (jnp.abs(raw_linear) < CLAMP_LIMIT).astype(jnp.float32)
    slope_part = sigmoid_part + gate_part * SWIGLU_SLOPE * sigmoid_part * (1.0 - sigmoid_part)
    gate_grad = upstream * (linear_part + 1.0) * slope_part * gate_open
    linear_grad = upstream * gate_part * sigmoid_part * linear_open
    return jnp.concatenate([gate_grad, linear_grad], axis=1)


def mixing_of(rows, routes, router_weight, router_bias):
    logits = mul(rows, router_weight) + router_bias
    experts = jnp.arange(router_bias.shape[0], dtype=jnp.int32)
    chosen = jnp.any(routes[:, :, None] == experts, axis=1)
    logits = jnp.where(chosen, logits, -jnp.inf)
    weights = jnp.exp(logits - jnp.max(logits, axis=1, keepdims=True))
    return weights / jnp.sum(weights, axis=1, keepdims=True)


def rows_of(values, index, size):
    return lax.dynamic_slice_in_dim(values, index * size, size, axis=0)


def columns_of(values, index, size):
    return lax.dynamic_slice_in_dim(values, index * size, size, axis=1)


def body(
    hidden,
    out_grad,
    routes,
    norm1_gain,
    qkv_weight,
    qkv_bias,
    sink_logits,
    out_weight,
    out_bias,
    norm2_gain,
    router_weight,
    router_bias,
    gate_up_weight,
    gate_up_bias,
    down_weight,
    down_bias,
):
    tokens = hidden.shape[1]
    groups = lax.axis_size("seq")
    position = lax.axis_index("seq")
    spots = np.argsort(np.array(group_places(lax.axis_size("seq")))).astype(np.int32)
    group = jnp.asarray(spots)[position]
    fsdp = lax.axis_size("fsdp")
    part = lax.axis_index("fsdp")
    device = part * groups + position
    head_count = sink_logits.shape[0]
    group_heads = head_count // groups
    expert_width = down_weight.shape[1] * fsdp
    capacity = tokens * TOPK * 9 // (8 * groups)
    slot_count = groups * capacity
    length = tokens * groups
    query_width = head_count * HD
    pair_width = KV_HEADS * HD
    group_query = group_heads * HD
    ids = ring_ids()

    planned = groups == KV_HEADS and fsdp == 4 and qkv_weight.shape[1] % (HD // 2) == 0
    qkv_rows = straight(qkv_weight.T)
    held = {}
    freight = Freight()
    out_moves, out_found = out_pairs(fsdp, groups)

    def keep(name):
        return lambda values: held.__setitem__(name, values)

    if planned:
        unit, rounds, pairs, send_slots, order, back, home = unit_plan(
            fsdp, groups, query_width, pair_width
        )
        slots = jnp.asarray(send_slots)[:, device]
        bias_at = (group, group, group)
        head_units = jnp.asarray(order)[device]

        def open_units(weight):
            units = weight.reshape(rounds, unit, -1)
            blocks = [
                send(lax.dynamic_index_in_dim(units, slots[i], 0, keepdims=False), BOTH, pairs[i])
                for i in range(rounds)
            ]
            freight.need(lay(*blocks).reshape(rounds * unit, -1), units_there)

        def units_there(mine):
            held["qkv"] = lax.all_gather(mine, "fsdp", axis=0, tiled=True)

        freight.need(qkv_rows, open_units)
    else:
        pair_index = group * KV_HEADS // groups
        bias_at = (group, pair_index, pair_index)
        head_units = jnp.arange(2 * group_heads + 4, dtype=jnp.int32)
    bias_group = jnp.concatenate(
        [
            rows_of(qkv_bias[:query_width], bias_at[0], group_query),
            rows_of(qkv_bias[query_width : query_width + pair_width], bias_at[1], HD),
            rows_of(qkv_bias[query_width + pair_width :], bias_at[2], HD),
        ]
    )
    block_heads = out_weight.shape[0] // HD
    by_block = out_weight.shape[0] % HD == 0
    head_ids = jnp.arange(group_heads, dtype=jnp.int32)
    if by_block:
        turns = jnp.asarray(np.repeat(out_found, block_heads, axis=1))[device]
        head_ids = turns * block_heads + head_ids % block_heads
    places_at = jnp.concatenate([head_units, head_ids])

    def open_out(weight):
        freight.after(2, send(weight, BOTH, out_moves), out_there)

    def out_there(mine):
        held["out_mine"], held["out_far"] = mine, swap(mine, "fsdp", 2)

    def open_gate_up(shard):
        held["gate_up"] = lax.all_gather(shard, "fsdp", axis=0, tiled=True)

    held["down"] = lax.all_gather(down_weight[0], "fsdp", axis=0, tiled=True)
    freight.after(2, out_weight, open_out)
    freight.after(3, gate_up_weight[0], open_gate_up)

    def open_routes(own):
        own = jnp.broadcast_to(own.reshape(1, -1), (groups, tokens * TOPK))
        held["routes"] = lax.all_to_all(own, "seq", split_axis=0, concat_axis=0, tiled=True)

    freight.after(4, routes, open_routes)

    inputs = hidden[0].astype(WIDE)
    first_normed, first_factor = rms_scale(inputs, norm1_gain)
    first_full, first_last = ring_gather(first_normed.astype(LOW), ids, freight)
    frequency = ROPE_BASE ** (-(jnp.arange(HD // 2, dtype=WIDE) * 2.0) / HD)
    angles = jnp.arange(length, dtype=jnp.int32).astype(WIDE)[None, :] * frequency[:, None]
    cosine, sine = jnp.cos(angles), jnp.sin(angles)
    sink_part = rows_of(sink_logits, group, group_heads)
    gather = ring_gather_steps(out_grad[0], ids, freight, first_last)
    hop = next(gather)
    if planned:
        qkv_group = held["qkv"]
    else:
        qkv_full = lax.all_gather(qkv_rows, BOTH, axis=0, tiled=True)
        qkv_group = jnp.concatenate(
            [
                rows_of(qkv_full[:query_width], group, group_query),
                rows_of(qkv_full[query_width : query_width + pair_width], pair_index, HD),
                rows_of(qkv_full[query_width + pair_width :], pair_index, HD),
            ]
        )
    projected, held["routes"] = lax.optimization_barrier(
        (mul(qkv_group, first_full, NT), held["routes"])
    )
    turned, pair_rows, attended, log_totals = attend(
        places_at, projected, bias_group[:, None], sink_part, cosine, sine, group_heads
    )
    mine, far, attended = lax.optimization_barrier((held["out_mine"], held["out_far"], attended))
    near = swap(lay(mine, far), "fsdp", 1)
    parts = part ^ jnp.arange(fsdp, dtype=jnp.int32)
    out_group = lay(mine, (near, 0), far, (near, 1), at=parts).reshape(fsdp * mine.shape[0], -1)

    freight.need(hop, gather.send)
    biases = jnp.concatenate([gate_up_bias, down_bias], axis=1)
    freight.chain(biases, xor_steps("fsdp"), keep("biases"))
    branch = ring_reduce(
        lambda index: mul(columns_of(attended, index, tokens), out_group, TN), ids, freight
    )
    middle = inputs + (branch + out_bias)
    second_normed, second_factor = rms_scale(middle, norm2_gain)
    second_low = second_normed.astype(LOW)

    second_full, last = ring_gather(second_low, ids, freight)
    freight.need(last[0], lambda values: None)
    next(gather)
    freight.finish()
    joined_weight, down_full = held["gate_up"], held["down"]
    all_routes = held["routes"].reshape(length, TOPK)
    biases = straighten(held["biases"], "fsdp")
    joined_bias = biases[:, : gate_up_bias.shape[1]].reshape(-1).astype(WIDE)
    down_shift = biases[:, gate_up_bias.shape[1] :].reshape(-1).astype(WIDE)
    mine = jnp.any(all_routes == position, axis=1)
    counted = mine.astype(jnp.int32)
    earlier = jnp.cumsum(counted) - counted
    places = jnp.where(mine, earlier, -1)
    slots_here = jnp.arange(slot_count, dtype=jnp.int32)
    into = slots_here[:, None] == places[None, :]
    back_to = places[:, None] == slots_here[None, :]
    into_low, back_low = into.astype(LOW), back_to.astype(LOW)
    mixing_all = mixing_of(second_full, all_routes, router_weight, router_bias)
    expert_ids = jnp.arange(groups, dtype=jnp.int32)
    mixing_mine = jnp.sum(jnp.where(expert_ids == position, mixing_all, 0.0), axis=1)
    mixing_rows = jnp.sum(jnp.where(into, mixing_mine[None, :], 0.0), axis=1)[:, None]
    next(gather)
    expert_rows = mul(into_low, second_full).astype(LOW)
    freight.need(straight(mul(expert_rows, joined_weight) + joined_bias), keep("joined"))
    next(gather)
    joined = held["joined"]
    activated = lax.optimization_barrier(clamped_glu(joined, expert_width).astype(LOW))
    expert_columns = expert_rows.T
    upstream_full = None
    for upstream_full in gather:
        pass
    upstream_full = upstream_full[0]
    freight.finish()
    freight = Freight()
    upstream_rows = mul(into_low, upstream_full)
    rows_grad = (upstream_rows * mixing_rows).astype(LOW)
    down_term = straight(mul(activated, rows_grad, TN).astype(LOW))
    down_total = lax.psum_scatter(down_term, "fsdp", scatter_dimension=0, tiled=True)
    freight.at(9, down_total, lambda total: freight.need(total.astype(WIDE), keep("down_shard")))
    activated, _ = lax.optimization_barrier((activated, down_term))
    expert_out = (mul(activated, down_full) + down_shift).astype(LOW).astype(WIDE)
    weighted = (expert_out * mixing_rows).astype(LOW)
    mixing_grad_rows = jnp.sum(upstream_rows * expert_out, axis=1)
    down_sums = jnp.sum(rows_grad.astype(WIDE), axis=0, keepdims=True)


    def back_first(upstream):
        activated_grad = mul(upstream, down_full, NT)
        grad = straight(glu_back(joined, expert_width, activated_grad).astype(LOW))
        freight.need(grad, back_second)

    def back_second(grad):
        held["input_rows_grad"] = straight(mul(grad, joined_weight, NT).astype(LOW))
        back_third(grad)

    def back_third(grad):
        sums = jnp.sum(grad.astype(WIDE), axis=0, keepdims=True)
        extra = jnp.concatenate([sums, jnp.pad(down_sums, ((0, 0), (0, expert_width)))])
        extra = jnp.pad(extra, ((0, EXTRA - 2), (0, 0)))
        block, split = column_parts(grad.shape[1], 3)
        held["joined_parts"] = [None] * len(split)
        held["joined_shard"] = blank((hidden.shape[2] // fsdp, grad.shape[1]), WIDE)

        def part_there(i, term):
            total = lax.psum_scatter(term, "fsdp", scatter_dimension=0, tiled=True)
            freight.at([11, 14, 16][i], total, functools.partial(part_kept, i))

        def part_kept(i, total):
            own_rows = hidden.shape[2] // fsdp
            rows = total[:own_rows].astype(WIDE)
            start = split[i][0] * block
            held["joined_shard"] = lax.dynamic_update_slice(held["joined_shard"], rows, (0, start))
            held["joined_parts"][i] = total[own_rows : own_rows + 2].astype(WIDE)
            if i + 1 < len(split):
                freight.need(held["joined_shard"], keep("joined_shard"))

        def begin(i, held_here):
            grad, extra = held_here
            size = hidden.shape[2] // fsdp
            term = weight_term(expert_columns, grad, extra, size, block, split[i])
            freight.need(term, functools.partial(part_there, i))

        begin(0, (grad, extra))
        for i in range(1, len(split)):
            freight.at([2, 5, 7][i], (grad, extra), functools.partial(begin, i))

    def mixing_back(rows):
        tokens_grad = jnp.sum(jnp.where(back_to, rows[None, :], 0.0), axis=1)
        by_device = lax.all_to_all(
            tokens_grad.reshape(groups, tokens), "seq", split_axis=0, concat_axis=0, tiled=True
        )
        freight.need(by_device, keep("mixing_grad"))

    freight.need(mixing_grad_rows, mixing_back)
    freight.need(rows_grad, back_first)
    combined = ring_reduce(lambda index: mul(rows_of(back_low, index, tokens), weighted), ids, freight)
    freight.need((middle + combined).astype(LOW), keep("outputs"))
    if "input_rows_grad" not in held:
        freight.finish()
    input_rows_grad = held["input_rows_grad"]
    second_grad = ring_reduce(
        lambda index: mul(rows_of(back_low, index, tokens), input_rows_grad), ids, freight
    )
    mixing = mixing_of(second_low, routes[0], router_weight, router_bias)
    mixing_grad = held["mixing_grad"].T
    logits_grad = mixing * (
        mixing_grad - jnp.sum(mixing * mixing_grad, axis=-1, keepdims=True)
    )
    second_grad = second_grad + jnp.dot(
        logits_grad, router_weight.astype(WIDE).T, precision=PRECISE
    )
    upstream = out_grad[0].astype(WIDE)
    middle_part, gain2_grad = rms_back(middle, second_factor, norm2_gain, second_grad)
    middle_grad = upstream + middle_part
    branch_low = middle_grad.astype(LOW)

    width = hidden.shape[2]

    router_weight_grad = jnp.dot(second_low.astype(WIDE).T, logits_grad, precision=PRECISE)
    router_bias_grad = jnp.sum(logits_grad, axis=0)
    out_bias_grad = jnp.sum(branch_low.astype(WIDE), axis=0)
    early = [out_bias_grad, gain2_grad, router_weight_grad.T.reshape(-1), router_bias_grad]
    branch_full, _ = ring_gather(branch_low, ids, freight)
    heads_grad = mul(out_group, branch_full, NT).astype(LOW)
    query_grad, pair_grad, sink_grad = attend_back(
        places_at, sink_part, turned, pair_rows, attended, heads_grad, log_totals, cosine, sine
    )
    projected_grad = jnp.concatenate([query_grad, pair_grad])
    bias_term = jnp.sum(projected_grad.astype(WIDE), axis=1)
    if planned:
        projected_grad = jnp.take(
            projected_grad.reshape(fsdp * rounds, unit, -1),
            jnp.asarray(back)[device],
            axis=0,
            mode="clip",
        ).reshape(projected_grad.shape)

    bias_full = jnp.zeros((query_width + 2 * pair_width,), WIDE)
    bias_full = lax.dynamic_update_slice(
        bias_full, bias_term[:group_query], (bias_at[0] * group_query,)
    )
    bias_full = lax.dynamic_update_slice(
        bias_full, bias_term[group_query : group_query + HD], (query_width + bias_at[1] * HD,)
    )
    bias_full = lax.dynamic_update_slice(
        bias_full,
        bias_term[group_query + HD :],
        (query_width + pair_width + bias_at[2] * HD,),
    )
    sink_full = lax.dynamic_update_slice_in_dim(
        jnp.zeros((head_count,), WIDE), sink_grad[:, 0, 0], group * group_heads, 0
    )

    def out_first(grad):
        terms = straight(mul(attended, grad).astype(LOW))

        def use(total):
            held["out_total"] = total.astype(LOW)

        freight.blocks(terms.reshape(fsdp, out_weight.shape[0], -1), 15, 16, use)

    def qkv_first(grad):
        terms = mul(grad, first_full)
        low = straight(terms.astype(LOW))
        sums = jnp.sum(low.astype(WIDE) * qkv_group.astype(WIDE), axis=0) / norm1_gain
        late = jnp.concatenate([sums, bias_full, sink_full, *early])
        freight.chain(late, sum_steps(["seq"]), keep("late"))
        if not planned:
            held["qkv_term"] = terms
            return

        def come_back(total):
            held["qkv_total"] = straight(total.astype(LOW))

        freight.blocks(low.reshape(fsdp, rounds, unit, -1), 14, 16, come_back)

    freight.need(projected_grad, qkv_first)
    freight.at(14, branch_full, out_first)
    first_grad = ring_reduce(
        lambda index: mul(columns_of(projected_grad, index, tokens), qkv_group, TN), ids, freight
    )
    freight.finish()
    joined_sums = jnp.concatenate(held["joined_parts"], axis=1)
    joined_shard = held["joined_shard"]
    joined_bias_shard = rows_of(joined_sums[0], part, gate_up_bias.shape[1])
    down_bias_shard = rows_of(joined_sums[1, :width], part, down_bias.shape[1])
    down_shard = held["down_shard"]
    qkv_total = held.get("qkv_total", held["out_total"])
    late, first_grad, out_total, qkv_total = lax.optimization_barrier(
        (held["late"], first_grad, held["out_total"], qkv_total)
    )
    if planned:
        returned = lay(
            *[
                send(qkv_total[i], BOTH, [(b, a) for a, b in pairs[i]])
                for i in range(rounds)
            ]
        )
    if planned:
        qkv_shard = jnp.take(returned, jnp.asarray(home)[:, device], axis=0, mode="clip")
        qkv_shard = qkv_shard.reshape(rounds * unit, -1).T.astype(WIDE)
    else:
        qkv_term = held["qkv_term"]
        scattered = jnp.zeros((query_width + 2 * pair_width, width), WIDE)
        for start, stop, row in (
            (0, group_query, group * group_query),
            (group_query, group_query + HD, query_width + pair_index * HD),
            (group_query + HD, group_query + 2 * HD, query_width + pair_width + pair_index * HD),
        ):
            scattered = lax.dynamic_update_slice(scattered, qkv_term[start:stop], (row, 0))
        qkv_shard = lax.psum_scatter(scattered, BOTH, scatter_dimension=0, tiled=True).T
    out_shard = send(out_total, BOTH, [(b, a) for a, b in out_moves]).astype(WIDE)
    for step in sum_steps(["fsdp"]):
        late = step(late)
    input_part, _ = rms_back(inputs, first_factor, norm1_gain, first_grad)
    input_grad = middle_grad + input_part

    early = late[width + qkv_bias.shape[0] + head_count :]
    router_sums = early[2 * width : 2 * width + width * groups].reshape(groups, width).T
    return (
        held["outputs"][None],
        input_grad.astype(LOW)[None],
        late[:width],
        qkv_shard,
        late[width : width + qkv_bias.shape[0]],
        late[width + qkv_bias.shape[0] : width + qkv_bias.shape[0] + head_count],
        out_shard,
        early[:width],
        early[width : 2 * width],
        router_sums,
        early[2 * width + width * groups : 2 * width + (width + 1) * groups],
        joined_shard[None],
        joined_bias_shard[None],
        down_shard[None],
        down_bias_shard[None],
    )


def solution(mesh):
    tokens = P("fsdp", "seq", None)
    by_expert = P("seq", "fsdp", None)
    return jax.shard_map(
        body,
        mesh=mesh,
        in_specs=(
            tokens, tokens, tokens, P(), P(None, BOTH), P(), P(), P(BOTH, None), P(), P(), P(), P(),
            by_expert, P("seq", "fsdp"), by_expert, P("seq", "fsdp"),
        ),
        out_specs=(
            tokens, tokens, P(), P(None, BOTH), P(), P(), P(BOTH, None), P(), P(), P(), P(),
            by_expert, P("seq", "fsdp"), by_expert, P("seq", "fsdp"),
        ),
        check_vma=False,
    )
```
